32 devices in a mesh: dp: 8 (over y, x, core), mp: 4 (over z).
Axes of the slice: x: 2, y: 2, z: 4, core: 2. Of those that a mesh axis runs over, the one named last changes fastest.
Arguments:
- tokens: bfloat16 [16384, 768], P('dp'), may hold values from -6 to 6
- segments: int32 [16, 1024], P('dp'), may hold values from 0 to 7, never falling along the last dimension, each value on 1 to 512 neighbouring positions
- norm_gains: float32 [2, 768], replicated, may hold values from 0.1 to 1.9
- norm_shifts: float32 [2, 768], replicated, may hold values from -1.75 to 1.75
- qkv_weight: float32 [3, 768, 768], P(None, None, 'mp'), may hold values from -0.21875 to 0.21875
- qv_bias: float32 [2, 768], P(None, 'mp'), may hold values from -0.625 to 0.625
- out_weight: float32 [768, 768], P('mp'), may hold values from -1.75 to 1.75
- out_biases: float32 [2, 768], replicated, may hold values from -1.75 to 1.75
- up_weight: float32 [768, 3072], P(None, 'mp'), may hold values from -0.21875 to 0.21875
- up_bias: float32 [3072], P('mp'), may hold values from -3 to 3
- down_weight: float32 [3072, 768], P('mp'), may hold values from -0.109375 to 0.109375
- cotangent: bfloat16 [16384, 768], P('dp'), may hold values from -6 to 6
Outputs:
- result: bfloat16 [16384, 768], P('dp')
- token_grad: float32 [16384, 768], P('dp')
- gains_grad: float32 [2, 768], replicated
- shifts_grad: float32 [2, 768], replicated
- qkv_grad: float32 [3, 768, 768], P(None, None, 'mp')
- qv_bias_grad: float32 [2, 768], P(None, 'mp')
- out_weight_grad: float32 [768, 768], P('mp')
- out_biases_grad: float32 [2, 768], replicated
- up_grad: float32 [768, 3072], P(None, 'mp')
- up_bias_grad: float32 [3072], P('mp')
- down_grad: float32 [3072, 768], P('mp')
The draws below stay inside these ranges and needn't reach their ends.
Inputs may be any that keep to these rules, and one draw needn't show every extreme that they name: `segments`: within each packed row the document numbers never fall, every number of 0 to 7 occurs, each document has 1 to 512 tokens, and some document has exactly 512.
All inputs are finite; a program needn't handle non-finite values.
Results may differ from the reference program's by a relative error of at most 0.012.
The reference program's roundings to bfloat16 on the way count: a program that leaves them out, or rounds other values in their place, can miss the bound.
Values sent between devices are 32-bit elements; how exact they have to be, the bound alone decides.
A program may use at most 192 MiB of HBM per device.

```python
import math
import jax
import jax.numpy as jnp
import numpy as np
from jax import lax

D = 768
HEADS = 12
HEAD_DIM = 64
FF = 3072
SEQ = 1024
DOCS = 8
ROWS = 16
TOKENS = 16384


def level_of(stream_key, dims, shards, least, largest):
    factor_of = 1.0
    for dim, blocks in shards:
        draws = jax.random.uniform(jax.random.fold_in(jax.random.fold_in(stream_key, 6), dim), (blocks,), jnp.float32, least / len(shards), largest / len(shards))
        factor_of = factor_of * jnp.repeat(jnp.exp(draws), dims[dim] // blocks).reshape((-1,) + (1,) * (len(dims) - 1 - dim))
    return factor_of


def split_up(number_of, total, bound, slope):
    weights = [(1 << 20) // math.isqrt(standing ** slope) + 1 for standing in range(2, number_of + 1)]
    rest, counts = total - bound - (number_of - 1), [1] * (number_of - 1)
    while rest > 0:
        candidates = [i for i in range(number_of - 1) if counts[i] < bound]
        whole, remaining = sum([weights[i] for i in candidates]), rest
        for i in candidates:
            more = min(bound - counts[i], max(1, remaining * weights[i] // whole), rest)
            counts[i] = counts[i] + more
            rest = rest - more
    return np.array([bound] + counts)


def ragged(rng, amount, total, most, lean):
    if amount == 2:
        one = jax.random.randint(rng, (), max(1, total - most), min(most, total - 1) + 1)
        return jnp.stack([one, total - one])
    sizes = jnp.asarray(split_up(amount, total, most, lean), jnp.int32)
    pairs = (amount - 1) // 2
    giver, taker = sizes[1:1 + 2 * pairs:2], sizes[2:2 + 2 * pairs:2]
    margin = jnp.minimum(giver - 1, most - taker)
    passed = jax.random.randint(jax.random.fold_in(rng, 1), (pairs,), 0, 1 << 20) % (margin + 1)
    sizes = sizes.at[1:1 + 2 * pairs:2].set(giver - passed).at[2:2 + 2 * pairs:2].set(taker + passed)
    return sizes[jax.random.permutation(jax.random.fold_in(rng, 2), amount)]


def noise(stream_key, shape, scale, limit, cuts=(), kind=jnp.bfloat16):
    array = jax.random.normal(stream_key, shape, jnp.float32) * scale
    if len(cuts) > 0:
        array = level_of(stream_key, shape, cuts, -0.22, 0.18) * array
    return jnp.clip(array, min=-limit, max=limit).astype(kind)


def setup_inputs(seed: int = 0) -> dict:
    streams_of = jax.random.split(jax.random.key(seed), 13)
    return {
        "tokens": noise(streams_of[0], (TOKENS, D), 1.0, 6.0, ((0, 8),)),
        "segments": jax.vmap(lambda own: jnp.searchsorted(jnp.cumsum(ragged(own, DOCS, SEQ, SEQ // 2, 0)), jnp.arange(SEQ), side="right"))(jax.random.split(streams_of[1], ROWS)).reshape((ROWS, SEQ)).astype(jnp.int32),
        "norm_gains": jnp.clip(1.0 + 0.18 * jax.random.normal(streams_of[2], (2, D), jnp.float32), 0.1, 1.9),
        "norm_shifts": noise(streams_of[3], (2, D), 0.3, 1.75, (), jnp.float32),
        "qkv_weight": noise(streams_of[4], (3, D, D), D ** -0.5, 0.21875, ((2, 4),), jnp.float32),
        "qv_bias": noise(streams_of[5], (2, D), 0.1, 0.625, ((1, 4),), jnp.float32),
        "out_weight": noise(streams_of[6], (D, D), (max(D // 64, 2)) ** -0.5, 1.75, ((0, 4),), jnp.float32),
        "out_biases": noise(streams_of[7], (2, D), 0.3, 1.75, (), jnp.float32),
        "up_weight": noise(streams_of[8], (D, FF), D ** -0.5, 0.21875, ((1, 4),), jnp.float32),
        "up_bias": noise(streams_of[9], (FF,), 0.5, 3.0, ((0, 4),), jnp.float32),
        "down_weight": noise(streams_of[10], (FF, D), FF ** -0.5, 0.109375, ((0, 4),), jnp.float32),
        "cotangent": noise(streams_of[11], (TOKENS, D), 1.0, 6.0, ((0, 8),)),
    }


@jax.custom_vjp
def low(v):
    return lax.optimization_barrier(v.astype(jnp.bfloat16)).astype(jnp.float32)

@jax.custom_vjp
def low_back(v):
    return v

def low_keep(v):
    return (low(v), None)

def low_pass(kept, grad):
    return (grad,)

def back_keep(v):
    return (v, None)

def back_low(kept, grad):
    return (low(grad),)
low.defvjp(low_keep, low_pass)
low_back.defvjp(back_keep, back_low)
NORM_EPSILON = 1e-06
MASKED_SCORE = -1000000000.0

def matmul(left, right):
    return jnp.dot(left, right, precision=lax.Precision.HIGHEST, preferred_element_type=jnp.float32)

def standardize(values):
    centered = values - lax.optimization_barrier(jnp.mean(values, -1, keepdims=True))
    return centered * lax.rsqrt(lax.optimization_barrier(jnp.mean(centered * centered, -1, keepdims=True)) + NORM_EPSILON)

def attend(pieces):
    queries, keys_row, values_row, doc_ids = pieces
    scores = jnp.einsum('qhd,khd->hqk', queries, keys_row, precision=lax.Precision.HIGHEST) * HEAD_DIM ** (-0.5)
    scores = low_back(scores)
    same_doc = doc_ids[:, None] == doc_ids[None, :]
    scores = jnp.where(same_doc[None], scores, MASKED_SCORE)
    probs = low(jax.nn.softmax(scores, axis=-1))
    return jnp.einsum('hqk,khd->qhd', probs, values_row, precision=lax.Precision.HIGHEST)

def layer(inputs, norm_gains, norm_shifts, qkv_weight, qv_bias, out_weight, out_biases, up_weight, up_bias, down_weight, segments):
    hidden_one = low(standardize(inputs) * norm_gains[0] + norm_shifts[0])
    queries = low_back(low(matmul(hidden_one, low(qkv_weight[0])) + qv_bias[0]))
    keys_all = low_back(low(matmul(hidden_one, low(qkv_weight[1]))))
    values_all = low_back(low(matmul(hidden_one, low(qkv_weight[2])) + qv_bias[1]))
    row_shape = (ROWS, SEQ, HEADS, HEAD_DIM)
    attended = lax.map(jax.checkpoint(attend), (queries.reshape(row_shape), keys_all.reshape(row_shape), values_all.reshape(row_shape), segments))
    attended = low_back(low(attended.reshape(ROWS * SEQ, D)))
    mixed = inputs + low_back(matmul(attended, low(out_weight))) + out_biases[0]
    hidden_two = low(standardize(mixed) * norm_gains[1] + norm_shifts[1])
    pre_act = low_back(matmul(hidden_two, low(up_weight)) + up_bias)
    activated = low(jax.nn.gelu(pre_act, approximate=True))
    return mixed + low_back(matmul(activated, low(down_weight))) + out_biases[1]

def reference(tokens, segments, norm_gains, norm_shifts, qkv_weight, qv_bias, out_weight, out_biases, up_weight, up_bias, down_weight, cotangent):

    def forward(inputs, gains, shifts, w_qkv, b_qv, w_out, b_out, w_up, b_up, w_down):
        return layer(inputs, gains, shifts, w_qkv, b_qv, w_out, b_out, w_up, b_up, w_down, segments)
    output, backward = jax.vjp(forward, tokens.astype(jnp.float32), norm_gains, norm_shifts, qkv_weight, qv_bias, out_weight, out_biases, up_weight, up_bias, down_weight)
    grads = backward(cotangent.astype(jnp.float32))
    return (output.astype(jnp.bfloat16), grads[0], grads[1], grads[2], grads[3], grads[4], grads[5], grads[6], grads[7], grads[8], grads[9])
```

```python
from functools import partial

import jax
import jax.numpy as jnp
from jax import lax
from jax.experimental import pallas as pl
from jax.experimental.pallas import tpu as pltpu
from jax.sharding import PartitionSpec as P

F32 = jnp.float32
BF = jnp.bfloat16
HEAD_DIM = 64
NORM_EPSILON = 1e-06
BIG = 1e30
LOG2E = 1.4426950408889634
SAFE_SCORE = 60.0
REACH = 512
TILE = 256
EXTRA = 16
FWD_UNROLL = 4
BWD_UNROLL = 3

NN = (((1,), (0,)), ((), ()))
NT = (((1,), (1,)), ((), ()))
TN = (((0,), (0,)), ((), ()))
WHOLE = pl.BlockSpec(memory_space=pltpu.VMEM)
SCALARS = pl.BlockSpec(memory_space=pltpu.SMEM)


def dot(left, right, dims):
    return lax.dot_general(left, right, dims, preferred_element_type=F32)


def params(mib=56):
    return pltpu.CompilerParams(vmem_limit_bytes=mib * 2**20)


def standardize(values):
    centered = values - jnp.mean(values, -1, keepdims=True)
    inv_std = lax.rsqrt(jnp.mean(centered * centered, -1, keepdims=True) + NORM_EPSILON)
    return centered * inv_std, inv_std


def norm_back(grad_in, normed, inv_std, gain):
    scaled = grad_in * gain
    return inv_std * (
        scaled
        - jnp.mean(scaled, -1, keepdims=True)
        - normed * jnp.mean(scaled * normed, -1, keepdims=True)
    )


def shape_of(shape, dtype):
    return jax.ShapeDtypeStruct(shape, dtype)


def cast_kernel(in_ref, out_ref):
    out_ref[...] = in_ref[...].astype(BF)


def cast_low(array):
    rows, width = array.shape
    block = pl.BlockSpec((256, width), lambda i: (i, 0))
    return pl.pallas_call(
        cast_kernel,
        grid=(rows // 256,),
        in_specs=[block],
        out_specs=block,
        out_shape=shape_of(array.shape, BF),
    )(array)


def attend_kernel(
    x_ref, seg_ref, gain_ref, shift_ref, w_ref, b_ref,
    h1_ref, qt_ref, kt_ref, vt_ref, ot_ref, lse_ref,
    qx, kx, vx, kn,
):
    length, width = x_ref.shape
    heads = width // HEAD_DIM
    normed, _ = standardize(x_ref[...].astype(F32))
    h1_ref[...] = (normed * gain_ref[0:1, :] + shift_ref[0:1, :]).astype(BF)
    for j, out in enumerate((qt_ref, kt_ref, vt_ref)):
        value = dot(w_ref[j * width : (j + 1) * width, :], h1_ref[...], NT)
        if j != 1:
            value = value + b_ref[j * width : (j + 1) * width, :]
        value = value.astype(BF)
        if j == 0:
            value = value * jnp.asarray(HEAD_DIM**-0.5, BF)
        out[...] = value
    row = lax.broadcasted_iota(jnp.int32, (EXTRA, length), 0)
    same = row == seg_ref[0]
    for u in range(FWD_UNROLL):
        qx[u, HEAD_DIM:, :] = jnp.where(same | (row >= 8), 0.0, -BIG).astype(BF)
        kx[u, HEAD_DIM:, :] = jnp.where(same, 1.0, 0.0).astype(BF)
        vx[u, HEAD_DIM:, :] = jnp.ones((EXTRA, length), BF)

    def load(h, u):
        rows = pl.ds(pl.multiple_of(h * HEAD_DIM, HEAD_DIM), HEAD_DIM)
        qx[u, :HEAD_DIM, :] = qt_ref[rows, :]
        kx[u, :HEAD_DIM, :] = kt_ref[rows, :]
        vx[u, :HEAD_DIM, :] = vt_ref[rows, :]
        kn[u] = kx[u].T

    def norm_bound(ref, u):
        value = ref[u, :HEAD_DIM, :].astype(F32)
        return jnp.max(jnp.sum(value * value, 0, keepdims=True))

    def head(h, u, safe):
        rows = pl.ds(pl.multiple_of(h * HEAD_DIM, HEAD_DIM), HEAD_DIM)
        for t in range(length // TILE):
            low, high = max(0, t * TILE - REACH), min(length, (t + 1) * TILE + REACH)
            cols = slice(t * TILE, (t + 1) * TILE)
            if safe:
                highest = jnp.full((1, TILE), -BIG, F32)
                for k in range(low, high, TILE):
                    scores = dot(kn[u, k : k + TILE, :], qx[u, :, cols], NN)
                    highest = jnp.maximum(highest, jnp.max(scores, 0, keepdims=True))
            probs = []
            for k in range(low, high, TILE):
                scores = dot(kn[u, k : k + TILE, :], qx[u, :, cols], NN)
                if safe:
                    scores = scores - highest
                probs.append(jnp.exp2(scores * LOG2E).astype(BF))
            out = dot(vx[u, :, low:high], jnp.concatenate(probs, 0), NN)
            total = out[HEAD_DIM : HEAD_DIM + 1, :]
            ot_ref[rows, cols] = (out[:HEAD_DIM, :] * (1.0 / total)).astype(BF)
            log_sum = jnp.log(total)
            if safe:
                log_sum = log_sum + highest
            lse_ref[pl.ds(h, 1), cols] = log_sum

    def step(i, carry):
        bound = 0.0
        for u in range(FWD_UNROLL):
            load(i * FWD_UNROLL + u, u)
            bound = jnp.maximum(bound, norm_bound(qx, u) * norm_bound(kx, u))

        @pl.when(bound < SAFE_SCORE**2)
        def _():
            for u in range(FWD_UNROLL):
                head(i * FWD_UNROLL + u, u, False)

        @pl.when(jnp.logical_not(bound < SAFE_SCORE**2))
        def _():
            lax.fori_loop(0, FWD_UNROLL, lambda u, c: (head(i * FWD_UNROLL + u, u, True), c)[1], 0)

        return carry

    lax.fori_loop(0, heads // FWD_UNROLL, step, 0)


def attend(x, seg, gains, shifts, weights, bias):
    tokens, width = x.shape
    rows, _, length = seg.shape
    row = pl.BlockSpec((length, width), lambda r: (r, 0))
    col = pl.BlockSpec((width, length), lambda r: (0, r))
    return pl.pallas_call(
        attend_kernel,
        grid=(rows,),
        in_specs=[row, pl.BlockSpec((1, 1, length), lambda r: (r, 0, 0)), WHOLE, WHOLE, WHOLE, WHOLE],
        out_specs=[row, col, col, col, col, pl.BlockSpec((16, length), lambda r: (0, r))],
        out_shape=[shape_of((tokens, width), BF)]
        + [shape_of((width, tokens), BF)] * 4
        + [shape_of((16, tokens), F32)],
        scratch_shapes=[pltpu.VMEM((FWD_UNROLL, HEAD_DIM + EXTRA, length), BF)] * 3
        + [pltpu.VMEM((FWD_UNROLL, length, HEAD_DIM + EXTRA), BF)],
        compiler_params=params(),
        name="attend",
    )(x, seg, gains, shifts, weights, bias)


def split3(value):
    first = value.astype(BF)
    rest = value - first.astype(F32)
    second = rest.astype(BF)
    return first, second, (rest - second.astype(F32)).astype(BF)


def attend_back_kernel(
    start_ref, seg_ref, qt_ref, kt_ref, vt_ref, ot_ref, dt_ref, lse_ref,
    dq_ref, dk_ref, dv_ref,
    qx, kx, vx, dx, qn, dn, kn, acc,
):
    length = qt_ref.shape[1]
    heads = qt_ref.shape[0] // HEAD_DIM
    row = lax.broadcasted_iota(jnp.int32, (EXTRA, length), 0)
    same = row == seg_ref[0]
    key_extra = jnp.where(same | ((row >= 8) & (row < 11)), 1.0, 0.0).astype(BF)
    value_extra = jnp.where(row < 3, 1.0, 0.0).astype(BF)
    query_extra = jnp.where(same | (row >= 8), 0.0, -BIG)

    def three_rows(value, at):
        first, second, third = split3(value)
        out = jnp.where(row == at, first.astype(F32), 0.0)
        out = jnp.where(row == at + 1, second.astype(F32), out)
        return jnp.where(row == at + 2, third.astype(F32), out)

    def head(i, u):
        h = lax.rem(start_ref[0] + i, heads)
        rows = pl.ds(pl.multiple_of(h * HEAD_DIM, HEAD_DIM), HEAD_DIM)
        qx[u, :HEAD_DIM, :] = qt_ref[rows, :]
        kx[u, :HEAD_DIM, :] = kt_ref[rows, :]
        vx[u, :HEAD_DIM, :] = vt_ref[rows, :]
        dx[u, :HEAD_DIM, :] = dt_ref[rows, :]
        inner = jnp.sum(dt_ref[rows, :].astype(F32) * ot_ref[rows, :].astype(F32), 0, keepdims=True)
        qx[u, HEAD_DIM:, :] = (query_extra + three_rows(-lse_ref[pl.ds(h, 1), :], 8)).astype(BF)
        kx[u, HEAD_DIM:, :] = key_extra
        vx[u, HEAD_DIM:, :] = value_extra
        dx[u, HEAD_DIM:, :] = three_rows(-inner, 0).astype(BF)
        qn[u] = qx[u].T
        dn[u] = dx[u].T
        kn[u] = kx[u].T
        for t in range(length // TILE):
            low, high = max(0, t * TILE - REACH), min(length, (t + 1) * TILE + REACH)
            keys = slice(t * TILE, (t + 1) * TILE)
            probs, score_grads = [], []
            for q in range(low, high, TILE):
                prob = jnp.exp2(dot(qn[u, q : q + TILE, :], kx[u, :, keys], NN) * LOG2E)
                prob_grad = dot(dn[u, q : q + TILE, :], vx[u, :, keys], NN)
                probs.append(prob.astype(BF))
                score_grads.append((prob * prob_grad).astype(BF))
            probs = jnp.concatenate(probs, 0)
            score_grads = jnp.concatenate(score_grads, 0)
            dv_ref[rows, keys] = dot(dx[u, :HEAD_DIM, low:high], probs, NN).astype(BF)
            dk_ref[rows, keys] = dot(qx[u, :HEAD_DIM, low:high], score_grads, NN).astype(BF)
            part = dot(score_grads, kx[u, :HEAD_DIM, keys], NT)
            if t == 0:
                acc[u, low:high, :] = part
                if high < length:
                    acc[u, high:, :] = jnp.zeros((length - high, HEAD_DIM), F32)
            else:
                acc[u, low:high, :] += part
        dq_ref[rows, :] = (acc[u] * HEAD_DIM**-0.5).T.astype(BF)

    def step(i, carry):
        for u in range(BWD_UNROLL):
            head(i * BWD_UNROLL + u, u)
        return carry

    lax.fori_loop(0, heads // BWD_UNROLL, step, 0)


def attend_back(start, seg, qt, kt, vt, ot, dt, lse):
    width, tokens = qt.shape
    rows, _, length = seg.shape
    col = pl.BlockSpec((width, length), lambda r: (0, r))
    wide = HEAD_DIM + EXTRA
    return pl.pallas_call(
        attend_back_kernel,
        grid=(rows,),
        in_specs=[SCALARS, pl.BlockSpec((1, 1, length), lambda r: (r, 0, 0))]
        + [col] * 5
        + [pl.BlockSpec((16, length), lambda r: (0, r))],
        out_specs=[col] * 3,
        out_shape=[shape_of((width, tokens), BF)] * 3,
        scratch_shapes=[pltpu.VMEM((BWD_UNROLL, wide, length), BF)] * 4
        + [pltpu.VMEM((BWD_UNROLL, length, wide), BF)] * 3
        + [pltpu.VMEM((BWD_UNROLL, length, HEAD_DIM), F32)],
        compiler_params=params(),
        name="attend_back",
    )(start, seg, qt, kt, vt, ot, dt, lse)


def mix_kernel(x_ref, ot_ref, wo_ref, bias_ref, gain_ref, shift_ref, mixed_ref, h2_ref):
    mixed = x_ref[...].astype(F32) + dot(ot_ref[...], wo_ref[...], TN) + bias_ref[0:1, :]
    mixed_ref[...] = mixed
    normed, _ = standardize(mixed)
    h2_ref[...] = (normed * gain_ref[1:2, :] + shift_ref[1:2, :]).astype(BF)


def mix(x, ot, wo, biases, gains, shifts):
    tokens, width = x.shape
    row = pl.BlockSpec((TILE, width), lambda t: (t, 0))
    col = pl.BlockSpec((width, TILE), lambda t: (0, t))
    return pl.pallas_call(
        mix_kernel,
        grid=(tokens // TILE,),
        in_specs=[row, col, WHOLE, WHOLE, WHOLE, WHOLE],
        out_specs=[row, row],
        out_shape=[shape_of((tokens, width), F32), shape_of((tokens, width), BF)],
        compiler_params=params(),
        name="mix",
    )(x, ot, wo, biases, gains, shifts)


GELU_C = 0.7978845608028654
GELU_A = 0.044715


def gelu_both(pre):
    square = pre * pre
    half = 0.5 + 0.5 * jnp.tanh(pre * (GELU_C + (GELU_C * GELU_A) * square))
    act = pre * half
    slope = half + act * (1.0 - half) * (2.0 * GELU_C + (6.0 * GELU_C * GELU_A) * square)
    return act, slope


def mlp_kernel(
    me_ref, h2_ref, g_ref, up_ref, down_ref, bias_ref,
    res_ref, hg_ref, upg_ref, downg_ref, upbg_ref,
    up_low, down_low,
):
    j = pl.program_id(0)
    tokens = h2_ref.shape[0]
    up_low[...] = up_ref[0].astype(BF)
    down_low[...] = down_ref[0].astype(BF)

    def tiles(own):
        def tile(i, carry):
            rows = pl.ds(pl.multiple_of(i * TILE, TILE), TILE)
            h2 = h2_ref[rows, :]
            g = g_ref[rows, :]
            pre = dot(h2, up_low[...], NN) + bias_ref[0]
            act, slope = gelu_both(pre)
            act = act.astype(BF)
            pre_grad = (dot(g, down_low[...], NT) * slope).astype(BF)
            res = dot(act, down_low[...], NN)
            hg = dot(pre_grad, up_low[...], NT)
            if own:
                res_ref[rows, :] = res
                hg_ref[rows, :] = hg
                downg_ref[...] += dot(act, g, TN)
                upg_ref[...] += dot(h2, pre_grad, TN)
                upbg_ref[...] += jnp.sum(pre_grad.astype(F32), 0, keepdims=True)
            else:
                res_ref[rows, :] += res
                hg_ref[rows, :] += hg
            return carry

        lax.fori_loop(0, tokens // TILE, tile, 0)

    @pl.when(j == 0)
    def _():
        upg_ref[...] = jnp.zeros_like(upg_ref)
        downg_ref[...] = jnp.zeros_like(downg_ref)
        upbg_ref[...] = jnp.zeros_like(upbg_ref)
        tiles(True)

    @pl.when(j > 0)
    def _():
        tiles(False)


def mlp(me, h2, g, up, down, bias):
    tokens, width = h2.shape
    parts, _, ff = up.shape
    pick = lambda j, me: (lax.rem(me[0] + j, parts), 0, 0)
    return pl.pallas_call(
        mlp_kernel,
        grid_spec=pltpu.PrefetchScalarGridSpec(
            num_scalar_prefetch=1,
            grid=(parts,),
            in_specs=[
                WHOLE,
                WHOLE,
                pl.BlockSpec((1, width, ff), pick),
                pl.BlockSpec((1, ff, width), pick),
                pl.BlockSpec((1, 1, ff), pick),
            ],
            out_specs=[WHOLE] * 5,
            scratch_shapes=[pltpu.VMEM((width, ff), BF), pltpu.VMEM((ff, width), BF)],
        ),
        out_shape=[
            shape_of((tokens, width), F32),
            shape_of((tokens, width), F32),
            shape_of((width, ff), F32),
            shape_of((ff, width), F32),
            shape_of((1, ff), F32),
        ],
        compiler_params=params(),
        name="mlp",
    )(me, h2, g, up, down, bias)


def mix_back_kernel(
    me_ref, mixed_ref, res_ref, hg_ref, g_ref, ot_ref, wo_ref, bias_ref, gain_ref,
    result_ref, mg_ref, dt_ref, owg_ref, sums_ref,
):
    @pl.when(pl.program_id(0) == 0)
    def _():
        owg_ref[...] = jnp.zeros_like(owg_ref)
        sums_ref[...] = jnp.zeros_like(sums_ref)

    mixed = mixed_ref[...]
    g = g_ref[...].astype(F32)
    result_ref[...] = (mixed + res_ref[...] + bias_ref[1:2, :]).astype(BF)
    normed, inv_std = standardize(mixed)
    hg = hg_ref[...]
    mg = g + norm_back(hg, normed, inv_std, gain_ref[1:2, :])
    mg_ref[...] = mg
    low = mg.astype(BF)
    dt_ref[...] = dot(wo_ref[...], low, NT).astype(BF)
    owg_ref[...] += dot(ot_ref[...], low, NN)
    sums_ref[0:1, :] += jnp.sum(hg * normed, 0, keepdims=True)
    sums_ref[1:2, :] += jnp.sum(hg, 0, keepdims=True)
    sums_ref[2:3, :] += jnp.sum(mg, 0, keepdims=True)
    sums_ref[3:4, :] += jnp.sum(g, 0, keepdims=True)


def mix_back(me, mixed, res, hg, g, ot, wo, biases, gains, own):
    tokens, width = mixed.shape
    row = pl.BlockSpec((TILE, width), lambda t, me: (t, 0))
    return pl.pallas_call(
        mix_back_kernel,
        grid_spec=pltpu.PrefetchScalarGridSpec(
            num_scalar_prefetch=1,
            grid=(tokens // TILE,),
            in_specs=[row, row, row, row, pl.BlockSpec((own, TILE), lambda t, me: (me[0], t)), WHOLE, WHOLE, WHOLE],
            out_specs=[row, row, pl.BlockSpec((width, TILE), lambda t, me: (0, t)), WHOLE, WHOLE],
        ),
        out_shape=[
            shape_of((tokens, width), BF),
            shape_of((tokens, width), F32),
            shape_of((width, tokens), BF),
            shape_of((own, width), F32),
            shape_of((8, width), F32),
        ],
        compiler_params=params(),
        name="mix_back",
    )(me, mixed, res, hg, g, ot, wo, biases, gains)


def token_kernel(
    me_ref, dq_ref, dk_ref, dv_ref, dqo_ref, dko_ref, dvo_ref, w_ref, x_ref, h1_ref, mg_ref, gain_ref,
    tg_ref, qkvg_ref, sums_ref, rowsum_ref,
):
    @pl.when(pl.program_id(0) == 0)
    def _():
        qkvg_ref[...] = jnp.zeros_like(qkvg_ref)
        sums_ref[...] = jnp.zeros_like(sums_ref)
        rowsum_ref[...] = jnp.zeros_like(rowsum_ref)

    width = x_ref.shape[1]
    hg = dot(dq_ref[...], w_ref[:width, :], TN)
    hg += dot(dk_ref[...], w_ref[width : 2 * width, :], TN)
    hg += dot(dv_ref[...], w_ref[2 * width :, :], TN)
    normed, inv_std = standardize(x_ref[...].astype(F32))
    tg_ref[...] = mg_ref[...] + norm_back(hg, normed, inv_std, gain_ref[0:1, :])
    sums_ref[0:1, :] += jnp.sum(hg * normed, 0, keepdims=True)
    sums_ref[1:2, :] += jnp.sum(hg, 0, keepdims=True)
    h1 = h1_ref[...]
    ones = jnp.ones((h1.shape[0], 128), BF)
    for j, ref in enumerate((dqo_ref, dko_ref, dvo_ref)):
        qkvg_ref[j] += dot(ref[...], h1, NN)
        if j != 1:
            rowsum_ref[j // 2] += dot(ref[...], ones, NN)


def token_back(me, dq, dk, dv, weights, x, h1, mg, gains, own):
    tokens, width = x.shape
    row = pl.BlockSpec((TILE, width), lambda t, me: (t, 0))
    col = pl.BlockSpec((width, TILE), lambda t, me: (0, t))
    mine = pl.BlockSpec((own, TILE), lambda t, me: (me[0], t))
    return pl.pallas_call(
        token_kernel,
        grid_spec=pltpu.PrefetchScalarGridSpec(
            num_scalar_prefetch=1,
            grid=(tokens // TILE,),
            in_specs=[col, col, col, mine, mine, mine, WHOLE, row, row, row, WHOLE],
            out_specs=[row, WHOLE, WHOLE, WHOLE],
        ),
        out_shape=[
            shape_of((tokens, width), F32),
            shape_of((3, own, width), F32),
            shape_of((8, width), F32),
            shape_of((2, own, 128), F32),
        ],
        compiler_params=params(),
        name="token_back",
    )(me, dq, dk, dv, dq, dk, dv, weights, x, h1, mg, gains)


def body(
    dp_size,
    tokens,
    segments,
    norm_gains,
    norm_shifts,
    qkv_weight,
    qv_bias,
    out_weight,
    out_biases,
    up_weight,
    up_bias,
    down_weight,
    cotangent,
):
    width = tokens.shape[1]
    own = qkv_weight.shape[2]
    ff = up_weight.shape[1]
    me = lax.axis_index("mp").astype(jnp.int32).reshape(1)
    seg = segments.reshape(segments.shape[0], 1, segments.shape[1])
    slab = jnp.concatenate(
        [qkv_weight.transpose(0, 2, 1).reshape(3 * own, width), out_weight, up_weight, down_weight], 0
    )
    share = slab.shape[0] // dp_size
    piece = lax.dynamic_slice_in_dim(slab, lax.axis_index("dp") * share, share, 0)
    gathered = lax.all_gather(piece, ("mp", "dp"), tiled=True).reshape(-1, slab.shape[0], width)
    small = jnp.concatenate([jnp.pad(qv_bias, ((0, 0), (0, width - own))), up_bias.reshape(1, ff)], 0)
    smalls = lax.all_gather(small, "mp")
    parts = gathered.shape[0]
    qkv_t = gathered[:, : 3 * own].reshape(parts, 3, own, width).transpose(1, 0, 2, 3).reshape(3 * parts * own, width)
    weights = cast_low(qkv_t)
    wo = cast_low(gathered[:, 3 * own : 4 * own].reshape(parts * own, width))
    up = gathered[:, 4 * own : 4 * own + width]
    down = gathered[:, 4 * own + width :]
    full_bias = smalls[:, :2, :own].transpose(1, 0, 2).reshape(2, parts * own)
    bias = jnp.concatenate([full_bias[0], jnp.zeros_like(full_bias[0]), full_bias[1]]).reshape(-1, 1)
    h1, qt, kt, vt, ot, lse = attend(tokens, seg, norm_gains, norm_shifts, weights, bias)
    mixed, h2 = mix(tokens, ot, wo, out_biases, norm_gains, norm_shifts)
    res, hg, up_grad, down_grad, up_bias_grad = mlp(me, h2, cotangent, up, down, smalls[:, 2:3, :])
    result, mg, dt, out_weight_grad, sums_two = mix_back(
        me, mixed, res, hg, cotangent, ot, wo, out_biases, norm_gains, own
    )
    up_grad, down_grad, out_weight_grad, up_bias_grad = lax.psum(
        (up_grad, down_grad, out_weight_grad, up_bias_grad), "dp"
    )
    dq, dk, dv = attend_back(me * (own // HEAD_DIM), seg, qt, kt, vt, ot, dt, lse)
    token_grad, qkv_grad, sums_one, row_sums = token_back(
        me, dq, dk, dv, weights, tokens, h1, mg, norm_gains, own
    )
    qkv_grad, sums_one, sums_two, row_sums = lax.psum(
        (qkv_grad, sums_one[:2], sums_two[:4], row_sums[:, :, 0]), "dp"
    )
    return (
        result,
        token_grad,
        jnp.stack([sums_one[0], sums_two[0]]),
        jnp.stack([sums_one[1], sums_two[1]]),
        qkv_grad.transpose(0, 2, 1),
        row_sums,
        out_weight_grad,
        sums_two[2:4],
        up_grad,
        up_bias_grad.reshape(ff),
        down_grad,
    )


def solution(mesh):
    in_specs = (
        P("dp", None),
        P("dp", None),
        P(),
        P(),
        P(None, None, "mp"),
        P(None, "mp"),
        P("mp", None),
        P(),
        P(None, "mp"),
        P("mp"),
        P("mp", None),
        P("dp", None),
    )
    out_specs = (
        P("dp", None),
        P("dp", None),
        P(),
        P(),
        P(None, None, "mp"),
        P(None, "mp"),
        P("mp", None),
        P(),
        P(None, "mp"),
        P("mp"),
        P("mp", None),
    )
    return jax.shard_map(
        partial(body, mesh.shape["dp"]), mesh=mesh, in_specs=in_specs, out_specs=out_specs, check_vma=False
    )
```

```python
from functools import partial

import jax
import jax.numpy as jnp
from jax import lax
from jax.experimental import pallas as pl
from jax.experimental.pallas import tpu as pltpu
from jax.sharding import PartitionSpec as P

F32 = jnp.float32
BF = jnp.bfloat16
HEAD_DIM = 64
NORM_EPSILON = 1e-06
BIG = 1e30
LOG2E = 1.4426950408889634
SAFE_SCORE = 60.0
REACH = 512
TILE = 256
EXTRA = 16
FWD_UNROLL = 4
BWD_UNROLL = 3

NN = (((1,), (0,)), ((), ()))
NT = (((1,), (1,)), ((), ()))
TN = (((0,), (0,)), ((), ()))
WHOLE = pl.BlockSpec(memory_space=pltpu.VMEM)
SCALARS = pl.BlockSpec(memory_space=pltpu.SMEM)


def dot(left, right, dims):
    return lax.dot_general(left, right, dims, preferred_element_type=F32)


def params(mib=56):
    return pltpu.CompilerParams(vmem_limit_bytes=mib * 2**20)


def standardize(values):
    centered = values - jnp.mean(values, -1, keepdims=True)
    inv_std = lax.rsqrt(jnp.mean(centered * centered, -1, keepdims=True) + NORM_EPSILON)
    return centered * inv_std, inv_std


def norm_back(grad_in, normed, inv_std, gain):
    scaled = grad_in * gain
    return inv_std * (
        scaled
        - jnp.mean(scaled, -1, keepdims=True)
        - normed * jnp.mean(scaled * normed, -1, keepdims=True)
    )


def shape_of(shape, dtype):
    return jax.ShapeDtypeStruct(shape, dtype)


def flip(index, bit):
    return index + bit - 2 * bit * lax.rem(lax.div(index, bit), 2)


def remote(src, dst, send_sem, recv_sem, **where):
    return pltpu.make_async_remote_copy(
        src_ref=src, dst_ref=dst, send_sem=send_sem, recv_sem=recv_sem, device_id=where,
        device_id_type=pl.DeviceIdType.MESH,
    )


CORE, SIDE, ACROSS, DIAG_A, DIAG_B, CORE_SIDE, CORE_ACROSS, CORE_A, CORE_B = range(9)


class Spread:
    def __init__(self, piece, send_sems, recv_sems, mine=None):
        self.piece, self.send_sems, self.recv_sems, self.mine = piece, send_sems, recv_sems, mine
        self.device = lax.axis_index("dp")
        self.place = lax.rem(self.device, 8)

    def copy(self, chunk, kind, origin, bit, half=None):
        ref = self.piece(chunk, origin, half)
        own = self.mine is not None and kind in (CORE, SIDE, ACROSS)
        return remote(
            self.mine(chunk) if own else ref, ref, self.send_sems.at[chunk, kind], self.recv_sems.at[chunk, kind], dp=flip(self.device, bit)
        )

    def origin(self, bits):
        place = self.place
        for bit in bits:
            place = flip(place, bit)
        return place

    def outgoing(self, chunk, kind):
        bits, bit, half = {
            CORE: ((), 1, None),
            SIDE: ((), 2, None),
            ACROSS: ((), 4, None),
            DIAG_A: ((2,), 4, 0),
            DIAG_B: ((4,), 2, 1),
            CORE_SIDE: ((2,), 1, None),
            CORE_ACROSS: ((4,), 1, None),
            CORE_A: ((2, 4), 1, 0),
            CORE_B: ((2, 4), 1, 1),
        }[kind]
        return self.copy(chunk, kind, self.origin(bits), bit, half)

    def incoming(self, chunk, kind):
        bits, bit, half = {
            CORE: ((1,), 1, None),
            SIDE: ((2,), 2, None),
            ACROSS: ((4,), 4, None),
            DIAG_A: ((2, 4), 4, 0),
            DIAG_B: ((2, 4), 2, 1),
            CORE_SIDE: ((1, 2), 1, None),
            CORE_ACROSS: ((1, 4), 1, None),
            CORE_A: ((1, 2, 4), 1, 0),
            CORE_B: ((1, 2, 4), 1, 1),
        }[kind]
        return self.copy(chunk, kind, self.origin(bits), bit, half)

    def start(self, chunk, *kinds):
        for kind in kinds:
            self.outgoing(chunk, kind).start()

    def arrived(self, chunk, *kinds):
        for kind in kinds:
            self.incoming(chunk, kind).wait_recv()

    def send(self, chunk):
        self.start(chunk, SIDE, ACROSS, CORE)

    def forward(self, chunk):
        self.arrived(chunk, SIDE)
        self.start(chunk, DIAG_A, CORE_SIDE)
        self.arrived(chunk, ACROSS)
        self.start(chunk, DIAG_B, CORE_ACROSS)

    def corner(self, chunk):
        self.arrived(chunk, DIAG_A)
        self.start(chunk, CORE_A)
        self.arrived(chunk, DIAG_B)
        self.start(chunk, CORE_B)

    def complete(self, chunk):
        self.arrived(chunk, CORE, CORE_SIDE, CORE_ACROSS, CORE_A, CORE_B)

    def sent(self, chunk):
        for kind in range(9):
            self.outgoing(chunk, kind).wait_send()


def greet(*peers):
    barrier = pltpu.get_barrier_semaphore()
    for peer in peers:
        pl.semaphore_signal(barrier, inc=1, device_id=peer, device_id_type=pl.DeviceIdType.MESH)
    pl.semaphore_wait(barrier, len(peers))


def foreign_order(me):
    half = lax.div(me, 2)
    return flip(me, 1), 2 - half, 3 - 3 * half


def gather_kernel(
    slab_ref, small_ref, w_ref, bias_ref, smalls_ref,
    land, small_land, z_send, z_recv, own_send, small_send, small_recv, send_sems, recv_sems,
):
    parts, rows, width = land.shape
    own = rows // 3
    share = rows // 8
    split = (0, share // 2 + 4, share)
    me = lax.axis_index("mp")
    device = lax.axis_index("dp")
    greet(
        *[{"mp": lax.rem(me + s, parts)} for s in range(1, parts)],
        *[{"dp": flip(device, bit)} for bit in (1, 2, 4)],
    )
    order = foreign_order(me)

    def rows_of(c, origin, half=None):
        start, stop = split[c % 2], split[c % 2 + 1]
        middle = start + (stop - start + 8) // 16 * 8
        if half is not None:
            start, stop = (start, middle) if half == 0 else (middle, stop)
        return pl.ds(pl.multiple_of(origin * share + start, 8), stop - start)

    def piece(c, origin, half):
        return land.at[order[c // 2], rows_of(c, origin, half), :]

    spread = Spread(piece, send_sems, recv_sems)

    def own_copy(h, up):
        rows = rows_of(h, spread.place)
        return remote(
            slab_ref.at[rows, :], land.at[me, rows, :], own_send.at[h, up], z_recv.at[me * 2 + h], mp=me + 2 * up - 1
        )

    def on_copy(c, step):
        ref = piece(c, spread.place, None)
        chunk = order[c // 2] * 2 + c % 2
        return remote(ref, ref, z_send.at[chunk], z_recv.at[chunk], mp=me + step)

    for h in range(2):
        @pl.when(me < parts - 1)
        def _():
            own_copy(h, 1).start()

        @pl.when(me > 0)
        def _():
            own_copy(h, 0).start()

    def small_copy(s):
        return remote(
            small_ref, small_land.at[me], small_send.at[s - 1], small_recv.at[me], mp=lax.rem(me + s, parts)
        )

    for s in range(1, parts):
        small_copy(s).start()

    def pass_on(c, act):
        source = order[c // 2]

        @pl.when((source < me) & (me < parts - 1))
        def _():
            act(on_copy(c, 1))

        @pl.when((source > me) & (me > 0))
        def _():
            act(on_copy(c, -1))

    def landed(c):
        on_copy(c, 0).wait_recv()
        pass_on(c, lambda copy: copy.start())
        spread.send(c)

    def use(source, ref):
        for j in range(3):
            at = pl.multiple_of((j * parts + lax.rem(source - me + parts, parts)) * own, own)
            w_ref[pl.ds(at, own), :] = ref[j * own : (j + 1) * own, :].astype(BF)

    use(me, slab_ref)
    small_land[me] = small_ref[...]
    landed(0)
    landed(1)
    last = 5
    for c in range(last + 1):
        spread.forward(c)
        if c + 2 <= last:
            landed(c + 2)
        if c > 0:
            spread.corner(c - 1)
    spread.corner(last)
    for s in range(1, parts):
        other = lax.rem(me + s, parts)
        remote(small_ref, small_land.at[other], small_send.at[0], small_recv.at[other], mp=me).wait_recv()
    bias_ref[...] = jnp.zeros_like(bias_ref)
    for source in range(parts):
        cols = small_land[source].T
        place = lax.rem(source - me + parts, parts)
        for j in range(2):
            at = pl.multiple_of((2 * j * parts + place) * own, own)
            bias_ref[pl.ds(at, own), :] = cols[:own, j : j + 1]
    smalls_ref[...] = small_land[...]
    for j in range(3):
        for h in range(2):
            spread.complete(2 * j + h)
        use(order[j], land.at[order[j]])
    for c in range(last + 1):
        spread.sent(c)
        pass_on(c, lambda copy: copy.wait_send())
    for s in range(1, parts):
        small_copy(s).wait_send()
    for h in range(2):
        @pl.when(me < parts - 1)
        def _():
            own_copy(h, 1).wait_send()

        @pl.when(me > 0)
        def _():
            own_copy(h, 0).wait_send()


def gather(slab, small, parts):
    rows, width = slab.shape
    dma = pltpu.SemaphoreType.DMA
    return pl.pallas_call(
        gather_kernel,
        in_specs=[WHOLE, WHOLE],
        out_specs=[WHOLE] * 3,
        out_shape=[
            shape_of((rows * parts, width), BF),
            shape_of((rows * parts, 1), F32),
            shape_of((parts,) + small.shape, F32),
        ],
        scratch_shapes=[
            pltpu.VMEM((parts, rows, width), F32),
            pltpu.VMEM((parts,) + small.shape, F32),
            dma((2 * parts,)),
            dma((2 * parts,)),
            dma((2, 2)),
            dma((parts - 1,)),
            dma((parts,)),
            dma((2 * parts, 9)),
            dma((2 * parts, 9)),
        ],
        compiler_params=pltpu.CompilerParams(vmem_limit_bytes=56 * 2**20, collective_id=0, has_side_effects=True),
        name="gather",
    )(slab, small)


def attend_kernel(
    x_ref, seg_ref, gain_ref, shift_ref, w_ref, b_ref,
    h1_ref, qt_ref, kt_ref, vt_ref, ot_ref, lse_ref,
    qx, kx, vx, kn,
):
    length, width = x_ref.shape
    heads = width // HEAD_DIM
    normed, _ = standardize(x_ref[...].astype(F32))
    h1_ref[...] = (normed * gain_ref[0:1, :] + shift_ref[0:1, :]).astype(BF)
    for j, out in enumerate((qt_ref, kt_ref, vt_ref)):
        value = dot(w_ref[j * width : (j + 1) * width, :], h1_ref[...], NT)
        if j != 1:
            value = value + b_ref[j * width : (j + 1) * width, :]
        value = value.astype(BF)
        if j == 0:
            value = value * jnp.asarray(HEAD_DIM**-0.5, BF)
        out[...] = value
    row = lax.broadcasted_iota(jnp.int32, (EXTRA, length), 0)
    same = row == seg_ref[0]
    for u in range(FWD_UNROLL):
        qx[u, HEAD_DIM:, :] = jnp.where(same | (row >= 8), 0.0, -BIG).astype(BF)
        kx[u, HEAD_DIM:, :] = jnp.where(same, 1.0, 0.0).astype(BF)
        vx[u, HEAD_DIM:, :] = jnp.ones((EXTRA, length), BF)

    def load(h, u):
        rows = pl.ds(pl.multiple_of(h * HEAD_DIM, HEAD_DIM), HEAD_DIM)
        qx[u, :HEAD_DIM, :] = qt_ref[rows, :]
        kx[u, :HEAD_DIM, :] = kt_ref[rows, :]
        vx[u, :HEAD_DIM, :] = vt_ref[rows, :]
        kn[u] = kx[u].T

    def norm_bound(ref, u):
        value = ref[u, :HEAD_DIM, :].astype(F32)
        return jnp.max(jnp.sum(value * value, 0, keepdims=True))

    def head(h, u, safe):
        rows = pl.ds(pl.multiple_of(h * HEAD_DIM, HEAD_DIM), HEAD_DIM)
        for t in range(length // TILE):
            low, high = max(0, t * TILE - REACH), min(length, (t + 1) * TILE + REACH)
            cols = slice(t * TILE, (t + 1) * TILE)
            if safe:
                highest = jnp.full((1, TILE), -BIG, F32)
                for k in range(low, high, TILE):
                    scores = dot(kn[u, k : k + TILE, :], qx[u, :, cols], NN)
                    highest = jnp.maximum(highest, jnp.max(scores, 0, keepdims=True))
            probs = []
            for k in range(low, high, TILE):
                scores = dot(kn[u, k : k + TILE, :], qx[u, :, cols], NN)
                if safe:
                    scores = scores - highest
                probs.append(jnp.exp2(scores * LOG2E).astype(BF))
            out = dot(vx[u, :, low:high], jnp.concatenate(probs, 0), NN)
            total = out[HEAD_DIM : HEAD_DIM + 1, :]
            ot_ref[rows, cols] = (out[:HEAD_DIM, :] * (1.0 / total)).astype(BF)
            log_sum = jnp.log(total)
            if safe:
                log_sum = log_sum + highest
            lse_ref[pl.ds(h, 1), cols] = log_sum

    def step(i, carry):
        bound = 0.0
        for u in range(FWD_UNROLL):
            load(i * FWD_UNROLL + u, u)
            bound = jnp.maximum(bound, norm_bound(qx, u) * norm_bound(kx, u))

        @pl.when(bound < SAFE_SCORE**2)
        def _():
            for u in range(FWD_UNROLL):
                head(i * FWD_UNROLL + u, u, False)

        @pl.when(jnp.logical_not(bound < SAFE_SCORE**2))
        def _():
            lax.fori_loop(0, FWD_UNROLL, lambda u, c: (head(i * FWD_UNROLL + u, u, True), c)[1], 0)

        return carry

    lax.fori_loop(0, heads // FWD_UNROLL, step, 0)


def attend(x, seg, gains, shifts, weights, bias):
    tokens, width = x.shape
    rows, _, length = seg.shape
    row = pl.BlockSpec((length, width), lambda r: (r, 0))
    col = pl.BlockSpec((width, length), lambda r: (0, r))
    return pl.pallas_call(
        attend_kernel,
        grid=(rows,),
        in_specs=[row, pl.BlockSpec((1, 1, length), lambda r: (r, 0, 0)), WHOLE, WHOLE, WHOLE, WHOLE],
        out_specs=[row, col, col, col, col, pl.BlockSpec((16, length), lambda r: (0, r))],
        out_shape=[shape_of((tokens, width), BF)]
        + [shape_of((width, tokens), BF)] * 4
        + [shape_of((16, tokens), F32)],
        scratch_shapes=[pltpu.VMEM((FWD_UNROLL, HEAD_DIM + EXTRA, length), BF)] * 3
        + [pltpu.VMEM((FWD_UNROLL, length, HEAD_DIM + EXTRA), BF)],
        compiler_params=params(),
        name="attend",
    )(x, seg, gains, shifts, weights, bias)


def split3(value):
    first = value.astype(BF)
    rest = value - first.astype(F32)
    second = rest.astype(BF)
    return first, second, (rest - second.astype(F32)).astype(BF)


def attend_back_kernel(
    start_ref, seg_ref, qt_ref, kt_ref, vt_ref, ot_ref, dt_ref, lse_ref,
    dq_ref, dk_ref, dv_ref,
    qx, kx, vx, dx, qn, dn, kn, acc,
):
    length = qt_ref.shape[1]
    heads = qt_ref.shape[0] // HEAD_DIM
    row = lax.broadcasted_iota(jnp.int32, (EXTRA, length), 0)
    same = row == seg_ref[0]
    key_extra = jnp.where(same | ((row >= 8) & (row < 11)), 1.0, 0.0).astype(BF)
    value_extra = jnp.where(row < 3, 1.0, 0.0).astype(BF)
    query_extra = jnp.where(same | (row >= 8), 0.0, -BIG)

    def three_rows(value, at):
        first, second, third = split3(value)
        out = jnp.where(row == at, first.astype(F32), 0.0)
        out = jnp.where(row == at + 1, second.astype(F32), out)
        return jnp.where(row == at + 2, third.astype(F32), out)

    def head(i, u):
        h = lax.rem(start_ref[0] + i, heads)
        rows = pl.ds(pl.multiple_of(h * HEAD_DIM, HEAD_DIM), HEAD_DIM)
        qx[u, :HEAD_DIM, :] = qt_ref[rows, :]
        kx[u, :HEAD_DIM, :] = kt_ref[rows, :]
        vx[u, :HEAD_DIM, :] = vt_ref[rows, :]
        dx[u, :HEAD_DIM, :] = dt_ref[rows, :]
        inner = jnp.sum(dt_ref[rows, :].astype(F32) * ot_ref[rows, :].astype(F32), 0, keepdims=True)
        qx[u, HEAD_DIM:, :] = (query_extra + three_rows(-lse_ref[pl.ds(h, 1), :], 8)).astype(BF)
        kx[u, HEAD_DIM:, :] = key_extra
        vx[u, HEAD_DIM:, :] = value_extra
        dx[u, HEAD_DIM:, :] = three_rows(-inner, 0).astype(BF)
        qn[u] = qx[u].T
        dn[u] = dx[u].T
        kn[u] = kx[u].T
        for t in range(length // TILE):
            low, high = max(0, t * TILE - REACH), min(length, (t + 1) * TILE + REACH)
            keys = slice(t * TILE, (t + 1) * TILE)
            probs, score_grads = [], []
            for q in range(low, high, TILE):
                prob = jnp.exp2(dot(qn[u, q : q + TILE, :], kx[u, :, keys], NN) * LOG2E)
                prob_grad = dot(dn[u, q : q + TILE, :], vx[u, :, keys], NN)
                probs.append(prob.astype(BF))
                score_grads.append((prob * prob_grad).astype(BF))
            probs = jnp.concatenate(probs, 0)
            score_grads = jnp.concatenate(score_grads, 0)
            dv_ref[rows, keys] = dot(dx[u, :HEAD_DIM, low:high], probs, NN).astype(BF)
            dk_ref[rows, keys] = dot(qx[u, :HEAD_DIM, low:high], score_grads, NN).astype(BF)
            part = dot(score_grads, kx[u, :HEAD_DIM, keys], NT)
            if t == 0:
                acc[u, low:high, :] = part
                if high < length:
                    acc[u, high:, :] = jnp.zeros((length - high, HEAD_DIM), F32)
            else:
                acc[u, low:high, :] += part
        dq_ref[rows, :] = (acc[u] * HEAD_DIM**-0.5).T.astype(BF)

    def step(i, carry):
        for u in range(BWD_UNROLL):
            head(i * BWD_UNROLL + u, u)
        return carry

    lax.fori_loop(0, heads // BWD_UNROLL, step, 0)


def attend_back(start, seg, qt, kt, vt, ot, dt, lse):
    width, tokens = qt.shape
    rows, _, length = seg.shape
    col = pl.BlockSpec((width, length), lambda r: (0, r))
    wide = HEAD_DIM + EXTRA
    return pl.pallas_call(
        attend_back_kernel,
        grid=(rows,),
        in_specs=[SCALARS, pl.BlockSpec((1, 1, length), lambda r: (r, 0, 0))]
        + [col] * 5
        + [pl.BlockSpec((16, length), lambda r: (0, r))],
        out_specs=[col] * 3,
        out_shape=[shape_of((width, tokens), BF)] * 3,
        scratch_shapes=[pltpu.VMEM((BWD_UNROLL, wide, length), BF)] * 4
        + [pltpu.VMEM((BWD_UNROLL, length, wide), BF)] * 3
        + [pltpu.VMEM((BWD_UNROLL, length, HEAD_DIM), F32)],
        compiler_params=params(),
        name="attend_back",
    )(start, seg, qt, kt, vt, ot, dt, lse)


GELU_C = 0.7978845608028654
GELU_A = 0.044715


def gelu_both(pre):
    square = pre * pre
    half = 0.5 + 0.5 * jnp.tanh(pre * (GELU_C + (GELU_C * GELU_A) * square))
    act = pre * half
    slope = half + act * (1.0 - half) * (2.0 * GELU_C + (6.0 * GELU_C * GELU_A) * square)
    return act, slope


ONCE = pl.BlockSpec(memory_space=pltpu.VMEM, pipeline_mode=pl.Buffered(1))
ANY = pl.BlockSpec(memory_space=pl.ANY)
UNIT = 256
LONG_TILE = 512
GAIN_TWO, SHIFT_TWO, BIAS_ONE, BIAS_TWO, UP_BIAS = range(5)


def mlp_kernel(
    x_ref, ot_ref, mine_ref, wo_ref, g_ref, pieces_ref, up_ref, down_ref, smalls_ref, bias_ref, gain_ref, shift_ref,
    result_ref, mg_ref, dt_ref, grads_ref,
    land, wo_low, mixed_ref, h2_ref, res_ref, hg_ref, up_low, down_low, local_sems, send_sems, recv_sems,
):
    step = pl.program_id(0)
    tokens, width = g_ref.shape
    parts, own, _ = wo_ref.shape
    ff = up_ref.shape[1]
    units = ff // UNIT
    chunks = units * (parts - 1)
    share = land.shape[2] // 8
    strip = UNIT // 8
    tiles = tokens // TILE
    first = tiles + 1
    out_at = 2 * ff
    sums_at = out_at + own
    me = lax.axis_index("mp")
    order = foreign_order(me)

    def source_of(chunk):
        j = lax.div(chunk, units)
        return jnp.where(j == 0, order[0], jnp.where(j == 1, order[1], order[2]))

    def piece(chunk, origin, half):
        rows = pl.ds(pl.multiple_of(origin * share, 8), share)
        if half is None:
            return land.at[chunk, :, rows, :]
        return land.at[chunk, half, rows, :]

    def mine(chunk):
        return pieces_ref.at[source_of(chunk), lax.rem(chunk, units)]

    spread = Spread(piece, send_sems, recv_sems, mine)

    def keep(chunk):
        return pltpu.make_async_copy(mine(chunk), piece(chunk, spread.place, None), local_sems.at[chunk])

    def serve(ahead):
        @pl.when(ahead < chunks)
        def _():
            spread.forward(ahead)

        @pl.when(ahead + 2 < chunks)
        def _():
            spread.send(ahead + 2)

        @pl.when((ahead > 0) & (ahead - 1 < chunks))
        def _():
            spread.corner(ahead - 1)

    def unit(bias, grads_at):
        def tile(i, carry):
            rows = pl.ds(pl.multiple_of(i * LONG_TILE, LONG_TILE), LONG_TILE)
            h2 = h2_ref[rows, :]
            g = g_ref[rows, :]
            pre = dot(h2, up_low[...], NN) + bias
            act, slope = gelu_both(pre)
            act = act.astype(BF)
            pre_grad = (dot(g, down_low[...], NT) * slope).astype(BF)
            res_ref[rows, :] += dot(act, down_low[...], NN)
            hg_ref[rows, :] += dot(pre_grad, up_low[...], NT)
            if grads_at is not None:
                cols = slice(grads_at, grads_at + UNIT)
                grads_ref[cols, :] += dot(act, g, TN)
                grads_ref[ff:out_at, cols] += dot(h2, pre_grad, TN)
                at = sums_at + UP_BIAS
                grads_ref[at : at + 1, cols] += jnp.sum(pre_grad.astype(F32), 0, keepdims=True)
            return carry

        lax.fori_loop(0, tokens // LONG_TILE, tile, 0)

    @pl.when(step == 0)
    def _():
        greet(*[{"dp": flip(spread.device, bit)} for bit in (1, 2, 4)])
        spread.send(0)
        spread.send(1)
        for c in range(chunks):
            keep(c).start()
        for source in range(parts):
            at = lax.rem(source - me + parts, parts) * own
            wo_low[pl.ds(pl.multiple_of(at, own), own), :] = wo_ref[source].astype(BF)
        grads_ref[...] = jnp.zeros_like(grads_ref)

    @pl.when(step < tiles)
    def _():
        rows = pl.ds(pl.multiple_of(step * TILE, TILE), TILE)
        mixed = x_ref[...].astype(F32) + dot(ot_ref[...], wo_low[...], TN) + bias_ref[0:1, :]
        mixed_ref[rows, :] = mixed
        res_ref[rows, :] = mixed + bias_ref[1:2, :]
        hg_ref[rows, :] = jnp.zeros((TILE, width), F32)
        normed, _ = standardize(mixed)
        h2_ref[rows, :] = (normed * gain_ref[1:2, :] + shift_ref[1:2, :]).astype(BF)

    @pl.when(step == tiles - 1)
    def _():
        serve(0)

    @pl.when(step == tiles)
    def _():
        for u in range(units):
            cols = slice(u * UNIT, (u + 1) * UNIT)
            up_low[...] = up_ref[:, cols].astype(BF)
            down_low[...] = down_ref[cols, :].astype(BF)
            unit(smalls_ref[me, 2:3, cols], u * UNIT)
            if u < 2:
                serve(u + 1)

    @pl.when((step >= first) & (step < first + chunks))
    def _():
        chunk = step - first
        keep(chunk).wait()
        spread.complete(chunk)
        up_low[...] = land[chunk, 0].astype(BF)
        for q in range(8):
            for c in range(width // UNIT):
                at = q * share + c * strip
                down_low[q * strip : (q + 1) * strip, c * UNIT : (c + 1) * UNIT] = land[
                    chunk, 1, at : at + strip, :
                ].astype(BF)
        cols = pl.ds(pl.multiple_of(lax.rem(chunk, units) * UNIT, UNIT), UNIT)
        unit(smalls_ref[source_of(chunk), 2:3, cols], None)
        serve(chunk + 3)

    @pl.when(step >= first + chunks)
    def _():
        rows = pl.ds(pl.multiple_of((step - first - chunks) * TILE, TILE), TILE)
        g = g_ref[rows, :].astype(F32)
        result_ref[...] = res_ref[rows, :].astype(BF)
        normed, inv_std = standardize(mixed_ref[rows, :])
        hg = hg_ref[rows, :]
        mg = g + norm_back(hg, normed, inv_std, gain_ref[1:2, :])
        mg_ref[...] = mg
        low = mg.astype(BF)
        dt_ref[...] = dot(wo_low[...], low, NT).astype(BF)
        grads_ref[out_at:sums_at, :] += dot(mine_ref[...], low, NN)
        for at, value in ((GAIN_TWO, hg * normed), (SHIFT_TWO, hg), (BIAS_ONE, mg), (BIAS_TWO, g)):
            grads_ref[sums_at + at : sums_at + at + 1, :] += jnp.sum(value, 0, keepdims=True)

    @pl.when(step == first + chunks + tiles - 1)
    def _():
        def done(c, carry):
            spread.sent(c)
            return carry

        lax.fori_loop(0, chunks, done, 0)


def mlp(x, ot, wo, g, pieces, up, down, smalls, biases, gains, shifts):
    tokens, width = x.shape
    parts, own, _ = wo.shape
    ff = up.shape[1]
    units = ff // UNIT
    chunks = units * (parts - 1)
    tiles = tokens // TILE
    steps = 2 * tiles + 1 + chunks
    rows = 2 * ff + own
    rows += -rows % 128 + (128 if rows % 128 > 120 or rows % 128 == 0 else 0)
    early = lambda s: jnp.minimum(s, tiles - 1)
    late = lambda s: jnp.maximum(s - (steps - tiles), 0)
    dma = pltpu.SemaphoreType.DMA
    return pl.pallas_call(
        mlp_kernel,
        grid=(steps,),
        in_specs=[
            pl.BlockSpec((TILE, width), lambda s: (early(s), 0)),
            pl.BlockSpec((width, TILE), lambda s: (0, early(s))),
            pl.BlockSpec((own, TILE), lambda s: (0, late(s))),
            ONCE, ONCE, ANY, ONCE, ONCE, ONCE, ONCE, ONCE, ONCE,
        ],
        out_specs=[
            pl.BlockSpec((TILE, width), lambda s: (late(s), 0)),
            pl.BlockSpec((TILE, width), lambda s: (late(s), 0)),
            pl.BlockSpec((width, TILE), lambda s: (0, late(s))),
            ONCE,
        ],
        out_shape=[
            shape_of((tokens, width), BF),
            shape_of((tokens, width), F32),
            shape_of((width, tokens), BF),
            shape_of((rows, width), F32),
        ],
        scratch_shapes=[
            pltpu.VMEM((chunks, 2, width, UNIT), F32),
            pltpu.VMEM((parts * own, width), BF),
            pltpu.VMEM((tokens, width), F32),
            pltpu.VMEM((tokens, width), BF),
            pltpu.VMEM((tokens, width), F32),
            pltpu.VMEM((tokens, width), F32),
            pltpu.VMEM((width, UNIT), BF),
            pltpu.VMEM((UNIT, width), BF),
            dma((chunks,)),
            dma((chunks, 9)),
            dma((chunks, 9)),
        ],
        compiler_params=pltpu.CompilerParams(vmem_limit_bytes=63 * 2**20, collective_id=1, has_side_effects=True),
        name="mlp",
    )(x, ot, ot, wo, g, pieces, up, down, smalls, biases, gains, shifts)


def token_kernel(
    me_ref, dq_ref, dk_ref, dv_ref, dqo_ref, dko_ref, dvo_ref, w_ref, x_ref, h1_ref, mg_ref, gain_ref,
    tg_ref, qkvg_ref, sums_ref, rowsum_ref,
):
    @pl.when(pl.program_id(0) == 0)
    def _():
        qkvg_ref[...] = jnp.zeros_like(qkvg_ref)
        sums_ref[...] = jnp.zeros_like(sums_ref)
        rowsum_ref[...] = jnp.zeros_like(rowsum_ref)

    width = x_ref.shape[1]
    hg = dot(dq_ref[...], w_ref[:width, :], TN)
    hg += dot(dk_ref[...], w_ref[width : 2 * width, :], TN)
    hg += dot(dv_ref[...], w_ref[2 * width :, :], TN)
    normed, inv_std = standardize(x_ref[...].astype(F32))
    tg_ref[...] = mg_ref[...] + norm_back(hg, normed, inv_std, gain_ref[0:1, :])
    sums_ref[0:1, :] += jnp.sum(hg * normed, 0, keepdims=True)
    sums_ref[1:2, :] += jnp.sum(hg, 0, keepdims=True)
    h1 = h1_ref[...]
    ones = jnp.ones((h1.shape[0], 128), BF)
    for j, ref in enumerate((dqo_ref, dko_ref, dvo_ref)):
        qkvg_ref[j] += dot(ref[...], h1, NN)
        if j != 1:
            rowsum_ref[j // 2] += dot(ref[...], ones, NN)


def token_back(me, dq, dk, dv, weights, x, h1, mg, gains, own):
    tokens, width = x.shape
    row = pl.BlockSpec((TILE, width), lambda t, me: (t, 0))
    col = pl.BlockSpec((width, TILE), lambda t, me: (0, t))
    mine = pl.BlockSpec((own, TILE), lambda t, me: (0, t))
    return pl.pallas_call(
        token_kernel,
        grid_spec=pltpu.PrefetchScalarGridSpec(
            num_scalar_prefetch=1,
            grid=(tokens // TILE,),
            in_specs=[col, col, col, mine, mine, mine, WHOLE, row, row, row, WHOLE],
            out_specs=[row, WHOLE, WHOLE, WHOLE],
        ),
        out_shape=[
            shape_of((tokens, width), F32),
            shape_of((3, own, width), F32),
            shape_of((8, width), F32),
            shape_of((2, own, 128), F32),
        ],
        compiler_params=params(),
        name="token_back",
    )(me, dq, dk, dv, dq, dk, dv, weights, x, h1, mg, gains)


def body(
    dp_size,
    tokens,
    segments,
    norm_gains,
    norm_shifts,
    qkv_weight,
    qv_bias,
    out_weight,
    out_biases,
    up_weight,
    up_bias,
    down_weight,
    cotangent,
):
    width = tokens.shape[1]
    own = qkv_weight.shape[2]
    ff = up_weight.shape[1]
    parts = width // own
    me = lax.axis_index("mp").astype(jnp.int32).reshape(1)
    place = lax.rem(lax.axis_index("dp"), 8)
    seg = segments.reshape(segments.shape[0], 1, segments.shape[1])
    out_piece = lax.dynamic_slice_in_dim(out_weight, place * (own // 8), own // 8, 0)
    wo = lax.all_gather(out_piece, ("mp", "dp"), tiled=True) if dp_size == 8 else lax.all_gather(
        out_weight, "mp", tiled=True
    )
    share, units, strip = width // 8, ff // UNIT, UNIT // 8
    up_piece = lax.dynamic_slice_in_dim(up_weight, place * share, share, 0).reshape(share, units, UNIT)
    down_piece = lax.dynamic_slice_in_dim(down_weight.reshape(units, 8, strip, -1, UNIT), place, 1, 1)
    down_piece = down_piece.reshape(units, strip, -1, UNIT).transpose(0, 2, 1, 3).reshape(units, share, UNIT)
    pieces = lax.all_gather(jnp.stack([up_piece.transpose(1, 0, 2), down_piece], 1), "mp")
    slab = qkv_weight.transpose(0, 2, 1).reshape(3 * own, width)
    small = jnp.concatenate(
        [jnp.pad(qv_bias, ((0, 0), (0, width - own))), up_bias.reshape(1, ff), jnp.zeros((5, width), F32)], 0
    )
    weights, bias, smalls = gather(slab, small, parts)
    h1, qt, kt, vt, ot, lse = attend(tokens, seg, norm_gains, norm_shifts, weights, bias)
    result, mg, dt, grads = mlp(
        tokens, ot, wo.reshape(parts, own, width), cotangent, pieces, up_weight, down_weight, smalls, out_biases,
        norm_gains, norm_shifts,
    )
    grads = lax.psum(grads, "dp")
    out_at = 2 * ff
    sums_at = out_at + own
    sums_two = grads[sums_at : sums_at + 4]
    down_grad, up_grad, out_weight_grad = grads[:ff], grads[ff:out_at], grads[out_at:sums_at]
    up_bias_grad = grads[sums_at + UP_BIAS]
    dq, dk, dv = attend_back(me * 0, seg, qt, kt, vt, ot, dt, lse)
    token_grad, qkv_grad, sums_one, row_sums = token_back(
        me, dq, dk, dv, weights, tokens, h1, mg, norm_gains, own
    )
    qkv_grad, sums_one, row_sums = lax.psum((qkv_grad, sums_one[:2], row_sums[:, :, 0]), "dp")
    return (
        result,
        token_grad,
        jnp.stack([sums_one[0], sums_two[0]]),
        jnp.stack([sums_one[1], sums_two[1]]),
        qkv_grad.transpose(0, 2, 1),
        row_sums,
        out_weight_grad,
        sums_two[2:4],
        up_grad,
        up_bias_grad.reshape(ff),
        down_grad,
    )


def solution(mesh):
    in_specs = (
        P("dp", None),
        P("dp", None),
        P(),
        P(),
        P(None, None, "mp"),
        P(None, "mp"),
        P("mp", None),
        P(),
        P(None, "mp"),
        P("mp"),
        P("mp", None),
        P("dp", None),
    )
    out_specs = (
        P("dp", None),
        P("dp", None),
        P(),
        P(),
        P(None, None, "mp"),
        P(None, "mp"),
        P("mp", None),
        P(),
        P(None, "mp"),
        P("mp"),
        P("mp", None),
    )
    return jax.shard_map(
        partial(body, mesh.shape["dp"]), mesh=mesh, in_specs=in_specs, out_specs=out_specs, check_vma=False
    )
```

```python
from functools import partial

import jax
import jax.numpy as jnp
from jax import lax
from jax.experimental import pallas as pl
from jax.experimental.pallas import tpu as pltpu
from jax.sharding import PartitionSpec as P

F32 = jnp.float32
BF = jnp.bfloat16
HEAD_DIM = 64
NORM_EPSILON = 1e-06
BIG = 1e30
LOG2E = 1.4426950408889634
SAFE_SCORE = 60.0
REACH = 512
TILE = 256
LONG_TILE = 512
EXTRA = 16
FWD_UNROLL = 4
UNIT = 256
EARLY = 5
BWD_UNROLL = 3

NN = (((1,), (0,)), ((), ()))
NT = (((1,), (1,)), ((), ()))
TN = (((0,), (0,)), ((), ()))
WHOLE = pl.BlockSpec(memory_space=pltpu.VMEM)
ONCE = pl.BlockSpec(memory_space=pltpu.VMEM, pipeline_mode=pl.Buffered(1))
ANY = pl.BlockSpec(memory_space=pl.ANY)


def dot(left, right, dims):
    return lax.dot_general(left, right, dims, preferred_element_type=F32)


def params(mib=56):
    return pltpu.CompilerParams(vmem_limit_bytes=mib * 2**20)


def standardize(values):
    centered = values - jnp.mean(values, -1, keepdims=True)
    inv_std = lax.rsqrt(jnp.mean(centered * centered, -1, keepdims=True) + NORM_EPSILON)
    return centered * inv_std, inv_std


def norm_back(grad_in, normed, inv_std, gain):
    scaled = grad_in * gain
    return inv_std * (
        scaled
        - jnp.mean(scaled, -1, keepdims=True)
        - normed * jnp.mean(scaled * normed, -1, keepdims=True)
    )


def shape_of(shape, dtype):
    return jax.ShapeDtypeStruct(shape, dtype)


def flip(index, bit):
    return index + bit - 2 * bit * lax.rem(lax.div(index, bit), 2)


def remote(src, dst, send_sem, recv_sem, **where):
    return pltpu.make_async_remote_copy(
        src_ref=src, dst_ref=dst, send_sem=send_sem, recv_sem=recv_sem, device_id=where,
        device_id_type=pl.DeviceIdType.MESH,
    )


CORE, SIDE, ACROSS, DIAG_A, DIAG_B, CORE_SIDE, CORE_ACROSS, CORE_A, CORE_B = range(9)


class Spread:
    def __init__(self, piece, send_sems, recv_sems, mine=None):
        self.piece, self.send_sems, self.recv_sems, self.mine = piece, send_sems, recv_sems, mine
        self.device = lax.axis_index("dp")
        self.place = lax.rem(self.device, 8)

    def copy(self, chunk, kind, origin, bit, half=None):
        ref = self.piece(chunk, origin, half)
        own = self.mine is not None and kind in (CORE, SIDE, ACROSS)
        return remote(
            self.mine(chunk) if own else ref, ref, self.send_sems.at[chunk, kind], self.recv_sems.at[chunk, kind], dp=flip(self.device, bit)
        )

    def origin(self, bits):
        place = self.place
        for bit in bits:
            place = flip(place, bit)
        return place

    def outgoing(self, chunk, kind):
        bits, bit, half = {
            CORE: ((), 1, None),
            SIDE: ((), 2, None),
            ACROSS: ((), 4, None),
            DIAG_A: ((2,), 4, 0),
            DIAG_B: ((4,), 2, 1),
            CORE_SIDE: ((2,), 1, None),
            CORE_ACROSS: ((4,), 1, None),
            CORE_A: ((2, 4), 1, 0),
            CORE_B: ((2, 4), 1, 1),
        }[kind]
        return self.copy(chunk, kind, self.origin(bits), bit, half)

    def incoming(self, chunk, kind):
        bits, bit, half = {
            CORE: ((1,), 1, None),
            SIDE: ((2,), 2, None),
            ACROSS: ((4,), 4, None),
            DIAG_A: ((2, 4), 4, 0),
            DIAG_B: ((2, 4), 2, 1),
            CORE_SIDE: ((1, 2), 1, None),
            CORE_ACROSS: ((1, 4), 1, None),
            CORE_A: ((1, 2, 4), 1, 0),
            CORE_B: ((1, 2, 4), 1, 1),
        }[kind]
        return self.copy(chunk, kind, self.origin(bits), bit, half)

    def start(self, chunk, *kinds):
        for kind in kinds:
            self.outgoing(chunk, kind).start()

    def arrived(self, chunk, *kinds):
        for kind in kinds:
            self.incoming(chunk, kind).wait_recv()

    def send(self, chunk):
        self.start(chunk, SIDE, ACROSS, CORE)

    def forward(self, chunk):
        self.arrived(chunk, SIDE)
        self.start(chunk, DIAG_A, CORE_SIDE)
        self.arrived(chunk, ACROSS)
        self.start(chunk, DIAG_B, CORE_ACROSS)

    def corner(self, chunk):
        self.arrived(chunk, DIAG_A)
        self.start(chunk, CORE_A)
        self.arrived(chunk, DIAG_B)
        self.start(chunk, CORE_B)

    def complete(self, chunk):
        self.arrived(chunk, CORE, CORE_SIDE, CORE_ACROSS, CORE_A, CORE_B)

    def sent(self, chunk):
        for kind in range(9):
            self.outgoing(chunk, kind).wait_send()


def greet(*peers):
    barrier = pltpu.get_barrier_semaphore()
    for peer in peers:
        pl.semaphore_signal(barrier, inc=1, device_id=peer, device_id_type=pl.DeviceIdType.MESH)
    pl.semaphore_wait(barrier, len(peers))


def foreign_order(me):
    half = lax.div(me, 2)
    return flip(me, 1), 2 - half, 3 - 3 * half


def gather_kernel(
    x_ref, gain_ref, shift_ref, qkv_ref, out_ref, qv_bias_ref, up_bias_ref,
    h1_ref, w_ref, wo_ref, bias_ref, smalls_ref,
    land, small_land, slab, x_in, h1_out, x_sem, h1_sem,
    z_send, z_recv, own_send, small_send, small_recv, send_sems, recv_sems,
):
    parts, rows, width = land.shape
    own = out_ref.shape[0]
    share = rows // 8
    split = (0, share // 16 * 8, share)
    tokens = x_in.shape[0]
    me = lax.axis_index("mp")
    device = lax.axis_index("dp")
    greet(
        *[{"mp": lax.rem(me + s, parts)} for s in range(1, parts)],
        *[{"dp": flip(device, bit)} for bit in (1, 2, 4)],
    )
    x_copy = pltpu.make_async_copy(x_ref, x_in, x_sem)
    x_copy.start()
    order = foreign_order(me)

    def rows_of(c, origin, half=None):
        start, stop = split[c % 2], split[c % 2 + 1]
        middle = start + (stop - start + 8) // 16 * 8
        if half is not None:
            start, stop = (start, middle) if half == 0 else (middle, stop)
        return pl.ds(pl.multiple_of(origin * share + start, 8), stop - start)

    def piece(c, origin, half):
        return land.at[order[c // 2], rows_of(c, origin, half), :]

    spread = Spread(piece, send_sems, recv_sems)

    def own_copy(h, up):
        rows = rows_of(h, spread.place)
        return remote(
            slab.at[rows, :], land.at[me, rows, :], own_send.at[h, up], z_recv.at[me * 2 + h], mp=me + 2 * up - 1
        )

    def on_copy(c, step):
        ref = piece(c, spread.place, None)
        chunk = order[c // 2] * 2 + c % 2
        return remote(ref, ref, z_send.at[chunk], z_recv.at[chunk], mp=me + step)

    for j in range(3):
        slab[j * own : (j + 1) * own, :] = qkv_ref[j].T
    slab[3 * own :, :] = out_ref[...]
    small_land[me] = jnp.zeros(small_land.shape[1:], F32)
    small_land[me, 0:2, :own] = qv_bias_ref[...]
    small_land[me, 2:3, :] = up_bias_ref[...]
    for h in range(2):
        @pl.when(me < parts - 1)
        def _():
            own_copy(h, 1).start()

        @pl.when(me > 0)
        def _():
            own_copy(h, 0).start()

    def small_copy(s):
        ref = small_land.at[me]
        return remote(ref, ref, small_send.at[s - 1], small_recv.at[me], mp=lax.rem(me + s, parts))

    for s in range(1, parts):
        small_copy(s).start()

    def pass_on(c, act):
        source = order[c // 2]

        @pl.when((source < me) & (me < parts - 1))
        def _():
            act(on_copy(c, 1))

        @pl.when((source > me) & (me > 0))
        def _():
            act(on_copy(c, -1))

    def landed(c):
        on_copy(c, 0).wait_recv()
        pass_on(c, lambda copy: copy.start())
        spread.send(c)

    def use(source, ref):
        place = lax.rem(source - me + parts, parts)
        for j in range(3):
            at = pl.multiple_of((j * parts + place) * own, own)
            w_ref[pl.ds(at, own), :] = ref[j * own : (j + 1) * own, :].astype(BF)
        wo_ref[pl.ds(pl.multiple_of(place * own, own), own), :] = ref[3 * own :, :].astype(BF)

    x_copy.wait()

    def norm_tiles(low, high):
        def tile(i, carry):
            at = pl.ds(pl.multiple_of(i * TILE, TILE), TILE)
            normed, _ = standardize(x_in[at, :].astype(F32))
            h1_out[at, :] = (normed * gain_ref[0:1, :] + shift_ref[0:1, :]).astype(BF)
            return carry

        lax.fori_loop(low, high, tile, 0)

    count = tokens // TILE
    norm_tiles(0, count // 2)
    landed(0)
    landed(1)
    norm_tiles(count // 2, count)
    h1_copy = pltpu.make_async_copy(h1_out, h1_ref, h1_sem)
    h1_copy.start()
    last = 5
    for c in range(last + 1):
        spread.forward(c)
        if c + 2 <= last:
            landed(c + 2)
        if c > 0:
            spread.corner(c - 1)
        if c == 0:
            use(me, slab)
    spread.corner(last)
    for s in range(1, parts):
        ref = small_land.at[lax.rem(me + s, parts)]
        remote(ref, ref, small_send.at[0], small_recv.at[lax.rem(me + s, parts)], mp=me).wait_recv()
    bias_ref[...] = jnp.zeros_like(bias_ref)
    for source in range(parts):
        cols = small_land[source].T
        place = lax.rem(source - me + parts, parts)
        for j in range(2):
            at = pl.multiple_of((2 * j * parts + place) * own, own)
            bias_ref[pl.ds(at, own), :] = cols[:own, j : j + 1]
    smalls_ref[...] = small_land[...]
    for j in range(3):
        for h in range(2):
            spread.complete(2 * j + h)
        use(order[j], land.at[order[j]])
    h1_copy.wait()
    for c in range(last + 1):
        spread.sent(c)
        pass_on(c, lambda copy: copy.wait_send())
    for s in range(1, parts):
        small_copy(s).wait_send()
    for h in range(2):
        @pl.when(me < parts - 1)
        def _():
            own_copy(h, 1).wait_send()

        @pl.when(me > 0)
        def _():
            own_copy(h, 0).wait_send()


def gather(x, gains, shifts, qkv_weight, out_weight, qv_bias, up_bias):
    tokens, width = x.shape
    own = out_weight.shape[0]
    parts = width // own
    rows = 4 * own
    dma = pltpu.SemaphoreType.DMA
    return pl.pallas_call(
        gather_kernel,
        in_specs=[ANY] + [WHOLE] * 6,
        out_specs=[ANY] + [WHOLE] * 4,
        out_shape=[
            shape_of((tokens, width), BF),
            shape_of((3 * own * parts, width), BF),
            shape_of((own * parts, width), BF),
            shape_of((3 * own * parts, 1), F32),
            shape_of((parts, 8, width), F32),
        ],
        scratch_shapes=[
            pltpu.VMEM((parts, rows, width), F32),
            pltpu.VMEM((parts, 8, width), F32),
            pltpu.VMEM((rows, width), F32),
            pltpu.VMEM((tokens, width), BF),
            pltpu.VMEM((tokens, width), BF),
            dma,
            dma,
            dma((2 * parts,)),
            dma((2 * parts,)),
            dma((2, 2)),
            dma((parts - 1,)),
            dma((parts,)),
            dma((6, 9)),
            dma((6, 9)),
        ],
        compiler_params=pltpu.CompilerParams(vmem_limit_bytes=56 * 2**20, collective_id=0, has_side_effects=True),
        name="gather",
    )(x, gains, shifts, qkv_weight, out_weight, qv_bias, up_bias)


def attend_kernel(
    h1_ref, seg_ref, w_ref, b_ref, up_any, down_any,
    qt_ref, kt_ref, vt_ref, ot_ref, lse_ref, bound_ref, land_out, z_out,
    qx, kx, vx, kn, land, z_land, pieces,
    piece_sems, keep_sems, out_sems, z_send, z_recv, own_send, send_sems, recv_sems,
):
    r = pl.program_id(0)
    length, width = h1_ref.shape
    heads = width // HEAD_DIM
    chunks = z_land.shape[0]
    units = pieces.shape[0]
    parts = chunks // units + 1
    share = z_land.shape[2]
    strip = UNIT // 8
    me = lax.axis_index("mp")
    order = foreign_order(me)

    def slot_of(c):
        source = order[c // units]
        return (source - jnp.where(source > me, 1, 0)) * units + c % units

    def mine(c):
        return z_land.at[slot_of(c)]

    def piece(c, origin, half):
        rows = pl.ds(pl.multiple_of(origin * share, 8), share)
        if half is None:
            return land.at[c, :, rows, :]
        return land.at[c, half, rows, :]

    spread = Spread(piece, send_sems, recv_sems, mine)

    def own_copy(u, up):
        slot = (me + up - 1) * units + u
        return remote(pieces.at[u], z_land.at[slot], own_send.at[u, up], z_recv.at[slot], mp=me + 2 * up - 1)

    def own_copies(act):
        for u in range(units):
            @pl.when(me < parts - 1)
            def _():
                act(own_copy(u, 1))

            @pl.when(me > 0)
            def _():
                act(own_copy(u, 0))

    def pass_on(c, act):
        source = order[c // units]
        slot = slot_of(c)

        def copy(step):
            ref = z_land.at[slot]
            return remote(ref, ref, z_send.at[slot], z_recv.at[slot], mp=me + step)

        @pl.when((source < me) & (me < parts - 1))
        def _():
            act(copy(1))

        @pl.when((source > me) & (me > 0))
        def _():
            act(copy(-1))

    def landed(c):
        slot = slot_of(c)
        remote(z_land.at[slot], z_land.at[slot], z_send.at[slot], z_recv.at[slot], mp=me).wait_recv()
        pass_on(c, lambda copy: copy.start())
        if c < EARLY:
            keep(c).start()

    def keep(c):
        return pltpu.make_async_copy(mine(c), piece(c, spread.place, None), keep_sems.at[c])

    def store(c):
        return pltpu.make_async_copy(land.at[c], land_out.at[c], out_sems.at[c])

    z_store = pltpu.make_async_copy(z_land, z_out, out_sems.at[EARLY])

    def serve(n):
        if n < 2:
            landed(n)
        if n == 1:
            landed(2)
        if n < EARLY:
            spread.send(n)
        if 0 <= n - 1 < EARLY:
            spread.forward(n - 1)
        if 1 <= n and n + 2 < chunks:
            landed(n + 2)
        if n + 2 == chunks:
            z_store.start()
        if 0 <= n - 2 < EARLY:
            spread.corner(n - 2)
        if 0 <= n - 3 < EARLY:
            spread.complete(n - 3)
            keep(n - 3).wait()
            store(n - 3).start()

    def serve_at(row, n):
        @pl.when(r == row)
        def _():
            serve(n)

    @pl.when(r == 0)
    def _():
        greet(
            *[{"mp": lax.rem(me + s, parts)} for s in range(1, parts)],
            *[{"dp": flip(spread.device, bit)} for bit in (1, 2, 4)],
        )
        copies = []
        for u in range(units):
            rows = pl.ds(pl.multiple_of(spread.place * share, 8), share)
            copies.append((up_any.at[rows, pl.ds(u * UNIT, UNIT)], pieces.at[u, 0]))
            for c in range(width // UNIT):
                rows = pl.ds(pl.multiple_of(u * UNIT + spread.place * strip, 8), strip)
                copies.append(
                    (down_any.at[rows, pl.ds(c * UNIT, UNIT)], pieces.at[u, 1, pl.ds(c * strip, strip), :])
                )
        copies = [pltpu.make_async_copy(a, b, piece_sems.at[i]) for i, (a, b) in enumerate(copies)]
        for copy in copies:
            copy.start()
        for copy in copies:
            copy.wait()
        own_copies(lambda copy: copy.start())
        bound_ref[...] = jnp.zeros_like(bound_ref)

    for j, out in enumerate((qt_ref, kt_ref, vt_ref)):
        value = dot(w_ref[j * width : (j + 1) * width, :], h1_ref[...], NT)
        if j != 1:
            value = value + b_ref[j * width : (j + 1) * width, :]
        value = value.astype(BF)
        if j == 0:
            value = value * jnp.asarray(HEAD_DIM**-0.5, BF)
        out[...] = value
        if j == 1:
            serve_at(1, 4)
    serve_at(0, 0)
    row = lax.broadcasted_iota(jnp.int32, (EXTRA, length), 0)
    same = row == seg_ref[0]
    for u in range(FWD_UNROLL):
        qx[u, HEAD_DIM:, :] = jnp.where(same | (row >= 8), 0.0, -BIG).astype(BF)
        kx[u, HEAD_DIM:, :] = jnp.where(same, 1.0, 0.0).astype(BF)
        vx[u, HEAD_DIM:, :] = jnp.ones((EXTRA, length), BF)

    def norm_bound(ref, u):
        value = ref[u, :HEAD_DIM, :].astype(F32)
        return jnp.max(jnp.sum(value * value, 0, keepdims=True), 1, keepdims=True)

    def head(h, u):
        rows = pl.ds(pl.multiple_of(h * HEAD_DIM, HEAD_DIM), HEAD_DIM)
        qx[u, :HEAD_DIM, :] = qt_ref[rows, :]
        kx[u, :HEAD_DIM, :] = kt_ref[rows, :]
        vx[u, :HEAD_DIM, :] = vt_ref[rows, :]
        kn[u] = kx[u].T
        bound_ref[...] = jnp.maximum(bound_ref[...], norm_bound(qx, u) * norm_bound(kx, u))
        for t in range(length // TILE):
            low, high = max(0, t * TILE - REACH), min(length, (t + 1) * TILE + REACH)
            cols = slice(t * TILE, (t + 1) * TILE)
            probs = [
                jnp.exp2(dot(kn[u, k : k + TILE, :], qx[u, :, cols], NN) * LOG2E).astype(BF)
                for k in range(low, high, TILE)
            ]
            out = dot(vx[u, :, low:high], jnp.concatenate(probs, 0), NN)
            total = out[HEAD_DIM : HEAD_DIM + 1, :]
            ot_ref[rows, cols] = (out[:HEAD_DIM, :] * (1.0 / total)).astype(BF)
            lse_ref[pl.ds(h, 1), cols] = jnp.log(total)

    def group(i, carry):
        for u in range(FWD_UNROLL):
            head(i * FWD_UNROLL + u, u)
        for at, (row, n) in enumerate(((0, 1), (0, 2), (0, 3), (1, 5), (1, 6), (1, 7))):
            @pl.when((r == row) & (i == at % 3))
            def _():
                serve(n)
        return carry

    lax.fori_loop(0, heads // FWD_UNROLL, group, 0)

    @pl.when(r == pl.num_programs(0) - 1)
    def _():
        for c in range(EARLY):
            spread.sent(c)
            store(c).wait()
        z_store.wait()
        for c in range(chunks):
            pass_on(c, lambda copy: copy.wait_send())
        own_copies(lambda copy: copy.wait_send())


def attend(h1, seg, weights, bias, up, down):
    tokens, width = h1.shape
    rows, _, length = seg.shape
    ff = up.shape[1]
    parts = width // (weights.shape[0] // 12)
    units = ff // UNIT
    chunks = (parts - 1) * units
    row = pl.BlockSpec((length, width), lambda r: (r, 0))
    col = pl.BlockSpec((width, length), lambda r: (0, r))
    dma = pltpu.SemaphoreType.DMA
    return pl.pallas_call(
        attend_kernel,
        grid=(rows,),
        in_specs=[row, pl.BlockSpec((1, 1, length), lambda r: (r, 0, 0)), ONCE, ONCE, ANY, ANY],
        out_specs=[col, col, col, col, pl.BlockSpec((16, length), lambda r: (0, r)), ONCE, ANY, ANY],
        out_shape=[shape_of((width, tokens), BF)] * 4
        + [
            shape_of((16, tokens), F32),
            shape_of((8, 128), F32),
            shape_of((EARLY, 2, width, UNIT), F32),
            shape_of((chunks, 2, width // 8, UNIT), F32),
        ],
        scratch_shapes=[pltpu.VMEM((FWD_UNROLL, HEAD_DIM + EXTRA, length), BF)] * 3
        + [
            pltpu.VMEM((FWD_UNROLL, length, HEAD_DIM + EXTRA), BF),
            pltpu.VMEM((EARLY, 2, width, UNIT), F32),
            pltpu.VMEM((chunks, 2, width // 8, UNIT), F32),
            pltpu.VMEM((units, 2, width // 8, UNIT), F32),
            dma((units * (1 + width // UNIT),)),
            dma((EARLY,)),
            dma((EARLY + 1,)),
            dma((chunks,)),
            dma((chunks,)),
            dma((units, 2)),
            dma((EARLY, 9)),
            dma((EARLY, 9)),
        ],
        compiler_params=pltpu.CompilerParams(vmem_limit_bytes=60 * 2**20, collective_id=4, has_side_effects=True),
        name="attend",
    )(h1, seg, weights, bias, up, down)


def repair_kernel(
    bound_ref, seg_ref, qt_any, kt_any, vt_any, ot_in, lse_in, ot_out, lse_out, qx, kx, vx, lse_row, sems,
):
    rows_here, _, length = seg_ref.shape
    heads = qt_any.shape[0] // HEAD_DIM
    safe = jnp.max(bound_ref[...]) < SAFE_SCORE**2

    @pl.when(jnp.logical_not(safe))
    def _():
        row = lax.broadcasted_iota(jnp.int32, (EXTRA, length), 0)
        vx[HEAD_DIM:, :] = jnp.ones((EXTRA, length), BF)

        def move(copies):
            copies = [pltpu.make_async_copy(a, b, sems.at[i]) for i, (a, b) in enumerate(copies)]
            for copy in copies:
                copy.start()
            for copy in copies:
                copy.wait()

        def head(i, carry):
            r, h = lax.div(i, heads), lax.rem(i, heads)
            rows = pl.ds(pl.multiple_of(h * HEAD_DIM, HEAD_DIM), HEAD_DIM)
            tokens = pl.ds(pl.multiple_of(r * length, length), length)
            same = row == seg_ref[r]
            qx[HEAD_DIM:, :] = jnp.where(same | (row >= 8), 0.0, -BIG).astype(BF)
            kx[HEAD_DIM:, :] = jnp.where(same, 1.0, 0.0).astype(BF)
            move([
                (source.at[rows, tokens], target.at[pl.ds(0, HEAD_DIM), :])
                for source, target in ((qt_any, qx), (kt_any, kx), (vt_any, vx))
            ])

            @pl.when(h == 0)
            def _():
                lse_row[...] = jnp.zeros_like(lse_row)

            for t in range(length // TILE):
                cols = slice(t * TILE, (t + 1) * TILE)
                scores = dot(kx[...], qx[:, cols], TN)
                highest = jnp.max(scores, 0, keepdims=True)
                probs = jnp.exp2((scores - highest) * LOG2E).astype(BF)
                out = dot(vx[...], probs, NN)
                total = out[HEAD_DIM : HEAD_DIM + 1, :]
                qx[:HEAD_DIM, cols] = (out[:HEAD_DIM, :] * (1.0 / total)).astype(BF)
                lse_row[pl.ds(h, 1), cols] = jnp.log(total) + highest
            move([(qx.at[pl.ds(0, HEAD_DIM), :], ot_out.at[rows, tokens])])

            @pl.when(h == heads - 1)
            def _():
                move([(lse_row, lse_out.at[:, tokens])])

            return carry

        lax.fori_loop(0, rows_here * heads, head, 0)


def repair(bound, seg, qt, kt, vt, ot, lse):
    length = seg.shape[2]
    return pl.pallas_call(
        repair_kernel,
        in_specs=[WHOLE, WHOLE, ANY, ANY, ANY, ANY, ANY],
        out_specs=[ANY, ANY],
        out_shape=[shape_of(ot.shape, BF), shape_of(lse.shape, F32)],
        input_output_aliases={5: 0, 6: 1},
        scratch_shapes=[pltpu.VMEM((HEAD_DIM + EXTRA, length), BF)] * 3
        + [pltpu.VMEM((16, length), F32), pltpu.SemaphoreType.DMA((3,))],
        compiler_params=params(),
        name="repair",
    )(bound, seg, qt, kt, vt, ot, lse)


def split3(value):
    first = value.astype(BF)
    rest = value - first.astype(F32)
    second = rest.astype(BF)
    return first, second, (rest - second.astype(F32)).astype(BF)


class Total:
    def __init__(self, out, sends, recvs, near=None, side_land=None, across_land=None):
        self.out, self.near = out, near
        self.side_land, self.across_land, self.sends, self.recvs = side_land, across_land, sends, recvs
        self.device = lax.axis_index("dp")
        place = lax.rem(self.device, 8)
        self.half = out.shape[0] // 2
        self.part, self.piece = self.half // 4, self.half // 8
        bits = [lax.rem(lax.div(place, bit), 2) for bit in (1, 2, 4)]
        self.base = bits[0] * self.half
        self.away = (1 - bits[0]) * self.half
        self.one = self.base + bits[1] * self.part
        self.one_away = self.base + (1 - bits[1]) * self.part
        self.two = self.base + 2 * self.part + bits[2] * self.part
        self.two_away = self.base + 2 * self.part + (1 - bits[2]) * self.part
        self.one_piece = self.one + bits[2] * self.piece
        self.one_piece_away = self.one + (1 - bits[2]) * self.piece
        self.two_piece = self.two + bits[1] * self.piece
        self.two_piece_away = self.two + (1 - bits[1]) * self.piece

    def rows(self, start, count):
        return self.out.at[pl.ds(pl.multiple_of(start, 8), count), :]

    def copy(self, sem, bit, src, dst):
        return remote(src, dst, self.sends.at[sem], self.recvs.at[sem], dp=flip(self.device, bit))

    def over(self, sem, bit, start, count):
        ref = self.rows(start, count)
        return self.copy(sem, bit, ref, ref)

    def copies(self, stage):
        part, piece = self.part, self.piece
        first, second = pl.ds(0, part), pl.ds(part, piece)
        if stage == 0:
            return [self.copy(0, 1, self.rows(self.away, self.half), self.near)]
        if stage == 1:
            return [
                self.copy(1, 2, self.rows(self.one_away, part), self.side_land.at[first, :]),
                self.copy(2, 4, self.rows(self.two_away, part), self.across_land.at[first, :]),
            ]
        if stage == 2:
            return [
                self.copy(3, 4, self.rows(self.one_piece_away, piece), self.across_land.at[second, :]),
                self.copy(4, 2, self.rows(self.two_piece_away, piece), self.side_land.at[second, :]),
            ]
        if stage == 3:
            return [self.over(5, 4, self.one_piece, piece), self.over(6, 2, self.two_piece, piece)]
        if stage == 4:
            return [self.over(7, 2, self.one, part), self.over(8, 4, self.two, part)]
        return [self.over(9, 1, self.base, self.half)]

    def arrivals(self, stage):
        part, piece = self.part, self.piece
        if stage == 3:
            return [self.over(5, 4, self.one_piece_away, piece), self.over(6, 2, self.two_piece_away, piece)]
        if stage == 4:
            return [self.over(7, 2, self.one_away, part), self.over(8, 4, self.two_away, part)]
        if stage == 5:
            return [self.over(9, 1, self.away, self.half)]
        return self.copies(stage)

    def add(self, start, ref, at, count):
        step = 48 if count % 48 == 0 else 56

        def some(i, carry):
            rows = pl.ds(pl.multiple_of(start + i * step, 8), step)
            self.out[rows, :] += ref[pl.ds(pl.multiple_of(at + i * step, 8), step), :]
            return carry

        lax.fori_loop(0, count // step, some, 0)

    def finish(self, stage):
        for copy in self.copies(stage):
            copy.wait_send()
        for copy in self.arrivals(stage):
            copy.wait_recv()
        if stage == 0:
            self.add(self.base, self.near, 0, self.half)
        elif stage == 1:
            self.add(self.one, self.side_land, 0, self.part)
            self.add(self.two, self.across_land, 0, self.part)
        elif stage == 2:
            self.add(self.one_piece, self.across_land, self.part, self.piece)
            self.add(self.two_piece, self.side_land, self.part, self.piece)

    def start(self, stage):
        for copy in self.copies(stage):
            copy.start()

    @staticmethod
    def scratch(rows, width):
        dma = pltpu.SemaphoreType.DMA
        return [
            dma((10,)),
            dma((10,)),
            pltpu.VMEM((rows // 2, width), F32),
            pltpu.VMEM((rows // 8 + rows // 16, width), F32),
            pltpu.VMEM((rows // 8 + rows // 16, width), F32),
        ]


def attend_back_kernel(
    seg_ref, qt_ref, kt_ref, vt_ref, ot_ref, dt_ref, lse_ref, h1_any, main_any, tail_any,
    dq_ref, dk_ref, dv_ref, main_out, rest_out,
    qx, kx, vx, dx, qn, dn, kn, acc, h1_ref, main_ref, rest_ref, whole_ref, in_sems, out_sems, main_send, main_recv, *comm,
):
    step = pl.program_id(0)
    own, length = qt_ref.shape
    width = h1_ref.shape[1]
    heads = own // HEAD_DIM
    tail_at = rest_ref.shape[0] - tail_any.shape[0]
    main = Total(main_ref, main_send, main_recv)
    rest = Total(rest_ref, *comm)
    whole = Total(whole_ref, *comm[:2])
    loads = [
        pltpu.make_async_copy(main_any.at[pl.ds(pl.multiple_of(at, 8), main.piece), :], main.rows(at, main.piece), sem)
        for at, sem in ((main.one_piece, in_sems.at[0]), (main.two_piece, in_sems.at[1]))
    ]
    loads.append(pltpu.make_async_copy(tail_any, rest_ref.at[pl.ds(tail_at, tail_any.shape[0]), :], in_sems.at[2]))
    loads.append(pltpu.make_async_copy(h1_any, h1_ref, in_sems.at[3]))
    stores = [
        pltpu.make_async_copy(main_ref, main_out, out_sems.at[0]),
        pltpu.make_async_copy(whole_ref, rest_out, out_sems.at[1]),
    ]

    @pl.when(step == 0)
    def _():
        for copy in loads:
            copy.start()
        greet(*[{"dp": flip(main.device, bit)} for bit in (1, 2, 4)])
        for copy in loads[:2]:
            copy.wait()
        main.start(3)

    @pl.when(step == 1)
    def _():
        main.finish(3)
        main.start(4)

    @pl.when(step == 3)
    def _():
        rest.finish(0)
        rest.start(1)
        main.finish(4)
        main.start(5)

    @pl.when(step == 4)
    def _():
        rest.finish(1)
        rest.start(2)

    @pl.when(step == 5)
    def _():
        rest.finish(2)
        for at in (rest.one_piece, rest.two_piece):
            rows = pl.ds(pl.multiple_of(at, 8), rest.piece)
            whole_ref[rows, :] = rest_ref[rows, :]
        whole.start(3)
        main.finish(5)
        stores[0].start()

    @pl.when(step == 6)
    def _():
        whole.finish(3)
        whole.start(4)

    @pl.when(step == 7)
    def _():
        whole.finish(4)
        whole.start(5)

    row = lax.broadcasted_iota(jnp.int32, (EXTRA, length), 0)
    same = row == seg_ref[0]
    key_extra = jnp.where(same | ((row >= 8) & (row < 11)), 1.0, 0.0).astype(BF)
    value_extra = jnp.where(row < 3, 1.0, 0.0).astype(BF)
    query_extra = jnp.where(same | (row >= 8), 0.0, -BIG)

    def three_rows(value, at):
        first, second, third = split3(value)
        out = jnp.where(row == at, first.astype(F32), 0.0)
        out = jnp.where(row == at + 1, second.astype(F32), out)
        return jnp.where(row == at + 2, third.astype(F32), out)

    head_at = jnp.where(step < 2, 0, lax.rem(step - 2, 3) + 1) * heads

    def head(u):
        rows = slice(u * HEAD_DIM, (u + 1) * HEAD_DIM)
        qx[u, :HEAD_DIM, :] = qt_ref[rows, :]
        kx[u, :HEAD_DIM, :] = kt_ref[rows, :]
        vx[u, :HEAD_DIM, :] = vt_ref[rows, :]
        dx[u, :HEAD_DIM, :] = dt_ref[rows, :]
        inner = jnp.sum(dt_ref[rows, :].astype(F32) * ot_ref[rows, :].astype(F32), 0, keepdims=True)
        log_sum = lse_ref[pl.ds(head_at + u, 1), :]
        qx[u, HEAD_DIM:, :] = (query_extra + three_rows(-log_sum, 8)).astype(BF)
        kx[u, HEAD_DIM:, :] = key_extra
        vx[u, HEAD_DIM:, :] = value_extra
        dx[u, HEAD_DIM:, :] = three_rows(-inner, 0).astype(BF)
        qn[u] = qx[u].T
        dn[u] = dx[u].T
        kn[u] = kx[u].T
        for t in range(length // TILE):
            low, high = max(0, t * TILE - REACH), min(length, (t + 1) * TILE + REACH)
            keys = slice(t * TILE, (t + 1) * TILE)
            probs, score_grads = [], []
            for q in range(low, high, TILE):
                prob = jnp.exp2(dot(qn[u, q : q + TILE, :], kx[u, :, keys], NN) * LOG2E)
                prob_grad = dot(dn[u, q : q + TILE, :], vx[u, :, keys], NN)
                probs.append(prob.astype(BF))
                score_grads.append((prob * prob_grad).astype(BF))
            probs = jnp.concatenate(probs, 0)
            score_grads = jnp.concatenate(score_grads, 0)
            dv_ref[rows, keys] = dot(dx[u, :HEAD_DIM, low:high], probs, NN).astype(BF)
            dk_ref[rows, keys] = dot(qx[u, :HEAD_DIM, low:high], score_grads, NN).astype(BF)
            part = dot(score_grads, kx[u, :HEAD_DIM, keys], NT)
            if t == 0:
                acc[u, low:high, :] = part
                if high < length:
                    acc[u, high:, :] = jnp.zeros((length - high, HEAD_DIM), F32)
            else:
                acc[u, low:high, :] += part
        dq_ref[rows, :] = (acc[u] * HEAD_DIM**-0.5).T.astype(BF)

    for u in range(heads):
        head(u)

    def own_grads(tokens, add):
        h1 = h1_ref[tokens, :]
        ones = jnp.ones((8, length), BF)
        for j, ref in enumerate((dq_ref, dk_ref, dv_ref)):
            rows = slice(j * own, (j + 1) * own)
            part = dot(ref[...], h1, NN)
            rest_ref[rows, :] = rest_ref[rows, :] + part if add else part
            if j != 1:
                rows = slice(3 * own + j * 4, 3 * own + j * 4 + 8)
                part = dot(ones, ref[...], NT)
                rest_ref[rows, :own] = rest_ref[rows, :own] + part if add else part

    @pl.when(step == 0)
    def _():
        rest_ref[3 * own : tail_at, :] = jnp.zeros((tail_at - 3 * own, width), F32)
        loads[3].wait()
        own_grads(slice(0, length), False)

    @pl.when(step == 1)
    def _():
        own_grads(slice(length, 2 * length), True)
        loads[2].wait()
        rest.start(0)

    @pl.when(step == 7)
    def _():
        whole.finish(5)
        stores[1].start()
        for copy in stores:
            copy.wait()


def attend_back(seg, qt, kt, vt, ot, dt, lse, h1, main, tail):
    width, tokens = qt.shape
    _, _, length = seg.shape
    own = width // 4
    heads = own // HEAD_DIM
    wide = HEAD_DIM + EXTRA
    rest_rows = 3 * own + 64 + tail.shape[0]
    row_of = lambda s: jnp.where((s == 1) | (s >= 5), 1, 0)
    part_of = lambda s: jnp.where(s < 2, 0, lax.rem(s - 2, 3) + 1)
    block = pl.BlockSpec((own, length), lambda s: (part_of(s), row_of(s)))
    dma = pltpu.SemaphoreType.DMA
    return pl.pallas_call(
        attend_back_kernel,
        grid=(8,),
        in_specs=[pl.BlockSpec((1, 1, length), lambda s: (row_of(s), 0, 0))]
        + [block] * 5
        + [pl.BlockSpec((16, length), lambda s: (0, row_of(s))), ANY, ANY, ANY],
        out_specs=[block] * 3 + [ANY, ANY],
        out_shape=[shape_of((width, tokens), BF)] * 3
        + [shape_of(main.shape, F32), shape_of((rest_rows, width), F32)],
        scratch_shapes=[pltpu.VMEM((heads, wide, length), BF)] * 4
        + [pltpu.VMEM((heads, length, wide), BF)] * 3
        + [
            pltpu.VMEM((heads, length, HEAD_DIM), F32),
            pltpu.VMEM((tokens, width), BF),
            pltpu.VMEM(main.shape, F32),
            pltpu.VMEM((rest_rows, width), F32),
            pltpu.VMEM((rest_rows, width), F32),
            dma((4,)),
            dma((2,)),
            dma((10,)),
            dma((10,)),
        ]
        + Total.scratch(rest_rows, width),
        compiler_params=pltpu.CompilerParams(vmem_limit_bytes=60 * 2**20, collective_id=2, has_side_effects=True),
        name="attend_back",
    )(seg, qt, kt, vt, ot, dt, lse, h1, main, tail)


def token_kernel(
    dq_ref, dk_ref, dv_ref, w_ref, x_ref, mg_ref, gain_ref, main_any, rest_any, result_any,
    tg_ref, sums_ref, down_ref, up_ref, out_ref, result_ref, qkvg_ref,
    main_v, rest_v, result_v, in_sems, out_sems,
):
    step = pl.program_id(0)
    last = pl.num_programs(0) - 1
    ff = down_ref.shape[0]
    own = out_ref.shape[0]
    out_at = 3 * own + 64
    loads = [
        pltpu.make_async_copy(source, target, in_sems.at[i])
        for i, (source, target) in enumerate(((rest_any, rest_v), (main_any, main_v), (result_any, result_v)))
    ]
    stores = [
        pltpu.make_async_copy(source, target, out_sems.at[i])
        for i, (source, target) in enumerate((
            (main_v.at[pl.ds(0, ff), :], down_ref),
            (main_v.at[pl.ds(ff, up_ref.shape[0]), :], up_ref),
            (rest_v.at[pl.ds(out_at, own), :], out_ref),
            (result_v, result_ref),
        ))
    ]

    @pl.when(step == 0)
    def _():
        for copy in loads:
            copy.start()
        sums_ref[...] = jnp.zeros_like(sums_ref)

    @pl.when(step == last - 1)
    def _():
        for copy in loads:
            copy.wait()
        for copy in stores:
            copy.start()
        for j in range(3):
            qkvg_ref[j] = rest_v[j * own : (j + 1) * own, :].T

    width = x_ref.shape[1]
    hg = dot(dq_ref[...], w_ref[:width, :], TN)
    hg += dot(dk_ref[...], w_ref[width : 2 * width, :], TN)
    hg += dot(dv_ref[...], w_ref[2 * width :, :], TN)
    normed, inv_std = standardize(x_ref[...].astype(F32))
    tg_ref[...] = mg_ref[...] + norm_back(hg, normed, inv_std, gain_ref[0:1, :])
    sums_ref[0:1, :] += jnp.sum(hg * normed, 0, keepdims=True)
    sums_ref[1:2, :] += jnp.sum(hg, 0, keepdims=True)

    @pl.when(step == last)
    def _():
        for copy in stores:
            copy.wait()


def token_back(dq, dk, dv, weights, x, mg, gains, main, rest, result, ff, own):
    tokens, width = x.shape
    row = pl.BlockSpec((LONG_TILE, width), lambda t: (t, 0))
    col = pl.BlockSpec((width, LONG_TILE), lambda t: (0, t))
    dma = pltpu.SemaphoreType.DMA
    return pl.pallas_call(
        token_kernel,
        grid=(tokens // LONG_TILE,),
        in_specs=[col, col, col, ONCE, row, row, ONCE, ANY, ANY, ANY],
        out_specs=[row, ONCE, ANY, ANY, ANY, ANY, ONCE],
        out_shape=[
            shape_of((tokens, width), F32),
            shape_of((8, width), F32),
            shape_of((ff, width), F32),
            shape_of((width, ff), F32),
            shape_of((own, width), F32),
            shape_of((tokens, width), BF),
            shape_of((3, width, own), F32),
        ],
        scratch_shapes=[
            pltpu.VMEM(main.shape, F32),
            pltpu.VMEM(rest.shape, F32),
            pltpu.VMEM((tokens, width), BF),
            dma((3,)),
            dma((4,)),
        ],
        compiler_params=params(),
        name="token_back",
    )(dq, dk, dv, weights, x, mg, gains, main, rest, result)


def sums_kernel(in_ref, out_ref, land, sends, recvs):
    device = lax.axis_index("dp")
    place = lax.rem(device, 8)
    others = []
    for bits in range(1, 8):
        other = device
        for bit in (1, 2, 4):
            if bits & bit:
                other = flip(other, bit)
        others.append(other)
    greet(*[{"dp": other} for other in others])
    copies = [
        remote(in_ref, land.at[place], sends.at[i], recvs.at[place], dp=other) for i, other in enumerate(others)
    ]
    for copy in copies:
        copy.start()
    land[place] = in_ref[...]
    for other in others:
        at = lax.rem(other, 8)
        remote(in_ref, land.at[at], sends.at[0], recvs.at[at], dp=other).wait_recv()
    out_ref[...] = jnp.sum(land[...], 0)
    for copy in copies:
        copy.wait_send()


def add_sums(sums):
    dma = pltpu.SemaphoreType.DMA
    return pl.pallas_call(
        sums_kernel,
        in_specs=[WHOLE],
        out_specs=WHOLE,
        out_shape=shape_of(sums.shape, F32),
        scratch_shapes=[pltpu.VMEM((8,) + sums.shape, F32), dma((7,)), dma((8,))],
        compiler_params=pltpu.CompilerParams(collective_id=3, has_side_effects=True),
        name="add_sums",
    )(sums)


GELU_C = 0.7978845608028654
GELU_A = 0.044715


def gelu_both(pre):
    square = pre * pre
    half = 0.5 + 0.5 * jnp.tanh(pre * (GELU_C + (GELU_C * GELU_A) * square))
    act = pre * half
    slope = half + act * (1.0 - half) * (2.0 * GELU_C + (6.0 * GELU_C * GELU_A) * square)
    return act, slope


GAIN_TWO, SHIFT_TWO, BIAS_ONE, BIAS_TWO, UP_BIAS = range(5)


def mlp_kernel(
    wo_ref, smalls_ref, bias_ref, gain_ref, shift_ref, x_any, ot_any, g_any, up_any, down_any, land_any, z_any,
    result_out, mg_out, dt_out, main_out, tail_out,
    land, wide_w, own_w, g_ref, h2_ref, dt_ref, mine_ref, main_ref, tail_ref, mixed_ref, res_ref, hg_ref,
    up_low, down_low, pre_s, ag_s,
    in_sems, w_sems, keep_sems, out_sems, tile_sems, send_sems, recv_sems, *comm,
):
    tokens, width = g_ref.shape
    parts = smalls_ref.shape[0]
    own = mine_ref.shape[0]
    ff = up_any.shape[1]
    units = ff // UNIT
    chunks = units * (parts - 1)
    late = land.shape[0]
    early = chunks - late
    share = z_any.shape[2]
    strip = UNIT // 8
    tiles = tokens // TILE
    me = lax.axis_index("mp")
    order = foreign_order(me)
    total = Total(main_ref, *comm)

    def source_of(c):
        j = lax.div(c, units)
        return jnp.where(j == 0, order[0], jnp.where(j == 1, order[1], order[2]))

    def piece(e, origin, half):
        rows = pl.ds(pl.multiple_of(origin * share, 8), share)
        if half is None:
            return land.at[e, :, rows, :]
        return land.at[e, half, rows, :]

    def mine(e):
        c = early + e
        source = source_of(c)
        return z_any.at[(source - jnp.where(source > me, 1, 0)) * units + lax.rem(c, units)]

    spread = Spread(piece, send_sems, recv_sems, mine)

    def keep(e):
        return pltpu.make_async_copy(mine(e), piece(e, spread.place, None), keep_sems.at[e])

    def serve(n):
        for e in range(late):
            @pl.when(n == e)
            def _():
                spread.send(e)

            @pl.when(n == e + 1)
            def _():
                spread.forward(e)

            @pl.when(n == e + 2)
            def _():
                spread.corner(e)

    def reduce(n):
        @pl.when(n == units)
        def _():
            total.start(0)

        @pl.when(n == units + 2)
        def _():
            total.finish(0)
            total.start(1)

        @pl.when(n == units + 6)
        def _():
            total.finish(1)
            total.start(2)

    def unit(bias, grads_at):
        def front(i):
            rows = slice(i * TILE, (i + 1) * TILE)
            pre_s[i % 2] = dot(h2_ref[rows, :], up_low[...], NN) + bias
            ag_s[i % 2] = dot(g_ref[rows, :], down_low[...], NT)

        def back(i):
            rows = slice(i * TILE, (i + 1) * TILE)
            act, slope = gelu_both(pre_s[i % 2])
            act = act.astype(BF)
            pre_grad = (ag_s[i % 2] * slope).astype(BF)
            res_ref[rows, :] += dot(act, down_low[...], NN)
            hg_ref[rows, :] += dot(pre_grad, up_low[...], NT)
            if grads_at is not None:
                h2 = h2_ref[rows, :]
                g = g_ref[rows, :]
                cols = pl.ds(pl.multiple_of(grads_at, UNIT), UNIT)
                main_ref[cols, :] += dot(act, g, TN)
                main_ref[ff:, cols] += dot(h2, pre_grad, TN)
                at = own + UP_BIAS
                tail_ref[at : at + 1, cols] += jnp.sum(pre_grad.astype(F32), 0, keepdims=True)

        front(0)
        for i in range(tiles):
            if i + 1 < tiles:
                front(i + 1)
            back(i)

    loads = [
        pltpu.make_async_copy(source, target, in_sems.at[i])
        for i, (source, target) in enumerate(((ot_any, dt_ref), (x_any, h2_ref), (g_any, g_ref)))
    ]

    def own_load(u):
        cols = pl.ds(pl.multiple_of(u * UNIT, UNIT), UNIT)
        return [
            pltpu.make_async_copy(up_any.at[:, cols], wide_w.at[0], w_sems.at[0]),
            pltpu.make_async_copy(down_any.at[cols, :], own_w, w_sems.at[1]),
        ]

    def chunk_load(c):
        return pltpu.make_async_copy(land_any.at[c], wide_w, w_sems.at[0])

    for copy in loads:
        copy.start()
    for copy in own_load(0):
        copy.start()
    for e in range(late):
        keep(e).start()
    greet(*[{"dp": flip(spread.device, bit)} for bit in (1, 2, 4)])
    serve(0)
    main_ref[...] = jnp.zeros_like(main_ref)
    tail_ref[...] = jnp.zeros_like(tail_ref)
    for copy in loads[:2]:
        copy.wait()
    mine_ref[...] = dt_ref[:own, :]

    def first(i, carry):
        rows = pl.ds(pl.multiple_of(i * TILE, TILE), TILE)
        mixed = h2_ref[rows, :].astype(F32) + dot(dt_ref[:, rows], wo_ref[...], TN) + bias_ref[0:1, :]
        mixed_ref[rows, :] = mixed
        res_ref[rows, :] = mixed + bias_ref[1:2, :]
        hg_ref[rows, :] = jnp.zeros((TILE, width), F32)
        normed, _ = standardize(mixed)
        h2_ref[rows, :] = (normed * gain_ref[1:2, :] + shift_ref[1:2, :]).astype(BF)
        return carry

    lax.fori_loop(0, tiles, first, 0)
    loads[2].wait()

    def own_unit(u, carry):
        for copy in own_load(u):
            copy.wait()
        up_low[...] = wide_w[0].astype(BF)
        down_low[...] = own_w[...].astype(BF)

        @pl.when(u + 1 < units)
        def _():
            for copy in own_load(u + 1):
                copy.start()

        @pl.when(u + 1 == units)
        def _():
            chunk_load(0).start()

        unit(smalls_ref[me, 2:3, pl.ds(pl.multiple_of(u * UNIT, UNIT), UNIT)], u * UNIT)
        serve(u + 1)
        reduce(u + 1)
        return carry

    lax.fori_loop(0, units, own_unit, 0)

    def take(ref, at):
        up_low[...] = ref[at + (0,)].astype(BF)
        for q in range(8):
            for k in range(width // UNIT):
                low = q * share + k * strip
                down_low[q * strip : (q + 1) * strip, k * UNIT : (k + 1) * UNIT] = ref[
                    at + (1, slice(low, low + strip))
                ].astype(BF)

    def foreign_unit(c, carry):
        @pl.when(c < early)
        def _():
            chunk_load(c).wait()
            take(wide_w, ())

        @pl.when(c + 1 < early)
        def _():
            chunk_load(c + 1).start()

        @pl.when(c >= early)
        def _():
            e = c - early
            keep(e).wait()
            spread.complete(e)
            take(land, (e,))

        cols = pl.ds(pl.multiple_of(lax.rem(c, units) * UNIT, UNIT), UNIT)
        unit(smalls_ref[source_of(c), 2:3, cols], None)
        serve(c + units + 1)
        reduce(c + units + 1)
        return carry

    lax.fori_loop(0, chunks, foreign_unit, 0)

    def tile_stores(i):
        rows = pl.ds(pl.multiple_of(i * TILE, TILE), TILE)
        return [
            pltpu.make_async_copy(source, target, tile_sems.at[i, k])
            for k, (source, target) in enumerate((
                (h2_ref.at[rows, :], result_out.at[rows, :]),
                (hg_ref.at[rows, :], mg_out.at[rows, :]),
                (dt_ref.at[:, rows], dt_out.at[:, rows]),
            ))
        ]

    def finish(i, carry):
        rows = pl.ds(pl.multiple_of(i * TILE, TILE), TILE)
        g = g_ref[rows, :].astype(F32)
        h2_ref[rows, :] = res_ref[rows, :].astype(BF)
        normed, inv_std = standardize(mixed_ref[rows, :])
        hg = hg_ref[rows, :]
        mg = g + norm_back(hg, normed, inv_std, gain_ref[1:2, :])
        hg_ref[rows, :] = mg
        low = mg.astype(BF)
        dt_ref[:, rows] = dot(wo_ref[...], low, NT).astype(BF)
        tail_ref[:own, :] += dot(mine_ref[:, rows], low, NN)
        for at, value in ((GAIN_TWO, hg * normed), (SHIFT_TWO, hg), (BIAS_ONE, mg), (BIAS_TWO, g)):
            tail_ref[own + at : own + at + 1, :] += jnp.sum(value, 0, keepdims=True)
        for copy in tile_stores(i):
            copy.start()
        return carry

    lax.fori_loop(0, tiles, finish, 0)
    total.finish(2)
    ends = [
        pltpu.make_async_copy(total.rows(at, total.piece), main_out.at[pl.ds(pl.multiple_of(at, 8), total.piece), :], sem)
        for at, sem in ((total.one_piece, out_sems.at[0]), (total.two_piece, out_sems.at[1]))
    ]
    ends.append(pltpu.make_async_copy(tail_ref, tail_out, out_sems.at[2]))
    for copy in ends:
        copy.start()
    for e in range(late):
        spread.sent(e)

    def drain(i, carry):
        for copy in tile_stores(i):
            copy.wait()
        return carry

    lax.fori_loop(0, tiles, drain, 0)
    for copy in ends:
        copy.wait()


def mlp(x, ot, wo, g, up, down, smalls, biases, gains, shifts, land, z):
    tokens, width = x.shape
    parts = smalls.shape[0]
    own = width // parts
    ff = up.shape[1]
    units = ff // UNIT
    chunks = units * (parts - 1)
    late = chunks - land.shape[0]
    tiles = tokens // TILE
    rows = 2 * ff
    tail = own + 64
    dma = pltpu.SemaphoreType.DMA
    return pl.pallas_call(
        mlp_kernel,
        in_specs=[WHOLE] * 5 + [ANY] * 7,
        out_specs=[ANY] * 5,
        out_shape=[
            shape_of((tokens, width), BF),
            shape_of((tokens, width), F32),
            shape_of((width, tokens), BF),
            shape_of((rows, width), F32),
            shape_of((tail, width), F32),
        ],
        scratch_shapes=[
            pltpu.VMEM((late, 2, width, UNIT), F32),
            pltpu.VMEM((2, width, UNIT), F32),
            pltpu.VMEM((UNIT, width), F32),
            pltpu.VMEM((tokens, width), BF),
            pltpu.VMEM((tokens, width), BF),
            pltpu.VMEM((width, tokens), BF),
            pltpu.VMEM((own, tokens), BF),
            pltpu.VMEM((rows, width), F32),
            pltpu.VMEM((tail, width), F32),
            pltpu.VMEM((tokens, width), F32),
            pltpu.VMEM((tokens, width), F32),
            pltpu.VMEM((tokens, width), F32),
            pltpu.VMEM((width, UNIT), BF),
            pltpu.VMEM((UNIT, width), BF),
            pltpu.VMEM((2, TILE, UNIT), F32),
            pltpu.VMEM((2, TILE, UNIT), F32),
            dma((3,)),
            dma((2,)),
            dma((late,)),
            dma((3,)),
            dma((tiles, 3)),
            dma((late, 9)),
            dma((late, 9)),
        ]
        + Total.scratch(rows, width),
        compiler_params=pltpu.CompilerParams(vmem_limit_bytes=63 * 2**20, collective_id=1, has_side_effects=True),
        name="mlp",
    )(wo, smalls, biases, gains, shifts, x, ot, g, up, down, land, z)


def body(
    dp_size,
    tokens,
    segments,
    norm_gains,
    norm_shifts,
    qkv_weight,
    qv_bias,
    out_weight,
    out_biases,
    up_weight,
    up_bias,
    down_weight,
    cotangent,
):
    width = tokens.shape[1]
    own = qkv_weight.shape[2]
    ff = up_weight.shape[1]
    seg = segments.reshape(segments.shape[0], 1, segments.shape[1])
    h1, weights, wo, bias, smalls = gather(
        tokens, norm_gains, norm_shifts, qkv_weight, out_weight, qv_bias, up_bias.reshape(1, ff)
    )
    qt, kt, vt, ot, lse, bound, land, z = attend(h1, seg, weights, bias, up_weight, down_weight)
    ot, lse = repair(bound, seg, qt, kt, vt, ot, lse)
    result, mg, dt, main, tail = mlp(
        tokens, ot, wo, cotangent, up_weight, down_weight, smalls, out_biases, norm_gains, norm_shifts, land, z
    )
    dq, dk, dv, main, rest = attend_back(seg, qt, kt, vt, ot, dt, lse, h1, main, tail)
    if dp_size > 8:
        main, rest = (value / 8 for value in lax.psum((main, rest), "dp"))
    token_grad, sums_one, down_grad, up_grad, out_weight_grad, result, qkv_grad = token_back(
        dq, dk, dv, weights, tokens, mg, norm_gains, main, rest, result, ff, own
    )
    sums_one = add_sums(sums_one)
    if dp_size > 8:
        sums_one = lax.psum(sums_one, "dp") / 8
    sums_two = rest[4 * own + 64 :]
    rows = rest[3 * own : 3 * own + 16, :own]
    return (
        result,
        token_grad,
        jnp.stack([sums_one[0], sums_two[GAIN_TWO]]),
        jnp.stack([sums_one[1], sums_two[SHIFT_TWO]]),
        qkv_grad,
        jnp.stack([rows[0], rows[8]]),
        out_weight_grad,
        sums_two[BIAS_ONE : BIAS_TWO + 1],
        up_grad,
        sums_two[UP_BIAS],
        down_grad,
    )


def solution(mesh):
    in_specs = (
        P("dp", None),
        P("dp", None),
        P(),
        P(),
        P(None, None, "mp"),
        P(None, "mp"),
        P("mp", None),
        P(),
        P(None, "mp"),
        P("mp"),
        P("mp", None),
        P("dp", None),
    )
    out_specs = (
        P("dp", None),
        P("dp", None),
        P(),
        P(),
        P(None, None, "mp"),
        P(None, "mp"),
        P("mp", None),
        P(),
        P(None, "mp"),
        P("mp"),
        P("mp", None),
    )
    return jax.shard_map(
        partial(body, mesh.shape["dp"]), mesh=mesh, in_specs=in_specs, out_specs=out_specs, check_vma=False
    )
```

```python
from functools import partial

import jax
import jax.numpy as jnp
from jax import lax
from jax.experimental import pallas as pl
from jax.experimental.pallas import tpu as pltpu
from jax.sharding import PartitionSpec as P

F32 = jnp.float32
BF = jnp.bfloat16
HEAD_DIM = 64
NORM_EPSILON = 1e-06
BIG = 1e30
LOG2E = 1.4426950408889634
SAFE_SCORE = 60.0
REACH = 512
TILE = 256
LONG_TILE = 512
EXTRA = 16
UNIT = 256
EARLY = 2

NN = (((1,), (0,)), ((), ()))
NT = (((1,), (1,)), ((), ()))
TN = (((0,), (0,)), ((), ()))
WHOLE = pl.BlockSpec(memory_space=pltpu.VMEM)
ONCE = pl.BlockSpec(memory_space=pltpu.VMEM, pipeline_mode=pl.Buffered(1))
ANY = pl.BlockSpec(memory_space=pl.ANY)


def dot(left, right, dims):
    return lax.dot_general(left, right, dims, preferred_element_type=F32)


def params(mib=56):
    return pltpu.CompilerParams(vmem_limit_bytes=mib * 2**20)


def standardize(values):
    centered = values - jnp.mean(values, -1, keepdims=True)
    inv_std = lax.rsqrt(jnp.mean(centered * centered, -1, keepdims=True) + NORM_EPSILON)
    return centered * inv_std, inv_std


def norm_back(grad_in, normed, inv_std, gain):
    scaled = grad_in * gain
    return inv_std * (
        scaled
        - jnp.mean(scaled, -1, keepdims=True)
        - normed * jnp.mean(scaled * normed, -1, keepdims=True)
    )


def shape_of(shape, dtype):
    return jax.ShapeDtypeStruct(shape, dtype)


def flip(index, bit):
    return index + bit - 2 * bit * lax.rem(lax.div(index, bit), 2)


def remote(src, dst, send_sem, recv_sem, **where):
    return pltpu.make_async_remote_copy(
        src_ref=src, dst_ref=dst, send_sem=send_sem, recv_sem=recv_sem, device_id=where,
        device_id_type=pl.DeviceIdType.MESH,
    )


CORE, SIDE, ACROSS, DIAG_A, DIAG_B, CORE_SIDE, CORE_ACROSS, CORE_A, CORE_B = range(9)


class Spread:
    def __init__(self, piece, send_sems, recv_sems, mine=None):
        self.piece, self.send_sems, self.recv_sems, self.mine = piece, send_sems, recv_sems, mine
        self.device = lax.axis_index("dp")
        self.place = lax.rem(self.device, 8)

    def copy(self, chunk, kind, origin, bit, half=None, own=False):
        ref = self.piece(chunk, origin, half)
        return remote(
            self.mine(chunk) if own else ref, ref, self.send_sems.at[chunk, kind], self.recv_sems.at[chunk, kind], dp=flip(self.device, bit)
        )

    def origin(self, bits):
        place = self.place
        for bit in bits:
            place = flip(place, bit)
        return place

    def outgoing(self, chunk, kind):
        bits, bit, half = {
            CORE: ((), 1, None),
            SIDE: ((), 2, None),
            ACROSS: ((), 4, None),
            DIAG_A: ((2,), 4, 0),
            DIAG_B: ((4,), 2, 1),
            CORE_SIDE: ((2,), 1, None),
            CORE_ACROSS: ((4,), 1, None),
            CORE_A: ((2, 4), 1, 0),
            CORE_B: ((2, 4), 1, 1),
        }[kind]
        own = self.mine is not None and kind in (CORE, SIDE, ACROSS)
        return self.copy(chunk, kind, self.origin(bits), bit, half, own)

    def incoming(self, chunk, kind):
        bits, bit, half = {
            CORE: ((1,), 1, None),
            SIDE: ((2,), 2, None),
            ACROSS: ((4,), 4, None),
            DIAG_A: ((2, 4), 4, 0),
            DIAG_B: ((2, 4), 2, 1),
            CORE_SIDE: ((1, 2), 1, None),
            CORE_ACROSS: ((1, 4), 1, None),
            CORE_A: ((1, 2, 4), 1, 0),
            CORE_B: ((1, 2, 4), 1, 1),
        }[kind]
        return self.copy(chunk, kind, self.origin(bits), bit, half)

    def start(self, chunk, *kinds):
        for kind in kinds:
            self.outgoing(chunk, kind).start()

    def arrived(self, chunk, *kinds):
        for kind in kinds:
            self.incoming(chunk, kind).wait_recv()

    def send(self, chunk):
        self.start(chunk, SIDE, ACROSS, CORE)

    def forward(self, chunk):
        self.arrived(chunk, SIDE)
        self.start(chunk, DIAG_A, CORE_SIDE)
        self.arrived(chunk, ACROSS)
        self.start(chunk, DIAG_B, CORE_ACROSS)

    def corner(self, chunk):
        self.arrived(chunk, DIAG_A)
        self.start(chunk, CORE_A)
        self.arrived(chunk, DIAG_B)
        self.start(chunk, CORE_B)

    def complete(self, chunk):
        self.arrived(chunk, CORE, CORE_SIDE, CORE_ACROSS, CORE_A, CORE_B)

    def sent(self, chunk):
        for kind in range(9):
            self.outgoing(chunk, kind).wait_send()


def greet(*peers):
    barrier = pltpu.get_barrier_semaphore()
    for peer in peers:
        pl.semaphore_signal(barrier, inc=1, device_id=peer, device_id_type=pl.DeviceIdType.MESH)
    pl.semaphore_wait(barrier, len(peers))


def foreign_order(me):
    half = lax.div(me, 2)
    return flip(me, 1), 2 - half, 3 - 3 * half


def front_kernel(
    gain_ref, shift_ref, qkv_ref, out_ref, qv_bias_ref, up_bias_ref, seg_ref, x_any, up_any, down_any,
    smalls_ref, bound_ref, h1_out, w_out, wo_out, qkvt_out, ot_out, lse_out, land_out, z_out,
    x_in, h1_ref, land, wo_land, z_land, mlp_land, pieces, small_land, w_low, wo_low, bias_col,
    qkvt_ref, ot_ref, lse_ref, qx, kx, vx, kn,
    x_sem, piece_sems, keep_sems, out_sems, slice_sems, z_send, z_recv, own_send, small_send, small_recv,
    send_sems, recv_sems,
):
    parts, rows, width = land.shape
    own = out_ref.shape[0]
    heads = own // HEAD_DIM
    tokens = x_in.shape[0]
    length = seg_ref.shape[1]
    units = pieces.shape[0]
    items = 3 + units
    early = mlp_land.shape[0]
    share, out_share, mlp_share = rows // 8, own // 8, width // 8
    split = (0, share // 16 * 8 + 8, share)
    strip = UNIT // 8
    me = lax.axis_index("mp")
    device = lax.axis_index("dp")
    order = foreign_order(me)
    out_chunk, mlp_chunk = 2 * (parts - 1), 3 * (parts - 1)

    def slab_rows(h, origin, half=None):
        start, stop = split[h], split[h + 1]
        middle = start + (stop - start + 8) // 16 * 8
        if half is not None:
            start, stop = (start, middle) if half == 0 else (middle, stop)
        return pl.ds(pl.multiple_of(origin * share + start, 8), stop - start)

    def out_rows(origin, half=None):
        start, stop = {None: (0, out_share), 0: (0, 16), 1: (16, out_share)}[half]
        return pl.ds(pl.multiple_of(origin * out_share + start, 8), stop - start)

    def piece(c, origin, half):
        if c < out_chunk:
            return land.at[order[c // 2], slab_rows(c % 2, origin, half), :]
        if c < mlp_chunk:
            return wo_land.at[order[c - out_chunk], out_rows(origin, half), :]
        rows = pl.ds(pl.multiple_of(origin * mlp_share, 8), mlp_share)
        if half is None:
            return mlp_land.at[c - mlp_chunk, :, rows, :]
        return mlp_land.at[c - mlp_chunk, half, rows, :]

    def mine(c):
        if c < mlp_chunk:
            return piece(c, lax.rem(device, 8), None)
        return z_land.at[order[(c - mlp_chunk) // units], (c - mlp_chunk) % units]

    spread = Spread(piece, send_sems, recv_sems, mine)
    place = spread.place

    def hop_ref(source, item):
        if item < 2:
            return land.at[source, slab_rows(item, place), :]
        if item == 2:
            return wo_land.at[source, out_rows(place), :]
        return z_land.at[source, item - 3]

    def own_ref(item):
        if item < 2:
            return qkv_ref.at[slab_rows(item, place), :]
        if item == 2:
            return out_ref.at[out_rows(place), :]
        return pieces.at[item - 3]

    def own_copies(item, act):
        def copy(up):
            return remote(
                own_ref(item), hop_ref(me, item), own_send.at[item, up], z_recv.at[me, item], mp=me + 2 * up - 1
            )

        @pl.when(me < parts - 1)
        def _():
            act(copy(1))

        @pl.when(me > 0)
        def _():
            act(copy(0))

    def pass_on(j, item, act):
        source = order[j]
        ref = hop_ref(source, item)

        def copy(step):
            return remote(ref, ref, z_send.at[source, item], z_recv.at[source, item], mp=me + step)

        end = 0 if j < parts - 2 or item < 3 else 1

        @pl.when((source < me) & (me < parts - 1 - end))
        def _():
            act(copy(1))

        @pl.when((source > me) & (me > end))
        def _():
            act(copy(-1))

    def landed(j, item):
        ref = hop_ref(order[j], item)
        remote(ref, ref, z_send.at[order[j], item], z_recv.at[order[j], item], mp=me).wait_recv()
        pass_on(j, item, lambda copy: copy.start())
        if item >= 3 and j * units + item - 3 < early:
            keep(j * units + item - 3).start()

    inner = (me > 0) & (me < parts - 1)

    def landings(inner_items, outer_items):
        @pl.when(inner)
        def _():
            for j, item in inner_items:
                landed(j, item)

        @pl.when(jnp.logical_not(inner))
        def _():
            for j, item in outer_items:
                landed(j, item)

    def keep(c):
        return pltpu.make_async_copy(
            mine(mlp_chunk + c), piece(mlp_chunk + c, place, None), keep_sems.at[c]
        )

    def small_copy(s):
        ref = small_land.at[me]
        return remote(ref, ref, small_send.at[s - 1], small_recv.at[me], mp=lax.rem(me + s, parts))

    def at_place(at, ref):
        w_low[at] = ref[...].astype(BF)

    def slice_stores(at):
        rows_at = pl.ds(pl.multiple_of(at * rows, rows), rows)
        own_at = pl.ds(pl.multiple_of(at * own, own), own)
        return [
            pltpu.make_async_copy(w_low.at[at], w_out.at[rows_at, :], slice_sems.at[at, 0]),
            pltpu.make_async_copy(qkvt_ref.at[rows_at, :], qkvt_out.at[rows_at, :], slice_sems.at[at, 1]),
            pltpu.make_async_copy(ot_ref.at[own_at, :], ot_out.at[own_at, :], slice_sems.at[at, 2]),
        ]

    x_copy = pltpu.make_async_copy(x_any, x_in, x_sem)
    h1_copy = pltpu.make_async_copy(h1_ref, h1_out, out_sems.at[0])
    lse_copy = pltpu.make_async_copy(lse_ref, lse_out, out_sems.at[1])
    wo_copy = pltpu.make_async_copy(wo_low, wo_out, out_sems.at[2])
    z_copy = pltpu.make_async_copy(z_land, z_out, out_sems.at[3])
    land_copy = pltpu.make_async_copy(mlp_land, land_out, out_sems.at[4])

    x_copy.start()
    copies = []
    for u in range(units):
        at = pl.ds(pl.multiple_of(place * mlp_share, 8), mlp_share)
        copies.append((up_any.at[at, pl.ds(u * UNIT, UNIT)], pieces.at[u, 0]))
        for c in range(width // UNIT):
            at = pl.ds(pl.multiple_of(u * UNIT + place * strip, 8), strip)
            copies.append((down_any.at[at, pl.ds(c * UNIT, UNIT)], pieces.at[u, 1, pl.ds(c * strip, strip), :]))
    piece_copies = [pltpu.make_async_copy(a, b, piece_sems.at[i]) for i, (a, b) in enumerate(copies)]
    for copy in piece_copies:
        copy.start()
    greet(
        *[{"mp": lax.rem(me + s, parts)} for s in range(1, parts)],
        *[{"dp": flip(device, bit)} for bit in (1, 2, 4)],
    )
    for item in range(2):
        own_copies(item, lambda copy: copy.start())
    small_land[me] = jnp.zeros(small_land.shape[1:], F32)
    small_land[me, 0:2, :own] = qv_bias_ref[...]
    small_land[me, 2:3, :] = up_bias_ref[...].reshape(1, width)
    for s in range(1, parts):
        small_copy(s).start()
    own_copies(2, lambda copy: copy.start())
    bound_ref[...] = jnp.zeros_like(bound_ref)
    bias_col[...] = jnp.zeros_like(bias_col)
    lse_ref[...] = jnp.zeros_like(lse_ref)
    z_land[me] = jnp.zeros(z_land.shape[1:], F32)

    @pl.when(jnp.logical_not(inner))
    def _():
        z_land[order[2]] = jnp.zeros(z_land.shape[1:], F32)

    for j in range(2):
        bias_col[0, 2 * j * own : (2 * j + 1) * own, :] = small_land[me].T[:own, j : j + 1]
    at_place(0, qkv_ref)
    wo_low[:own, :] = out_ref[...].astype(BF)
    x_copy.wait()

    def norm_tile(i, carry):
        at = pl.ds(pl.multiple_of(i * TILE, TILE), TILE)
        normed, _ = standardize(x_in[at, :].astype(F32))
        h1_ref[at, :] = (normed * gain_ref[0:1, :] + shift_ref[0:1, :]).astype(BF)
        return carry

    lax.fori_loop(0, tokens // TILE, norm_tile, 0)
    h1_copy.start()
    row = lax.broadcasted_iota(jnp.int32, (EXTRA, length), 0)
    for u in range(heads):
        vx[u, HEAD_DIM:, :] = jnp.ones((EXTRA, length), BF)

    def norm_bound(ref, u):
        value = ref[u, :HEAD_DIM, :].astype(F32)
        return jnp.max(jnp.sum(value * value, 0, keepdims=True), 1, keepdims=True)

    def attend(at, r):
        tokens_r = pl.ds(pl.multiple_of(r * length, length), length)
        base = at * rows
        value = dot(w_low[at], h1_ref[tokens_r, :], NT) + bias_col[at]
        scale = HEAD_DIM**-0.5
        qkvt_ref[pl.ds(pl.multiple_of(base, own), own), tokens_r] = value[:own].astype(BF) * jnp.asarray(scale, BF)
        qkvt_ref[pl.ds(pl.multiple_of(base + own, own), 2 * own), tokens_r] = value[own:].astype(BF)
        same = row == seg_ref[pl.ds(r, 1), :]
        for u in range(heads):
            qx[u, HEAD_DIM:, :] = jnp.where(same | (row >= 8), 0.0, -BIG).astype(BF)
            kx[u, HEAD_DIM:, :] = jnp.where(same, 1.0, 0.0).astype(BF)
        for u in range(heads):
            for k, ref in enumerate((qx, kx, vx)):
                from_row = pl.multiple_of(base + k * own + u * HEAD_DIM, HEAD_DIM)
                ref[u, :HEAD_DIM, :] = qkvt_ref[pl.ds(from_row, HEAD_DIM), tokens_r]
            kn[u] = kx[u].T
            bound_ref[...] = jnp.maximum(bound_ref[...], norm_bound(qx, u) * norm_bound(kx, u))
            to_row = pl.ds(pl.multiple_of(at * own + u * HEAD_DIM, HEAD_DIM), HEAD_DIM)
            for t in range(length // TILE):
                low, high = max(0, t * TILE - REACH), min(length, (t + 1) * TILE + REACH)
                cols = slice(t * TILE, (t + 1) * TILE)
                to_cols = pl.ds(pl.multiple_of(r * length + t * TILE, TILE), TILE)
                probs = [
                    jnp.exp2(dot(kn[u, k : k + TILE, :], qx[u, :, cols], NN) * LOG2E).astype(BF)
                    for k in range(low, high, TILE)
                ]
                out = dot(vx[u, :, low:high], jnp.concatenate(probs, 0), NN)
                total = out[HEAD_DIM : HEAD_DIM + 1, :]
                ot_ref[to_row, to_cols] = (out[:HEAD_DIM, :] * (1.0 / total)).astype(BF)
                lse_ref[pl.ds(at * heads + u, 1), to_cols] = jnp.log(total)

    w, m = out_chunk, mlp_chunk

    def event(n):
        if n == 0:
            landings(((0, 0), (1, 0)), ((0, 0),))
            spread.send(0)
            landings(((0, 1), (1, 1)), ((0, 1),))
            spread.send(1)
        if n == 1:
            for copy in piece_copies:
                copy.wait()
            landings(((2, 0),), ((1, 0),))
            spread.send(2)
            spread.forward(0)
            landings(((2, 1),), ((1, 1),))
            spread.send(3)
            own_copies(3, lambda copy: copy.start())
            spread.forward(1)
        if n == 2:
            landings(((0, 2), (1, 2)), ((2, 0),))
            spread.send(4)
            spread.corner(0)
            spread.forward(2)
            landings((), ((2, 1),))
            spread.send(5)
            own_copies(4, lambda copy: copy.start())
            spread.corner(1)
            spread.forward(3)
            for s in range(1, parts):
                ref = small_land.at[lax.rem(me + s, parts)]
                remote(ref, ref, small_send.at[0], small_recv.at[lax.rem(me + s, parts)], mp=me).wait_recv()
            smalls_ref[...] = small_land[...]
            for j, source in enumerate(order):
                cols = small_land[source].T
                for k in range(2):
                    bias_col[1 + j, 2 * k * own : (2 * k + 1) * own, :] = cols[:own, k : k + 1]
            spread.complete(0)
            spread.complete(1)
            at_place(1, land.at[order[0]])
        if n == 3:
            landings(((2, 2), (0, 3), (1, 3)), ((0, 2),))
            spread.send(w)
            spread.corner(2)
            spread.forward(4)
            own_copies(5, lambda copy: copy.start())
            spread.corner(3)
            spread.forward(5)
        if n == 4:
            landings(((0, 4), (1, 4)), ((1, 2), (0, 3)))
            spread.send(w + 1)
            spread.send(m)
            spread.corner(4)
            spread.corner(5)
            spread.forward(w)
            spread.complete(2)
            spread.complete(3)
            at_place(2, land.at[order[1]])
        if n == 5:
            landings(((0, 5), (1, 5)), ((2, 2), (0, 4)))
            spread.send(w + 2)
            spread.send(m + 1)
            spread.corner(w)
            spread.forward(w + 1)
            spread.forward(m)
        if n == 6:
            landings(((2, 3), (2, 4)), ((0, 5), (1, 3)))
            spread.forward(w + 2)
            spread.corner(w + 1)
            spread.corner(m)
            spread.forward(m + 1)
            spread.complete(4)
            spread.complete(5)
            at_place(3, land.at[order[2]])
        if n == 7:
            landings(((2, 5),), ((1, 4),))
            spread.corner(w + 2)
            spread.corner(m + 1)
            spread.complete(w)
            spread.complete(m)
        if n == 8:
            landings((), ((1, 5),))
            z_copy.start()
            spread.complete(w + 1)
            spread.complete(w + 2)
            spread.complete(m + 1)
            for c in range(early):
                keep(c).wait()
            land_copy.start()
            for j in range(parts - 1):
                wo_low[(j + 1) * own : (j + 2) * own, :] = wo_land[order[j]].astype(BF)
            wo_copy.start()
            lse_copy.start()

    event(0)

    def step(n, carry):
        at, r = lax.div(n, 2), lax.rem(n, 2)
        attend(at, r)

        @pl.when(r == 1)
        def _():
            for copy in slice_stores(at):
                copy.start()

        for e in range(1, 9):
            @pl.when(n + 1 == e)
            def _():
                event(e)

        return carry

    lax.fori_loop(0, 2 * parts, step, 0)
    for c in range(mlp_chunk + early):
        spread.sent(c)
    for item in range(items):
        own_copies(item, lambda copy: copy.wait_send())
        for j in range(parts - 1):
            pass_on(j, item, lambda copy: copy.wait_send())
    for s in range(1, parts):
        small_copy(s).wait_send()
    for copy in (h1_copy, lse_copy, wo_copy, z_copy, land_copy):
        copy.wait()
    for at in range(parts):
        for copy in slice_stores(at):
            copy.wait()


def front(x, seg, gains, shifts, qkv, out, qv_bias, up_bias, up, down):
    tokens, width = x.shape
    length = seg.shape[1]
    rows = qkv.shape[0]
    own = out.shape[0]
    parts = width // own
    heads = own // HEAD_DIM
    units = up.shape[1] // UNIT
    chunks = 3 * (parts - 1) + EARLY
    wide = HEAD_DIM + EXTRA
    dma = pltpu.SemaphoreType.DMA
    return pl.pallas_call(
        front_kernel,
        in_specs=[WHOLE] * 7 + [ANY] * 3,
        out_specs=[WHOLE] * 2 + [ANY] * 8,
        out_shape=[
            shape_of((parts, 8, width), F32),
            shape_of((8, 128), F32),
            shape_of((tokens, width), BF),
            shape_of((parts * rows, width), BF),
            shape_of((width, width), BF),
            shape_of((parts * rows, tokens), BF),
            shape_of((width, tokens), BF),
            shape_of((16, tokens), F32),
            shape_of((EARLY, 2, width, UNIT), F32),
            shape_of((parts, units, 2, width // 8, UNIT), F32),
        ],
        scratch_shapes=[
            pltpu.VMEM((tokens, width), BF),
            pltpu.VMEM((tokens, width), BF),
            pltpu.VMEM((parts, rows, width), F32),
            pltpu.VMEM((parts, own, width), F32),
            pltpu.VMEM((parts, units, 2, width // 8, UNIT), F32),
            pltpu.VMEM((EARLY, 2, width, UNIT), F32),
            pltpu.VMEM((units, 2, width // 8, UNIT), F32),
            pltpu.VMEM((parts, 8, width), F32),
            pltpu.VMEM((parts, rows, width), BF),
            pltpu.VMEM((width, width), BF),
            pltpu.VMEM((parts, rows, 1), F32),
            pltpu.VMEM((parts * rows, tokens), BF),
            pltpu.VMEM((width, tokens), BF),
            pltpu.VMEM((16, tokens), F32),
            pltpu.VMEM((heads, wide, length), BF),
            pltpu.VMEM((heads, wide, length), BF),
            pltpu.VMEM((heads, wide, length), BF),
            pltpu.VMEM((heads, length, wide), BF),
            dma,
            dma((units * (1 + width // UNIT),)),
            dma((EARLY,)),
            dma((5,)),
            dma((parts, 3)),
            dma((parts, 3 + units)),
            dma((parts, 3 + units)),
            dma((3 + units, 2)),
            dma((parts - 1,)),
            dma((parts,)),
            dma((chunks, 9)),
            dma((chunks, 9)),
        ],
        compiler_params=pltpu.CompilerParams(vmem_limit_bytes=62 * 2**20, collective_id=0, has_side_effects=True),
        name="front",
    )(gains, shifts, qkv, out, qv_bias, up_bias, seg, x, up, down)


def repair_kernel(
    bound_ref, seg_ref, qkvt_any, ot_in, lse_in, ot_out, lse_out, qx, kx, vx, lse_row, sems,
):
    rows_here, length = seg_ref.shape
    parts = 4
    own = qkvt_any.shape[0] // (3 * parts)
    heads = parts * own // HEAD_DIM
    safe = jnp.max(bound_ref[...]) < SAFE_SCORE**2

    @pl.when(jnp.logical_not(safe))
    def _():
        row = lax.broadcasted_iota(jnp.int32, (EXTRA, length), 0)
        vx[HEAD_DIM:, :] = jnp.ones((EXTRA, length), BF)

        def move(copies):
            copies = [pltpu.make_async_copy(a, b, sems.at[i]) for i, (a, b) in enumerate(copies)]
            for copy in copies:
                copy.start()
            for copy in copies:
                copy.wait()

        def head(i, carry):
            r, h = lax.div(i, heads), lax.rem(i, heads)
            rows = pl.ds(pl.multiple_of(h * HEAD_DIM, HEAD_DIM), HEAD_DIM)
            tokens = pl.ds(pl.multiple_of(r * length, length), length)
            head_at = lax.div(h, heads // parts) * 3 * own + lax.rem(h, heads // parts) * HEAD_DIM
            same = row == seg_ref[pl.ds(r, 1), :]
            qx[HEAD_DIM:, :] = jnp.where(same | (row >= 8), 0.0, -BIG).astype(BF)
            kx[HEAD_DIM:, :] = jnp.where(same, 1.0, 0.0).astype(BF)
            move([
                (
                    qkvt_any.at[pl.ds(pl.multiple_of(head_at + k * own, HEAD_DIM), HEAD_DIM), tokens],
                    target.at[pl.ds(0, HEAD_DIM), :],
                )
                for k, target in enumerate((qx, kx, vx))
            ])

            @pl.when(h == 0)
            def _():
                lse_row[...] = jnp.zeros_like(lse_row)

            for t in range(length // TILE):
                cols = slice(t * TILE, (t + 1) * TILE)
                scores = dot(kx[...], qx[:, cols], TN)
                highest = jnp.max(scores, 0, keepdims=True)
                probs = jnp.exp2((scores - highest) * LOG2E).astype(BF)
                out = dot(vx[...], probs, NN)
                total = out[HEAD_DIM : HEAD_DIM + 1, :]
                qx[:HEAD_DIM, cols] = (out[:HEAD_DIM, :] * (1.0 / total)).astype(BF)
                lse_row[pl.ds(h, 1), cols] = jnp.log(total) + highest
            move([(qx.at[pl.ds(0, HEAD_DIM), :], ot_out.at[rows, tokens])])

            @pl.when(h == heads - 1)
            def _():
                move([(lse_row, lse_out.at[:, tokens])])

            return carry

        lax.fori_loop(0, rows_here * heads, head, 0)


def repair(bound, seg, qkvt, ot, lse):
    length = seg.shape[1]
    return pl.pallas_call(
        repair_kernel,
        in_specs=[WHOLE, WHOLE, ANY, ANY, ANY],
        out_specs=[ANY, ANY],
        out_shape=[shape_of(ot.shape, BF), shape_of(lse.shape, F32)],
        input_output_aliases={3: 0, 4: 1},
        scratch_shapes=[pltpu.VMEM((HEAD_DIM + EXTRA, length), BF)] * 3
        + [pltpu.VMEM((16, length), F32), pltpu.SemaphoreType.DMA((3,))],
        compiler_params=params(),
        name="repair",
    )(bound, seg, qkvt, ot, lse)


def split3(value):
    first = value.astype(BF)
    rest = value - first.astype(F32)
    second = rest.astype(BF)
    return first, second, (rest - second.astype(F32)).astype(BF)


class Total:
    def __init__(self, out, sends, recvs, near=None, side_land=None, across_land=None):
        self.out, self.near = out, near
        self.side_land, self.across_land, self.sends, self.recvs = side_land, across_land, sends, recvs
        self.device = lax.axis_index("dp")
        place = lax.rem(self.device, 8)
        self.half = out.shape[0] // 2
        self.part, self.piece = self.half // 4, self.half // 8
        bits = [lax.rem(lax.div(place, bit), 2) for bit in (1, 2, 4)]
        self.base = bits[0] * self.half
        self.away = (1 - bits[0]) * self.half
        self.one = self.base + bits[1] * self.part
        self.one_away = self.base + (1 - bits[1]) * self.part
        self.two = self.base + 2 * self.part + bits[2] * self.part
        self.two_away = self.base + 2 * self.part + (1 - bits[2]) * self.part
        self.one_piece = self.one + bits[2] * self.piece
        self.one_piece_away = self.one + (1 - bits[2]) * self.piece
        self.two_piece = self.two + bits[1] * self.piece
        self.two_piece_away = self.two + (1 - bits[1]) * self.piece

    def rows(self, start, count):
        return self.out.at[pl.ds(pl.multiple_of(start, 8), count), :]

    def copy(self, sem, bit, src, dst):
        return remote(src, dst, self.sends.at[sem], self.recvs.at[sem], dp=flip(self.device, bit))

    def over(self, sem, bit, start, count):
        ref = self.rows(start, count)
        return self.copy(sem, bit, ref, ref)

    def copies(self, stage):
        part, piece = self.part, self.piece
        first, second = pl.ds(0, part), pl.ds(part, piece)
        if stage == 0:
            return [self.copy(0, 1, self.rows(self.away, self.half), self.near)]
        if stage == 1:
            return [
                self.copy(1, 2, self.rows(self.one_away, part), self.side_land.at[first, :]),
                self.copy(2, 4, self.rows(self.two_away, part), self.across_land.at[first, :]),
            ]
        if stage == 2:
            return [
                self.copy(3, 4, self.rows(self.one_piece_away, piece), self.across_land.at[second, :]),
                self.copy(4, 2, self.rows(self.two_piece_away, piece), self.side_land.at[second, :]),
            ]
        if stage == 3:
            return [self.over(5, 4, self.one_piece, piece), self.over(6, 2, self.two_piece, piece)]
        if stage == 4:
            return [self.over(7, 2, self.one, part), self.over(8, 4, self.two, part)]
        return [self.over(9, 1, self.base, self.half)]

    def arrivals(self, stage):
        part, piece = self.part, self.piece
        if stage == 3:
            return [self.over(5, 4, self.one_piece_away, piece), self.over(6, 2, self.two_piece_away, piece)]
        if stage == 4:
            return [self.over(7, 2, self.one_away, part), self.over(8, 4, self.two_away, part)]
        if stage == 5:
            return [self.over(9, 1, self.away, self.half)]
        return self.copies(stage)

    def add(self, start, ref, at, count):
        step = 48 if count % 48 == 0 else 56

        def some(i, carry):
            rows = pl.ds(pl.multiple_of(start + i * step, 8), step)
            self.out[rows, :] += ref[pl.ds(pl.multiple_of(at + i * step, 8), step), :]
            return carry

        lax.fori_loop(0, count // step, some, 0)

    def finish(self, stage):
        for copy in self.copies(stage):
            copy.wait_send()
        for copy in self.arrivals(stage):
            copy.wait_recv()
        if stage == 0:
            self.add(self.base, self.near, 0, self.half)
        elif stage == 1:
            self.add(self.one, self.side_land, 0, self.part)
            self.add(self.two, self.across_land, 0, self.part)
        elif stage == 2:
            self.add(self.one_piece, self.across_land, self.part, self.piece)
            self.add(self.two_piece, self.side_land, self.part, self.piece)

    def start(self, stage):
        for copy in self.copies(stage):
            copy.start()

    @staticmethod
    def scratch(rows, width):
        dma = pltpu.SemaphoreType.DMA
        return [
            dma((10,)),
            dma((10,)),
            pltpu.VMEM((rows // 2, width), F32),
            pltpu.VMEM((rows // 8 + rows // 16, width), F32),
            pltpu.VMEM((rows // 8 + rows // 16, width), F32),
        ]


def attend_back_kernel(
    seg_ref, qkv_ref, ot_ref, dt_ref, lse_ref, h1_any, main_any, tail_any,
    dqkv_ref, main_out, rest_out,
    qx, kx, vx, dx, qn, dn, kn, acc, h1_ref, main_ref, rest_ref, whole_ref, in_sems, out_sems, main_send, main_recv, *comm,
):
    step = pl.program_id(0)
    own, length = ot_ref.shape
    width = h1_ref.shape[1]
    heads = own // HEAD_DIM
    tail_at = rest_ref.shape[0] - tail_any.shape[0]
    main = Total(main_ref, main_send, main_recv)
    rest = Total(rest_ref, *comm)
    whole = Total(whole_ref, *comm[:2])
    loads = [
        pltpu.make_async_copy(main_any.at[pl.ds(pl.multiple_of(at, 8), main.piece), :], main.rows(at, main.piece), sem)
        for at, sem in ((main.one_piece, in_sems.at[0]), (main.two_piece, in_sems.at[1]))
    ]
    loads.append(pltpu.make_async_copy(tail_any, rest_ref.at[pl.ds(tail_at, tail_any.shape[0]), :], in_sems.at[2]))
    loads.append(pltpu.make_async_copy(h1_any, h1_ref, in_sems.at[3]))
    stores = [
        pltpu.make_async_copy(main_ref, main_out, out_sems.at[0]),
        pltpu.make_async_copy(whole_ref, rest_out, out_sems.at[1]),
    ]

    @pl.when(step == 0)
    def _():
        for copy in loads:
            copy.start()
        greet(*[{"dp": flip(main.device, bit)} for bit in (1, 2, 4)])
        for copy in loads[:2]:
            copy.wait()
        main.start(3)

    @pl.when(step == 1)
    def _():
        main.finish(3)
        main.start(4)

    @pl.when(step == 3)
    def _():
        rest.finish(0)
        rest.start(1)
        main.finish(4)
        main.start(5)

    @pl.when(step == 4)
    def _():
        rest.finish(1)
        rest.start(2)

    @pl.when(step == 5)
    def _():
        rest.finish(2)
        for at in (rest.one_piece, rest.two_piece):
            rows = pl.ds(pl.multiple_of(at, 8), rest.piece)
            whole_ref[rows, :] = rest_ref[rows, :]
        whole.start(3)
        main.finish(5)
        stores[0].start()

    @pl.when(step == 6)
    def _():
        whole.finish(3)
        whole.start(4)

    @pl.when(step == 7)
    def _():
        whole.finish(4)
        whole.start(5)

    row = lax.broadcasted_iota(jnp.int32, (EXTRA, length), 0)
    same = row == seg_ref[pl.ds(jnp.where((step == 1) | (step >= 5), 1, 0), 1), :]
    key_extra = jnp.where(same | ((row >= 8) & (row < 11)), 1.0, 0.0).astype(BF)
    value_extra = jnp.where(row < 3, 1.0, 0.0).astype(BF)
    query_extra = jnp.where(same | (row >= 8), 0.0, -BIG)

    def three_rows(value, at):
        first, second, third = split3(value)
        out = jnp.where(row == at, first.astype(F32), 0.0)
        out = jnp.where(row == at + 1, second.astype(F32), out)
        return jnp.where(row == at + 2, third.astype(F32), out)

    head_at = jnp.where(step < 2, 0, lax.rem(step - 2, 3) + 1) * heads

    def head(u):
        rows = slice(u * HEAD_DIM, (u + 1) * HEAD_DIM)
        dq_rows, dk_rows, dv_rows = (slice(rows.start + k * own, rows.stop + k * own) for k in range(3))
        qx[u, :HEAD_DIM, :] = qkv_ref[dq_rows, :]
        kx[u, :HEAD_DIM, :] = qkv_ref[dk_rows, :]
        vx[u, :HEAD_DIM, :] = qkv_ref[dv_rows, :]
        dx[u, :HEAD_DIM, :] = dt_ref[rows, :]
        inner = jnp.sum(dt_ref[rows, :].astype(F32) * ot_ref[rows, :].astype(F32), 0, keepdims=True)
        log_sum = lse_ref[pl.ds(head_at + u, 1), :]
        qx[u, HEAD_DIM:, :] = (query_extra + three_rows(-log_sum, 8)).astype(BF)
        kx[u, HEAD_DIM:, :] = key_extra
        vx[u, HEAD_DIM:, :] = value_extra
        dx[u, HEAD_DIM:, :] = three_rows(-inner, 0).astype(BF)
        qn[u] = qx[u].T
        dn[u] = dx[u].T
        kn[u] = kx[u].T
        for t in range(length // TILE):
            low, high = max(0, t * TILE - REACH), min(length, (t + 1) * TILE + REACH)
            keys = slice(t * TILE, (t + 1) * TILE)
            probs, score_grads = [], []
            for q in range(low, high, TILE):
                prob = jnp.exp2(dot(qn[u, q : q + TILE, :], kx[u, :, keys], NN) * LOG2E)
                prob_grad = dot(dn[u, q : q + TILE, :], vx[u, :, keys], NN)
                probs.append(prob.astype(BF))
                score_grads.append((prob * prob_grad).astype(BF))
            probs = jnp.concatenate(probs, 0)
            score_grads = jnp.concatenate(score_grads, 0)
            dqkv_ref[dv_rows, keys] = dot(dx[u, :HEAD_DIM, low:high], probs, NN).astype(BF)
            dqkv_ref[dk_rows, keys] = dot(qx[u, :HEAD_DIM, low:high], score_grads, NN).astype(BF)
            part = dot(score_grads, kx[u, :HEAD_DIM, keys], NT)
            if t == 0:
                acc[u, low:high, :] = part
                if high < length:
                    acc[u, high:, :] = jnp.zeros((length - high, HEAD_DIM), F32)
            else:
                acc[u, low:high, :] += part
        dqkv_ref[dq_rows, :] = (acc[u] * HEAD_DIM**-0.5).T.astype(BF)

    for u in range(heads):
        head(u)

    def own_grads(tokens, add):
        part = dot(dqkv_ref[...], h1_ref[tokens, :], NN)
        rest_ref[: 3 * own, :] = rest_ref[: 3 * own, :] + part if add else part
        ones = jnp.ones((8, length), BF)
        for k in (0, 2):
            rows = slice(3 * own + k * 4, 3 * own + k * 4 + 8)
            part = dot(ones, dqkv_ref[k * own : (k + 1) * own, :], NT)
            rest_ref[rows, :own] = rest_ref[rows, :own] + part if add else part

    @pl.when(step == 0)
    def _():
        rest_ref[3 * own : tail_at, :] = jnp.zeros((tail_at - 3 * own, width), F32)
        loads[3].wait()
        own_grads(slice(0, length), False)

    @pl.when(step == 1)
    def _():
        own_grads(slice(length, 2 * length), True)
        loads[2].wait()
        rest.start(0)

    @pl.when(step == 7)
    def _():
        whole.finish(5)
        stores[1].start()
        for copy in stores:
            copy.wait()


def attend_back(seg, qkvt, ot, dt, lse, h1, main, tail):
    width, tokens = ot.shape
    _, length = seg.shape
    own = width // 4
    heads = own // HEAD_DIM
    wide = HEAD_DIM + EXTRA
    rest_rows = 3 * own + 64 + tail.shape[0]
    row_of = lambda s: jnp.where((s == 1) | (s >= 5), 1, 0)
    part_of = lambda s: jnp.where(s < 2, 0, lax.rem(s - 2, 3) + 1)
    block = pl.BlockSpec((own, length), lambda s: (part_of(s), row_of(s)))
    wide_block = pl.BlockSpec((3 * own, length), lambda s: (part_of(s), row_of(s)))
    dma = pltpu.SemaphoreType.DMA
    return pl.pallas_call(
        attend_back_kernel,
        grid=(8,),
        in_specs=[ONCE, wide_block, block, block]
        + [pl.BlockSpec((16, length), lambda s: (0, row_of(s))), ANY, ANY, ANY],
        out_specs=[wide_block, ANY, ANY],
        out_shape=[shape_of(qkvt.shape, BF), shape_of(main.shape, F32), shape_of((rest_rows, width), F32)],
        scratch_shapes=[pltpu.VMEM((heads, wide, length), BF)] * 4
        + [pltpu.VMEM((heads, length, wide), BF)] * 3
        + [
            pltpu.VMEM((heads, length, HEAD_DIM), F32),
            pltpu.VMEM((tokens, width), BF),
            pltpu.VMEM(main.shape, F32),
            pltpu.VMEM((rest_rows, width), F32),
            pltpu.VMEM((rest_rows, width), F32),
            dma((4,)),
            dma((2,)),
            dma((10,)),
            dma((10,)),
        ]
        + Total.scratch(rest_rows, width),
        compiler_params=pltpu.CompilerParams(vmem_limit_bytes=60 * 2**20, collective_id=2, has_side_effects=True),
        name="attend_back",
    )(seg, qkvt, ot, dt, lse, h1, main, tail)


def token_kernel(
    dqkv_ref, w_ref, x_ref, mg_ref, gain_ref, main_any, rest_any, result_any,
    tg_ref, sums_ref, down_ref, up_ref, out_ref, result_ref, qkv_ref,
    main_v, rest_v, result_v, in_sems, out_sems,
):
    step = pl.program_id(0)
    last = pl.num_programs(0) - 1
    ff = down_ref.shape[0]
    own = out_ref.shape[0]
    out_at = 3 * own + 64
    loads = [
        pltpu.make_async_copy(source, target, in_sems.at[i])
        for i, (source, target) in enumerate(((rest_any, rest_v), (main_any, main_v), (result_any, result_v)))
    ]
    stores = [
        pltpu.make_async_copy(source, target, out_sems.at[i])
        for i, (source, target) in enumerate((
            (main_v.at[pl.ds(0, ff), :], down_ref),
            (main_v.at[pl.ds(ff, up_ref.shape[0]), :], up_ref),
            (rest_v.at[pl.ds(out_at, own), :], out_ref),
            (result_v, result_ref),
            (rest_v.at[pl.ds(0, 3 * own), :], qkv_ref),
        ))
    ]

    @pl.when(step == 0)
    def _():
        for copy in loads:
            copy.start()
        sums_ref[...] = jnp.zeros_like(sums_ref)

    @pl.when(step == last - 1)
    def _():
        for copy in loads:
            copy.wait()
        for copy in stores:
            copy.start()

    hg = dot(dqkv_ref[...], w_ref[...], TN)
    normed, inv_std = standardize(x_ref[...].astype(F32))
    tg_ref[...] = mg_ref[...] + norm_back(hg, normed, inv_std, gain_ref[0:1, :])
    sums_ref[0:1, :] += jnp.sum(hg * normed, 0, keepdims=True)
    sums_ref[1:2, :] += jnp.sum(hg, 0, keepdims=True)

    @pl.when(step == last)
    def _():
        for copy in stores:
            copy.wait()


def token_back(dqkv, weights, x, mg, gains, main, rest, result, ff, own):
    tokens, width = x.shape
    row = pl.BlockSpec((LONG_TILE, width), lambda t: (t, 0))
    col = pl.BlockSpec((weights.shape[0], LONG_TILE), lambda t: (0, t))
    dma = pltpu.SemaphoreType.DMA
    return pl.pallas_call(
        token_kernel,
        grid=(tokens // LONG_TILE,),
        in_specs=[col, ONCE, row, row, ONCE, ANY, ANY, ANY],
        out_specs=[row, ONCE, ANY, ANY, ANY, ANY, ANY],
        out_shape=[
            shape_of((tokens, width), F32),
            shape_of((8, width), F32),
            shape_of((ff, width), F32),
            shape_of((width, ff), F32),
            shape_of((own, width), F32),
            shape_of((tokens, width), BF),
            shape_of((3 * own, width), F32),
        ],
        scratch_shapes=[
            pltpu.VMEM(main.shape, F32),
            pltpu.VMEM(rest.shape, F32),
            pltpu.VMEM((tokens, width), BF),
            dma((3,)),
            dma((5,)),
        ],
        compiler_params=params(),
        name="token_back",
    )(dqkv, weights, x, mg, gains, main, rest, result)


def sums_kernel(
    in_ref, rest_any, gains_ref, shifts_ref, biases_ref, qv_bias_ref, up_bias_ref,
    land, rows_v, rows_sem, sends, recvs, *, own, exchange,
):
    width = in_ref.shape[1]
    at = 4 * own + 64
    loads = [
        pltpu.make_async_copy(rest_any.at[pl.ds(low, 16), :], rows_v.at[i], rows_sem.at[i])
        for i, low in enumerate((3 * own, at))
    ]
    for copy in loads:
        copy.start()
    if exchange:
        device = lax.axis_index("dp")
        place = lax.rem(device, 8)
        others = []
        for bits in range(1, 8):
            other = device
            for bit in (1, 2, 4):
                if bits & bit:
                    other = flip(other, bit)
            others.append(other)
        greet(*[{"dp": other} for other in others])
        copies = [
            remote(in_ref, land.at[place], sends.at[i], recvs.at[place], dp=other) for i, other in enumerate(others)
        ]
        for copy in copies:
            copy.start()
        land[place] = in_ref[...]
    for copy in loads:
        copy.wait()
    small = rows_v[1]
    biases_ref[...] = small[BIAS_ONE : BIAS_TWO + 1, :]
    up_bias_ref[...] = small[UP_BIAS : UP_BIAS + 1, :]
    qv_bias_ref[0:1, :] = rows_v[0, 0:1, :own]
    qv_bias_ref[1:2, :] = rows_v[0, 8:9, :own]
    gains_ref[1:2, :] = small[GAIN_TWO : GAIN_TWO + 1, :]
    shifts_ref[1:2, :] = small[SHIFT_TWO : SHIFT_TWO + 1, :]
    if exchange:
        for other in others:
            peer = lax.rem(other, 8)
            remote(in_ref, land.at[peer], sends.at[0], recvs.at[peer], dp=other).wait_recv()
        sums = jnp.sum(land[...], 0)
    else:
        sums = in_ref[...]
    gains_ref[0:1, :] = sums[0:1, :]
    shifts_ref[0:1, :] = sums[1:2, :]
    if exchange:
        for copy in copies:
            copy.wait_send()


def add_sums(sums, rest, own, exchange):
    width = sums.shape[1]
    dma = pltpu.SemaphoreType.DMA
    options = dict(collective_id=3, has_side_effects=True) if exchange else {}
    return pl.pallas_call(
        partial(sums_kernel, own=own, exchange=exchange),
        in_specs=[WHOLE, ANY],
        out_specs=[WHOLE] * 5,
        out_shape=[
            shape_of((2, width), F32),
            shape_of((2, width), F32),
            shape_of((2, width), F32),
            shape_of((2, own), F32),
            shape_of((1, width), F32),
        ],
        scratch_shapes=[
            pltpu.VMEM((8,) + sums.shape, F32),
            pltpu.VMEM((2, 16, width), F32),
            dma((2,)),
            dma((7,)),
            dma((8,)),
        ],
        compiler_params=pltpu.CompilerParams(**options),
        name="add_sums",
    )(sums, rest)


GELU_C = 0.7978845608028654
GELU_A = 0.044715


def gelu_both(pre):
    square = pre * pre
    half = 0.5 + 0.5 * jnp.tanh(pre * (GELU_C + (GELU_C * GELU_A) * square))
    act = pre * half
    slope = half + act * (1.0 - half) * (2.0 * GELU_C + (6.0 * GELU_C * GELU_A) * square)
    return act, slope


GAIN_TWO, SHIFT_TWO, BIAS_ONE, BIAS_TWO, UP_BIAS = range(5)


def mlp_kernel(
    wo_ref, smalls_ref, bias_ref, gain_ref, shift_ref, x_any, ot_any, g_any, up_any, down_any, land_any, z_any,
    result_out, mg_out, dt_out, main_out, tail_out,
    land, z_far, wide_w, own_w, g_ref, h2_ref, dt_ref, mine_ref, main_ref, tail_ref, mixed_ref, res_ref, hg_ref,
    up_low, down_low, pre_s, ag_s,
    in_sems, w_sems, keep_sems, far_keep, far_send, far_recv, out_sems, tile_sems, send_sems, recv_sems, *comm,
):
    tokens, width = g_ref.shape
    parts = smalls_ref.shape[0]
    own = mine_ref.shape[0]
    ff = up_any.shape[1]
    units = ff // UNIT
    chunks = units * (parts - 1)
    late = land.shape[0]
    early = chunks - late
    share = z_any.shape[3]
    strip = UNIT // 8
    tiles = tokens // TILE
    me = lax.axis_index("mp")
    order = foreign_order(me)
    total = Total(main_ref, *comm)

    def source_of(c):
        j = lax.div(c, units)
        return jnp.where(j == 0, order[0], jnp.where(j == 1, order[1], order[2]))

    def piece(e, origin, half):
        rows = pl.ds(pl.multiple_of(origin * share, 8), share)
        if half is None:
            return land.at[e, :, rows, :]
        return land.at[e, half, rows, :]

    far_at = units * (parts - 2) - early

    def mine(e):
        if e >= far_at:
            return z_far.at[e - far_at]
        return z_any.at[order[(early + e) // units], (early + e) % units]

    inner = (me > 0) & (me < parts - 1)

    def far_copy(u):
        step = jnp.where(lax.div(me, 2) == 0, -1, 1)
        return remote(z_any.at[order[2], u], z_far.at[u], far_send.at[u], far_recv.at[u], mp=me + step)

    def far_local(u):
        return pltpu.make_async_copy(z_any.at[order[2], u], z_far.at[u], far_keep.at[u])

    def far(u):
        @pl.when(inner)
        def _():
            far_local(u).wait()

        @pl.when(jnp.logical_not(inner))
        def _():
            remote(z_far.at[u], z_far.at[u], far_send.at[u], far_recv.at[u], mp=me).wait_recv()

    spread = Spread(piece, send_sems, recv_sems, mine)

    def keep(e):
        return pltpu.make_async_copy(mine(e), piece(e, spread.place, None), keep_sems.at[e])

    def serve(n):
        for e in range(late):
            @pl.when(n == e)
            def _():
                if e >= far_at:
                    far(e - far_at)
                    keep(e).start()
                spread.send(e)

            @pl.when(n == e + 1)
            def _():
                spread.forward(e)

            @pl.when(n == e + 2)
            def _():
                spread.corner(e)

    def reduce(n):
        @pl.when(n == units)
        def _():
            total.start(0)

        @pl.when(n == units + 5)
        def _():
            total.finish(0)
            total.start(1)

        @pl.when(n == units + 8)
        def _():
            total.finish(1)
            total.start(2)

    def unit(bias, grads_at):
        def front(i):
            rows = slice(i * TILE, (i + 1) * TILE)
            pre_s[i % 2] = dot(h2_ref[rows, :], up_low[...], NN) + bias
            ag_s[i % 2] = dot(g_ref[rows, :], down_low[...], NT)

        def back(i):
            rows = slice(i * TILE, (i + 1) * TILE)
            act, slope = gelu_both(pre_s[i % 2])
            act = act.astype(BF)
            pre_grad = (ag_s[i % 2] * slope).astype(BF)
            res_ref[rows, :] += dot(act, down_low[...], NN)
            hg_ref[rows, :] += dot(pre_grad, up_low[...], NT)
            if grads_at is not None:
                h2 = h2_ref[rows, :]
                g = g_ref[rows, :]
                cols = pl.ds(pl.multiple_of(grads_at, UNIT), UNIT)
                main_ref[cols, :] += dot(act, g, TN)
                main_ref[ff:, cols] += dot(h2, pre_grad, TN)
                at = own + UP_BIAS
                tail_ref[at : at + 1, cols] += jnp.sum(pre_grad.astype(F32), 0, keepdims=True)

        front(0)
        for i in range(tiles):
            if i + 1 < tiles:
                front(i + 1)
            back(i)

    loads = [
        pltpu.make_async_copy(source, target, in_sems.at[i])
        for i, (source, target) in enumerate(((ot_any, dt_ref), (x_any, h2_ref), (g_any, g_ref)))
    ]

    def own_load(u):
        cols = pl.ds(pl.multiple_of(u * UNIT, UNIT), UNIT)
        return [
            pltpu.make_async_copy(up_any.at[:, cols], wide_w.at[0], w_sems.at[0]),
            pltpu.make_async_copy(down_any.at[cols, :], own_w, w_sems.at[1]),
        ]

    def chunk_load(c):
        return pltpu.make_async_copy(land_any.at[c], wide_w, w_sems.at[0])

    for copy in loads:
        copy.start()
    for copy in own_load(0):
        copy.start()
    for e in range(far_at):
        keep(e).start()

    @pl.when(inner)
    def _():
        for u in range(units):
            far_local(u).start()

    greet(
        *[{"mp": lax.rem(me + s, parts)} for s in range(1, parts)],
        *[{"dp": flip(spread.device, bit)} for bit in (1, 2, 4)],
    )

    @pl.when(inner)
    def _():
        for u in range(units):
            far_copy(u).start()

    serve(0)
    main_ref[...] = jnp.zeros_like(main_ref)
    tail_ref[...] = jnp.zeros_like(tail_ref)
    for copy in loads[:2]:
        copy.wait()
    mine_ref[...] = dt_ref[:own, :]

    def first(i, carry):
        rows = pl.ds(pl.multiple_of(i * TILE, TILE), TILE)
        mixed = h2_ref[rows, :].astype(F32) + dot(dt_ref[:, rows], wo_ref[...], TN) + bias_ref[0:1, :]
        mixed_ref[rows, :] = mixed
        res_ref[rows, :] = mixed + bias_ref[1:2, :]
        hg_ref[rows, :] = jnp.zeros((TILE, width), F32)
        normed, _ = standardize(mixed)
        h2_ref[rows, :] = (normed * gain_ref[1:2, :] + shift_ref[1:2, :]).astype(BF)
        return carry

    lax.fori_loop(0, tiles, first, 0)
    loads[2].wait()

    def own_unit(u, carry):
        for copy in own_load(u):
            copy.wait()
        up_low[...] = wide_w[0].astype(BF)
        down_low[...] = own_w[...].astype(BF)

        @pl.when(u + 1 < units)
        def _():
            for copy in own_load(u + 1):
                copy.start()

        @pl.when(u + 1 == units)
        def _():
            chunk_load(0).start()

        unit(smalls_ref[me, 2:3, pl.ds(pl.multiple_of(u * UNIT, UNIT), UNIT)], u * UNIT)
        serve(u + 1)
        reduce(u + 1)
        return carry

    lax.fori_loop(0, units, own_unit, 0)

    def take(ref, at):
        up_low[...] = ref[at + (0,)].astype(BF)
        for q in range(8):
            for k in range(width // UNIT):
                low = q * share + k * strip
                down_low[q * strip : (q + 1) * strip, k * UNIT : (k + 1) * UNIT] = ref[
                    at + (1, slice(low, low + strip))
                ].astype(BF)

    def foreign_unit(c, carry):
        @pl.when(c < early)
        def _():
            chunk_load(c).wait()
            take(wide_w, ())

        @pl.when(c + 1 < early)
        def _():
            chunk_load(c + 1).start()

        @pl.when(c >= early)
        def _():
            e = c - early
            pltpu.make_async_copy(z_far.at[0], piece(e, spread.place, None), keep_sems.at[e]).wait()
            spread.complete(e)
            take(land, (e,))

        cols = pl.ds(pl.multiple_of(lax.rem(c, units) * UNIT, UNIT), UNIT)
        unit(smalls_ref[source_of(c), 2:3, cols], None)
        serve(c + units + 1)
        reduce(c + units + 1)
        return carry

    lax.fori_loop(0, chunks, foreign_unit, 0)

    def tile_stores(i):
        rows = pl.ds(pl.multiple_of(i * TILE, TILE), TILE)
        return [
            pltpu.make_async_copy(source, target, tile_sems.at[i, k])
            for k, (source, target) in enumerate((
                (h2_ref.at[rows, :], result_out.at[rows, :]),
                (hg_ref.at[rows, :], mg_out.at[rows, :]),
                (dt_ref.at[:, rows], dt_out.at[:, rows]),
            ))
        ]

    def finish(i, carry):
        rows = pl.ds(pl.multiple_of(i * TILE, TILE), TILE)
        g = g_ref[rows, :].astype(F32)
        h2_ref[rows, :] = res_ref[rows, :].astype(BF)
        normed, inv_std = standardize(mixed_ref[rows, :])
        hg = hg_ref[rows, :]
        mg = g + norm_back(hg, normed, inv_std, gain_ref[1:2, :])
        hg_ref[rows, :] = mg
        low = mg.astype(BF)
        dt_ref[:, rows] = dot(wo_ref[...], low, NT).astype(BF)
        tail_ref[:own, :] += dot(mine_ref[:, rows], low, NN)
        for at, value in ((GAIN_TWO, hg * normed), (SHIFT_TWO, hg), (BIAS_ONE, mg), (BIAS_TWO, g)):
            tail_ref[own + at : own + at + 1, :] += jnp.sum(value, 0, keepdims=True)
        for copy in tile_stores(i):
            copy.start()
        return carry

    lax.fori_loop(0, tiles, finish, 0)
    total.finish(2)
    ends = [
        pltpu.make_async_copy(total.rows(at, total.piece), main_out.at[pl.ds(pl.multiple_of(at, 8), total.piece), :], sem)
        for at, sem in ((total.one_piece, out_sems.at[0]), (total.two_piece, out_sems.at[1]))
    ]
    ends.append(pltpu.make_async_copy(tail_ref, tail_out, out_sems.at[2]))
    for copy in ends:
        copy.start()
    for e in range(late):
        spread.sent(e)

    @pl.when(inner)
    def _():
        for u in range(units):
            far_copy(u).wait_send()

    def drain(i, carry):
        for copy in tile_stores(i):
            copy.wait()
        return carry

    lax.fori_loop(0, tiles, drain, 0)
    for copy in ends:
        copy.wait()


def mlp(x, ot, wo, g, up, down, smalls, biases, gains, shifts, land, z):
    tokens, width = x.shape
    parts = smalls.shape[0]
    own = width // parts
    ff = up.shape[1]
    units = ff // UNIT
    chunks = units * (parts - 1)
    late = chunks - land.shape[0]
    tiles = tokens // TILE
    rows = 2 * ff
    tail = own + 64
    dma = pltpu.SemaphoreType.DMA
    return pl.pallas_call(
        mlp_kernel,
        in_specs=[WHOLE] * 5 + [ANY] * 7,
        out_specs=[ANY] * 5,
        out_shape=[
            shape_of((tokens, width), BF),
            shape_of((tokens, width), F32),
            shape_of((width, tokens), BF),
            shape_of((rows, width), F32),
            shape_of((tail, width), F32),
        ],
        scratch_shapes=[
            pltpu.VMEM((late, 2, width, UNIT), F32),
            pltpu.VMEM((units, 2, width // 8, UNIT), F32),
            pltpu.VMEM((2, width, UNIT), F32),
            pltpu.VMEM((UNIT, width), F32),
            pltpu.VMEM((tokens, width), BF),
            pltpu.VMEM((tokens, width), BF),
            pltpu.VMEM((width, tokens), BF),
            pltpu.VMEM((own, tokens), BF),
            pltpu.VMEM((rows, width), F32),
            pltpu.VMEM((tail, width), F32),
            pltpu.VMEM((tokens, width), F32),
            pltpu.VMEM((tokens, width), F32),
            pltpu.VMEM((tokens, width), F32),
            pltpu.VMEM((width, UNIT), BF),
            pltpu.VMEM((UNIT, width), BF),
            pltpu.VMEM((2, TILE, UNIT), F32),
            pltpu.VMEM((2, TILE, UNIT), F32),
            dma((3,)),
            dma((2,)),
            dma((late,)),
            dma((units,)),
            dma((units,)),
            dma((units,)),
            dma((3,)),
            dma((tiles, 3)),
            dma((late, 9)),
            dma((late, 9)),
        ]
        + Total.scratch(rows, width),
        compiler_params=pltpu.CompilerParams(vmem_limit_bytes=63 * 2**20, collective_id=1, has_side_effects=True),
        name="mlp",
    )(wo, smalls, biases, gains, shifts, x, ot, g, up, down, land, z)


def body(
    dp_size,
    tokens,
    segments,
    norm_gains,
    norm_shifts,
    qkv_weight,
    qv_bias,
    out_weight,
    out_biases,
    up_weight,
    up_bias,
    down_weight,
    cotangent,
):
    width = tokens.shape[1]
    own = qkv_weight.shape[2]
    ff = up_weight.shape[1]
    smalls, bound, h1, weights, wo, qkvt, ot, lse, land, z = front(
        tokens, segments, norm_gains, norm_shifts, qkv_weight.transpose(0, 2, 1).reshape(3 * own, width), out_weight,
        qv_bias, up_bias, up_weight, down_weight,
    )
    ot, lse = repair(bound, segments, qkvt, ot, lse)
    result, mg, dt, main, tail = mlp(
        tokens, ot, wo, cotangent, up_weight, down_weight, smalls, out_biases, norm_gains, norm_shifts, land, z
    )
    dqkv, main, rest = attend_back(segments, qkvt, ot, dt, lse, h1, main, tail)
    if dp_size > 8:
        main, rest = (value / 8 for value in lax.psum((main, rest), "dp"))
    token_grad, sums_one, down_grad, up_grad, out_weight_grad, result, qkv_grad = token_back(
        dqkv, weights, tokens, mg, norm_gains, main, rest, result, ff, own
    )
    if dp_size > 8:
        sums_one = lax.psum(sums_one, "dp")
    gains_grad, shifts_grad, out_biases_grad, qv_bias_grad, up_bias_grad = add_sums(sums_one, rest, own, dp_size == 8)
    return (
        result,
        token_grad,
        gains_grad,
        shifts_grad,
        qkv_grad.reshape(3, own, width).transpose(0, 2, 1),
        qv_bias_grad,
        out_weight_grad,
        out_biases_grad,
        up_grad,
        up_bias_grad.reshape(ff),
        down_grad,
    )


def solution(mesh):
    in_specs = (
        P("dp", None),
        P("dp", None),
        P(),
        P(),
        P(None, None, "mp"),
        P(None, "mp"),
        P("mp", None),
        P(),
        P(None, "mp"),
        P("mp"),
        P("mp", None),
        P("dp", None),
    )
    out_specs = (
        P("dp", None),
        P("dp", None),
        P(),
        P(),
        P(None, None, "mp"),
        P(None, "mp"),
        P("mp", None),
        P(),
        P(None, "mp"),
        P("mp"),
        P("mp", None),
    )
    return jax.shard_map(
        partial(body, mesh.shape["dp"]), mesh=mesh, in_specs=in_specs, out_specs=out_specs, check_vma=False
    )
```

```python
from functools import partial

import jax
import jax.numpy as jnp
from jax import lax
from jax.experimental import pallas as pl
from jax.experimental.pallas import tpu as pltpu
from jax.sharding import PartitionSpec as P

F32 = jnp.float32
BF = jnp.bfloat16
HEAD_DIM = 64
NORM_EPSILON = 1e-06
BIG = 1e30
LOG2E = 1.4426950408889634
SAFE_SCORE = 60.0
REACH = 512
TILE = 256
LONG_TILE = 512
EXTRA = 16
UNIT = 256
EARLY = 1

NN = (((1,), (0,)), ((), ()))
NT = (((1,), (1,)), ((), ()))
TN = (((0,), (0,)), ((), ()))
WHOLE = pl.BlockSpec(memory_space=pltpu.VMEM)
ONCE = pl.BlockSpec(memory_space=pltpu.VMEM, pipeline_mode=pl.Buffered(1))
ANY = pl.BlockSpec(memory_space=pl.ANY)


def dot(left, right, dims):
    return lax.dot_general(left, right, dims, preferred_element_type=F32)


def params(mib=56):
    return pltpu.CompilerParams(vmem_limit_bytes=mib * 2**20)


def standardize(values):
    centered = values - jnp.mean(values, -1, keepdims=True)
    inv_std = lax.rsqrt(jnp.mean(centered * centered, -1, keepdims=True) + NORM_EPSILON)
    return centered * inv_std, inv_std


def norm_back(grad_in, normed, inv_std, gain):
    scaled = grad_in * gain
    return inv_std * (
        scaled
        - jnp.mean(scaled, -1, keepdims=True)
        - normed * jnp.mean(scaled * normed, -1, keepdims=True)
    )


def shape_of(shape, dtype):
    return jax.ShapeDtypeStruct(shape, dtype)


def flip(index, bit):
    return index + bit - 2 * bit * lax.rem(lax.div(index, bit), 2)


def remote(src, dst, send_sem, recv_sem, **where):
    return pltpu.make_async_remote_copy(
        src_ref=src, dst_ref=dst, send_sem=send_sem, recv_sem=recv_sem, device_id=where,
        device_id_type=pl.DeviceIdType.MESH,
    )


SIDE, ACROSS, DIAG_A, DIAG_B, CORE = range(5)
NEAR, CORNER, OTHER = range(3)


def position(device):
    place = lax.rem(device, 8)
    return lax.rem(place, 2) * 4 + lax.div(place, 2)


class Spread:
    def __init__(self, pieces, send_sems, recv_sems, mine=None):
        self.pieces, self.send_sems, self.recv_sems, self.mine = pieces, send_sems, recv_sems, mine
        self.device = lax.axis_index("dp")
        self.at = position(self.device)
        self.side, self.across = flip(self.at, 1), flip(self.at, 2)
        self.corner_at = flip(self.side, 2)
        self.core = lax.div(self.at, 4) * 4

    def copy(self, chunk, kind, src=None):
        at, count, half, bit, arrival = {
            SIDE: (self.at, 1, None, 2, NEAR),
            ACROSS: (self.at, 1, None, 4, NEAR),
            DIAG_A: (self.side, 1, 0, 4, CORNER),
            DIAG_B: (self.across, 1, 1, 2, CORNER),
            CORE: (self.core, 4, None, 1, OTHER),
        }[kind]
        dst = self.pieces(chunk, at, count, half)
        return remote(
            dst if src is None else src, dst, self.send_sems.at[chunk], self.recv_sems.at[chunk, arrival],
            dp=flip(self.device, bit),
        )

    def arrived(self, chunk, arrival, count):
        ref = self.pieces(chunk, 0, count, None)
        remote(ref, ref, self.send_sems.at[chunk], self.recv_sems.at[chunk, arrival], dp=self.device).wait_recv()

    def send(self, chunk):
        src = None if self.mine is None else self.mine(chunk)
        for kind in (SIDE, ACROSS):
            self.copy(chunk, kind, src).start()

    def forward(self, chunk):
        self.arrived(chunk, NEAR, 2)
        for kind in (DIAG_A, DIAG_B):
            self.copy(chunk, kind).start()

    def corner(self, chunk):
        self.arrived(chunk, CORNER, 1)
        self.copy(chunk, CORE).start()

    def complete(self, chunk):
        self.arrived(chunk, OTHER, 4)

    def sent(self, chunk):
        ref = self.pieces(chunk, 0, 7, None)
        remote(ref, ref, self.send_sems.at[chunk], self.recv_sems.at[chunk, 0], dp=self.device).wait_send()


def greet(*peers):
    barrier = pltpu.get_barrier_semaphore()
    for peer in peers:
        pl.semaphore_signal(barrier, inc=1, device_id=peer, device_id_type=pl.DeviceIdType.MESH)
    pl.semaphore_wait(barrier, len(peers))


def foreign_order(me):
    half = lax.div(me, 2)
    return flip(me, 1), 2 - half, 3 - 3 * half


def front_kernel(
    gain_ref, shift_ref, qkv_ref, out_ref, qv_bias_ref, up_bias_ref, seg_ref, x_any, up_any, down_any,
    smalls_ref, bound_ref, h1_out, w_out, wo_out, qkvt_out, ot_out, lse_out, land_out, z_out,
    x_in, h1_ref, land, wo_land, z_land, mlp_land, pieces, small_land, w_low, wo_low, bias_col,
    qkvt_ref, ot_ref, lse_ref, qx, kx, vx, kn,
    x_sem, piece_sem, keep_sems, out_sems, slice_sems, z_send, z_recv, own_send, small_send, small_recv,
    send_sems, recv_sems,
):
    parts, rows, width = land.shape
    own = out_ref.shape[0]
    heads = own // HEAD_DIM
    tokens = x_in.shape[0]
    length = seg_ref.shape[1]
    units = pieces.shape[0]
    items = 3 + units
    early = mlp_land.shape[0]
    share, out_share, mlp_share = rows // 8, own // 8, width // 8
    split = (0, share // 16 * 8 + 8, share)
    strip = UNIT // 8
    me = lax.axis_index("mp")
    device = lax.axis_index("dp")
    order = foreign_order(me)
    out_chunk, mlp_chunk = 2 * (parts - 1), 3 * (parts - 1)

    def some_rows(start, size, at, count, half):
        low, high = 0, count * size
        if half is not None:
            middle = (size + 8) // 16 * 8
            low, high = (0, middle) if half == 0 else (middle, size)
        return pl.ds(pl.multiple_of(start + at * size + low, 8), high - low)

    def slab_rows(h, at, count=1, half=None):
        return some_rows(split[h] * 8, split[h + 1] - split[h], at, count, half)

    def out_rows(at, count=1, half=None):
        return some_rows(0, out_share, at, count, half)

    def pieces_at(c, at, count, half):
        if c < out_chunk:
            return land.at[order[c // 2], slab_rows(c % 2, at, count, half), :]
        if c < mlp_chunk:
            return wo_land.at[order[c - out_chunk], out_rows(at, count, half), :]
        rows = some_rows(0, mlp_share, at, count, None)
        if half is None:
            return mlp_land.at[c - mlp_chunk, :, rows, :]
        return mlp_land.at[c - mlp_chunk, half, rows, :]

    place = position(device)

    def mine(c):
        if c < mlp_chunk:
            return pieces_at(c, place, 1, None)
        return z_land.at[order[(c - mlp_chunk) // units], (c - mlp_chunk) % units]

    spread = Spread(pieces_at, send_sems, recv_sems, mine)

    def hop_ref(source, item):
        if item < 2:
            return land.at[source, slab_rows(item, place), :]
        if item == 2:
            return wo_land.at[source, out_rows(place), :]
        return z_land.at[source, item - 3]

    def own_ref(item):
        if item < 2:
            return qkv_ref.at[slab_rows(item, place), :]
        if item == 2:
            return out_ref.at[out_rows(place), :]
        return pieces.at[item - 3]

    def own_copies(item, act):
        def copy(up):
            return remote(
                own_ref(item), hop_ref(me, item), own_send.at[item, up], z_recv.at[me, item], mp=me + 2 * up - 1
            )

        @pl.when(me < parts - 1)
        def _():
            act(copy(1))

        @pl.when(me > 0)
        def _():
            act(copy(0))

    def pass_on(j, item, act):
        source = order[j]
        ref = hop_ref(source, item)

        def copy(step):
            return remote(ref, ref, z_send.at[source, item], z_recv.at[source, item], mp=me + step)

        end = 0 if item < 3 else 1

        @pl.when((source < me) & (me < parts - 1 - end))
        def _():
            act(copy(1))

        @pl.when((source > me) & (me > end))
        def _():
            act(copy(-1))

    def landed(j, item):
        ref = hop_ref(order[j], item)
        remote(ref, ref, z_send.at[order[j], item], z_recv.at[order[j], item], mp=me).wait_recv()
        pass_on(j, item, lambda copy: copy.start())
        if item >= 3 and j * units + item - 3 < early:
            keep(j * units + item - 3).start()

    inner = (me > 0) & (me < parts - 1)

    def landings(inner_items, outer_items):
        @pl.when(inner)
        def _():
            for j, item in inner_items:
                landed(j, item)

        @pl.when(jnp.logical_not(inner))
        def _():
            for j, item in outer_items:
                landed(j, item)

    def keep(c):
        return pltpu.make_async_copy(
            mine(mlp_chunk + c), pieces_at(mlp_chunk + c, place, 1, None), keep_sems.at[c]
        )

    def small_copy(s):
        ref = small_land.at[me]
        return remote(ref, ref, small_send.at[s - 1], small_recv.at[me], mp=lax.rem(me + s, parts))

    def at_place(at, ref):
        w_low[at] = ref[...].astype(BF)

    def slice_stores(at):
        rows_at = pl.ds(pl.multiple_of(at * rows, rows), rows)
        own_at = pl.ds(pl.multiple_of(at * own, own), own)
        return [
            pltpu.make_async_copy(w_low.at[at], w_out.at[rows_at, :], slice_sems.at[at, 0]),
            pltpu.make_async_copy(qkvt_ref.at[rows_at, :], qkvt_out.at[rows_at, :], slice_sems.at[at, 1]),
            pltpu.make_async_copy(ot_ref.at[own_at, :], ot_out.at[own_at, :], slice_sems.at[at, 2]),
        ]

    x_copy = pltpu.make_async_copy(x_any, x_in, x_sem)
    h1_copy = pltpu.make_async_copy(h1_ref, h1_out, out_sems.at[0])
    lse_copy = pltpu.make_async_copy(lse_ref, lse_out, out_sems.at[1])
    wo_copy = pltpu.make_async_copy(wo_low, wo_out, out_sems.at[2])
    z_copy = pltpu.make_async_copy(z_land, z_out, out_sems.at[3])
    land_copy = pltpu.make_async_copy(mlp_land, land_out, out_sems.at[4])

    x_copy.start()
    copies = []
    for u in range(units):
        at = pl.ds(pl.multiple_of(place * mlp_share, 8), mlp_share)
        copies.append((up_any.at[at, pl.ds(u * UNIT, UNIT)], pieces.at[u, 0]))
        for c in range(width // UNIT):
            at = pl.ds(pl.multiple_of(u * UNIT + place * strip, 8), strip)
            copies.append((down_any.at[at, pl.ds(c * UNIT, UNIT)], pieces.at[u, 1, pl.ds(c * strip, strip), :]))
    for source, target in copies:
        pltpu.make_async_copy(source, target, piece_sem).start()
    greet(
        *[{"mp": lax.rem(me + s, parts)} for s in range(1, parts)],
        *[{"dp": flip(device, bit)} for bit in (1, 2, 4)],
    )
    for item in range(2):
        own_copies(item, lambda copy: copy.start())
    small_land[me] = jnp.zeros(small_land.shape[1:], F32)
    small_land[me, 0:2, :own] = qv_bias_ref[...]
    small_land[me, 2:3, :] = up_bias_ref[...].reshape(1, width)
    for s in range(1, parts):
        small_copy(s).start()
    own_copies(2, lambda copy: copy.start())
    bound_ref[...] = jnp.zeros_like(bound_ref)
    bias_col[...] = jnp.zeros_like(bias_col)
    lse_ref[...] = jnp.zeros_like(lse_ref)
    z_land[me] = jnp.zeros(z_land.shape[1:], F32)

    @pl.when(jnp.logical_not(inner))
    def _():
        for source in order[1:]:
            z_land[source] = jnp.zeros(z_land.shape[1:], F32)

    for j in range(2):
        bias_col[0, 2 * j * own : (2 * j + 1) * own, :] = small_land[me].T[:own, j : j + 1]
    at_place(0, qkv_ref)
    wo_low[:own, :] = out_ref[...].astype(BF)
    x_copy.wait()

    def norm_tile(i, carry):
        at = pl.ds(pl.multiple_of(i * TILE, TILE), TILE)
        normed, _ = standardize(x_in[at, :].astype(F32))
        h1_ref[at, :] = (normed * gain_ref[0:1, :] + shift_ref[0:1, :]).astype(BF)
        return carry

    lax.fori_loop(0, tokens // TILE, norm_tile, 0)
    h1_copy.start()
    row = lax.broadcasted_iota(jnp.int32, (EXTRA, length), 0)
    for u in range(heads):
        vx[u, HEAD_DIM:, :] = jnp.ones((EXTRA, length), BF)

    def norm_bound(ref, u):
        value = ref[u, :HEAD_DIM, :].astype(F32)
        return jnp.max(jnp.sum(value * value, 0, keepdims=True), 1, keepdims=True)

    def project(at, r):
        tokens_r = pl.ds(pl.multiple_of(r * length, length), length)
        base = at * rows
        value = dot(w_low[at], h1_ref[tokens_r, :], NT) + bias_col[at]
        scale = HEAD_DIM**-0.5
        qkvt_ref[pl.ds(pl.multiple_of(base, own), own), tokens_r] = value[:own].astype(BF) * jnp.asarray(scale, BF)
        qkvt_ref[pl.ds(pl.multiple_of(base + own, own), 2 * own), tokens_r] = value[own:].astype(BF)

    def attend(at, r):
        tokens_r = pl.ds(pl.multiple_of(r * length, length), length)
        base = at * rows
        same = row == seg_ref[pl.ds(r, 1), :]
        for u in range(heads):
            qx[u, HEAD_DIM:, :] = jnp.where(same | (row >= 8), 0.0, -BIG).astype(BF)
            kx[u, HEAD_DIM:, :] = jnp.where(same, 1.0, 0.0).astype(BF)
        for u in range(heads):
            for k, ref in enumerate((qx, kx, vx)):
                from_row = pl.multiple_of(base + k * own + u * HEAD_DIM, HEAD_DIM)
                ref[u, :HEAD_DIM, :] = qkvt_ref[pl.ds(from_row, HEAD_DIM), tokens_r]
            kn[u] = kx[u].T
            bound_ref[...] = jnp.maximum(bound_ref[...], norm_bound(qx, u) * norm_bound(kx, u))
            to_row = pl.ds(pl.multiple_of(at * own + u * HEAD_DIM, HEAD_DIM), HEAD_DIM)
            for t in range(length // TILE):
                low, high = max(0, t * TILE - REACH), min(length, (t + 1) * TILE + REACH)
                cols = slice(t * TILE, (t + 1) * TILE)
                to_cols = pl.ds(pl.multiple_of(r * length + t * TILE, TILE), TILE)
                probs = [
                    jnp.exp2(dot(kn[u, k : k + TILE, :], qx[u, :, cols], NN) * LOG2E).astype(BF)
                    for k in range(low, high, TILE)
                ]
                out = dot(vx[u, :, low:high], jnp.concatenate(probs, 0), NN)
                total = out[HEAD_DIM : HEAD_DIM + 1, :]
                ot_ref[to_row, to_cols] = (out[:HEAD_DIM, :] * (1.0 / total)).astype(BF)
                lse_ref[pl.ds(at * heads + u, 1), to_cols] = jnp.log(total)

    w, m = out_chunk, mlp_chunk

    def event(n):
        if n == 0:
            landings(((0, 0), (1, 0)), ((0, 0),))
            spread.send(0)
            landings(((0, 1), (1, 1)), ((0, 1),))
            spread.send(1)
        if n == 1:
            spread.forward(0)
            spread.forward(1)
            landings(((2, 0),), ((1, 0),))
            spread.send(2)
        if n == 1.5:
            landings(((2, 1),), ((1, 1),))
            spread.send(3)
        if n == 2:
            spread.corner(0)
            spread.corner(1)
            spread.forward(2)
            landings(((0, 2), (1, 2)), ((2, 0),))
            spread.send(4)
            pltpu.make_async_copy(pieces, pieces, piece_sem).wait()
            own_copies(3, lambda copy: copy.start())
            for s in range(1, parts):
                ref = small_land.at[lax.rem(me + s, parts)]
                remote(ref, ref, small_send.at[0], small_recv.at[lax.rem(me + s, parts)], mp=me).wait_recv()
            smalls_ref[...] = small_land[...]
            for j, source in enumerate(order):
                cols = small_land[source].T
                for k in range(2):
                    bias_col[1 + j, 2 * k * own : (2 * k + 1) * own, :] = cols[:own, k : k + 1]
            spread.complete(0)
            spread.complete(1)
            at_place(1, land.at[order[0]])
        if n == 2.5:
            landings((), ((2, 1),))
            spread.send(5)
            spread.forward(3)
        if n == 3:
            spread.corner(2)
            spread.corner(3)
            spread.forward(4)
            landings(((2, 2),), ((0, 2),))
            spread.send(w)
            own_copies(4, lambda copy: copy.start())
        if n == 3.5:
            spread.forward(5)
        if n == 4:
            landings(((0, 3), (1, 3)), ((1, 2), (0, 3)))
            spread.send(w + 1)
            own_copies(5, lambda copy: copy.start())
            spread.corner(4)
            spread.corner(5)
            spread.forward(w)
            spread.complete(2)
            spread.complete(3)
            at_place(2, land.at[order[1]])
        if n == 5:
            landings(((0, 4), (1, 4)), ((2, 2), (0, 4)))
            spread.send(w + 2)
            for c in range(early):
                spread.send(m + c)
            spread.corner(w)
            spread.forward(w + 1)
        if n == 6:
            landings(((0, 5), (1, 5), (2, 3)), ((0, 5),))
            spread.forward(w + 2)
            spread.corner(w + 1)
            for c in range(early):
                spread.forward(m + c)
            spread.complete(4)
            spread.complete(5)
            at_place(3, land.at[order[2]])
        if n == 7:
            landings(((2, 4),), ())
            spread.corner(w + 2)
            for c in range(early):
                keep(c).wait()
                spread.corner(m + c)
            spread.complete(w)
        if n == 8:
            landings(((2, 5),), ())
            z_copy.start()
            spread.complete(w + 1)
            spread.complete(w + 2)
            for c in range(early):
                spread.complete(m + c)
            land_copy.start()
            for j in range(parts - 1):
                wo_low[(j + 1) * own : (j + 2) * own, :] = wo_land[order[j]].astype(BF)
            wo_copy.start()
            lse_copy.start()

    event(0)

    def step(n, carry):
        at, r = lax.div(n, 2), lax.rem(n, 2)
        project(at, r)
        for e in (1, 2, 3):
            @pl.when(n == e)
            def _():
                event(e + 0.5)

        attend(at, r)

        @pl.when(r == 1)
        def _():
            for copy in slice_stores(at):
                copy.start()

        for e in range(1, 9):
            @pl.when(n + 1 == e)
            def _():
                event(e)

        return carry

    lax.fori_loop(0, 2 * parts, step, 0)
    for c in range(mlp_chunk + early):
        spread.sent(c)
    for item in range(items):
        own_copies(item, lambda copy: copy.wait_send())
        for j in range(parts - 1):
            pass_on(j, item, lambda copy: copy.wait_send())
    for s in range(1, parts):
        small_copy(s).wait_send()
    for copy in (h1_copy, lse_copy, wo_copy, z_copy, land_copy):
        copy.wait()
    for at in range(parts):
        for copy in slice_stores(at):
            copy.wait()


def front(x, seg, gains, shifts, qkv, out, qv_bias, up_bias, up, down):
    tokens, width = x.shape
    length = seg.shape[1]
    rows = qkv.shape[0]
    own = out.shape[0]
    parts = width // own
    heads = own // HEAD_DIM
    units = up.shape[1] // UNIT
    chunks = 3 * (parts - 1) + EARLY
    wide = HEAD_DIM + EXTRA
    dma = pltpu.SemaphoreType.DMA
    return pl.pallas_call(
        front_kernel,
        in_specs=[WHOLE] * 7 + [ANY] * 3,
        out_specs=[WHOLE] * 2 + [ANY] * 8,
        out_shape=[
            shape_of((parts, 8, width), F32),
            shape_of((8, 128), F32),
            shape_of((tokens, width), BF),
            shape_of((parts * rows, width), BF),
            shape_of((width, width), BF),
            shape_of((parts * rows, tokens), BF),
            shape_of((width, tokens), BF),
            shape_of((16, tokens), F32),
            shape_of((EARLY, 2, width, UNIT), F32),
            shape_of((parts, units, 2, width // 8, UNIT), F32),
        ],
        scratch_shapes=[
            pltpu.VMEM((tokens, width), BF),
            pltpu.VMEM((tokens, width), BF),
            pltpu.VMEM((parts, rows, width), F32),
            pltpu.VMEM((parts, own, width), F32),
            pltpu.VMEM((parts, units, 2, width // 8, UNIT), F32),
            pltpu.VMEM((EARLY, 2, width, UNIT), F32),
            pltpu.VMEM((units, 2, width // 8, UNIT), F32),
            pltpu.VMEM((parts, 8, width), F32),
            pltpu.VMEM((parts, rows, width), BF),
            pltpu.VMEM((width, width), BF),
            pltpu.VMEM((parts, rows, 1), F32),
            pltpu.VMEM((parts * rows, tokens), BF),
            pltpu.VMEM((width, tokens), BF),
            pltpu.VMEM((16, tokens), F32),
            pltpu.VMEM((heads, wide, length), BF),
            pltpu.VMEM((heads, wide, length), BF),
            pltpu.VMEM((heads, wide, length), BF),
            pltpu.VMEM((heads, length, wide), BF),
            dma,
            dma,
            dma((EARLY,)),
            dma((5,)),
            dma((parts, 3)),
            dma((parts, 3 + units)),
            dma((parts, 3 + units)),
            dma((3 + units, 2)),
            dma((parts - 1,)),
            dma((parts,)),
            dma((chunks,)),
            dma((chunks, 3)),
        ],
        compiler_params=pltpu.CompilerParams(vmem_limit_bytes=62 * 2**20, collective_id=0, has_side_effects=True),
        name="front",
    )(gains, shifts, qkv, out, qv_bias, up_bias, seg, x, up, down)


def repair_kernel(
    bound_ref, seg_ref, qkvt_any, ot_in, lse_in, ot_out, lse_out, qx, kx, vx, lse_row, sems,
):
    rows_here, length = seg_ref.shape
    parts = 4
    own = qkvt_any.shape[0] // (3 * parts)
    heads = parts * own // HEAD_DIM
    safe = jnp.max(bound_ref[...]) < SAFE_SCORE**2

    @pl.when(jnp.logical_not(safe))
    def _():
        row = lax.broadcasted_iota(jnp.int32, (EXTRA, length), 0)
        vx[HEAD_DIM:, :] = jnp.ones((EXTRA, length), BF)

        def move(copies):
            copies = [pltpu.make_async_copy(a, b, sems.at[i]) for i, (a, b) in enumerate(copies)]
            for copy in copies:
                copy.start()
            for copy in copies:
                copy.wait()

        def head(i, carry):
            r, h = lax.div(i, heads), lax.rem(i, heads)
            rows = pl.ds(pl.multiple_of(h * HEAD_DIM, HEAD_DIM), HEAD_DIM)
            tokens = pl.ds(pl.multiple_of(r * length, length), length)
            head_at = lax.div(h, heads // parts) * 3 * own + lax.rem(h, heads // parts) * HEAD_DIM
            same = row == seg_ref[pl.ds(r, 1), :]
            qx[HEAD_DIM:, :] = jnp.where(same | (row >= 8), 0.0, -BIG).astype(BF)
            kx[HEAD_DIM:, :] = jnp.where(same, 1.0, 0.0).astype(BF)
            move([
                (
                    qkvt_any.at[pl.ds(pl.multiple_of(head_at + k * own, HEAD_DIM), HEAD_DIM), tokens],
                    target.at[pl.ds(0, HEAD_DIM), :],
                )
                for k, target in enumerate((qx, kx, vx))
            ])

            @pl.when(h == 0)
            def _():
                lse_row[...] = jnp.zeros_like(lse_row)

            for t in range(length // TILE):
                cols = slice(t * TILE, (t + 1) * TILE)
                scores = dot(kx[...], qx[:, cols], TN)
                highest = jnp.max(scores, 0, keepdims=True)
                probs = jnp.exp2((scores - highest) * LOG2E).astype(BF)
                out = dot(vx[...], probs, NN)
                total = out[HEAD_DIM : HEAD_DIM + 1, :]
                qx[:HEAD_DIM, cols] = (out[:HEAD_DIM, :] * (1.0 / total)).astype(BF)
                lse_row[pl.ds(h, 1), cols] = jnp.log(total) + highest
            move([(qx.at[pl.ds(0, HEAD_DIM), :], ot_out.at[rows, tokens])])

            @pl.when(h == heads - 1)
            def _():
                move([(lse_row, lse_out.at[:, tokens])])

            return carry

        lax.fori_loop(0, rows_here * heads, head, 0)


def repair(bound, seg, qkvt, ot, lse):
    length = seg.shape[1]
    return pl.pallas_call(
        repair_kernel,
        in_specs=[WHOLE, WHOLE, ANY, ANY, ANY],
        out_specs=[ANY, ANY],
        out_shape=[shape_of(ot.shape, BF), shape_of(lse.shape, F32)],
        input_output_aliases={3: 0, 4: 1},
        scratch_shapes=[pltpu.VMEM((HEAD_DIM + EXTRA, length), BF)] * 3
        + [pltpu.VMEM((16, length), F32), pltpu.SemaphoreType.DMA((3,))],
        compiler_params=params(),
        name="repair",
    )(bound, seg, qkvt, ot, lse)


def split3(value):
    first = value.astype(BF)
    rest = value - first.astype(F32)
    second = rest.astype(BF)
    return first, second, (rest - second.astype(F32)).astype(BF)


class Total:
    def __init__(self, out, sends, recvs, near=None, side_land=None, across_land=None):
        self.out, self.near = out, near
        self.side_land, self.across_land, self.sends, self.recvs = side_land, across_land, sends, recvs
        self.device = lax.axis_index("dp")
        place = lax.rem(self.device, 8)
        self.half = out.shape[0] // 2
        self.part, self.piece = self.half // 4, self.half // 8
        bits = [lax.rem(lax.div(place, bit), 2) for bit in (1, 2, 4)]
        self.base = bits[0] * self.half
        self.away = (1 - bits[0]) * self.half
        self.one = self.base + bits[1] * self.part
        self.one_away = self.base + (1 - bits[1]) * self.part
        self.two = self.base + 2 * self.part + bits[2] * self.part
        self.two_away = self.base + 2 * self.part + (1 - bits[2]) * self.part
        self.one_piece = self.one + bits[2] * self.piece
        self.one_piece_away = self.one + (1 - bits[2]) * self.piece
        self.two_piece = self.two + bits[1] * self.piece
        self.two_piece_away = self.two + (1 - bits[1]) * self.piece

    def rows(self, start, count):
        return self.out.at[pl.ds(pl.multiple_of(start, 8), count), :]

    def copy(self, sem, bit, src, dst):
        return remote(src, dst, self.sends.at[sem], self.recvs.at[sem], dp=flip(self.device, bit))

    def over(self, sem, bit, start, count):
        ref = self.rows(start, count)
        return self.copy(sem, bit, ref, ref)

    def copies(self, stage):
        part, piece = self.part, self.piece
        first, second = pl.ds(0, part), pl.ds(part, piece)
        if stage == 0:
            return [self.copy(0, 1, self.rows(self.away, self.half), self.near)]
        if stage == 1:
            return [
                self.copy(1, 2, self.rows(self.one_away, part), self.side_land.at[first, :]),
                self.copy(2, 4, self.rows(self.two_away, part), self.across_land.at[first, :]),
            ]
        if stage == 2:
            return [
                self.copy(3, 4, self.rows(self.one_piece_away, piece), self.across_land.at[second, :]),
                self.copy(4, 2, self.rows(self.two_piece_away, piece), self.side_land.at[second, :]),
            ]
        if stage == 3:
            return [self.over(5, 4, self.one_piece, piece), self.over(6, 2, self.two_piece, piece)]
        if stage == 4:
            return self.halves(0, self.one, self.two)
        if stage == 4.5:
            return self.halves(1, self.one, self.two)
        return [self.over(9, 1, self.base, self.half)]

    def halves(self, h, one, two):
        half = self.part // 2
        return [self.over(7 + 3 * h, 2, one + h * half, half), self.over(8 + 3 * h, 4, two + h * half, half)]

    def arrivals(self, stage):
        part, piece = self.part, self.piece
        if stage == 3:
            return [self.over(5, 4, self.one_piece_away, piece), self.over(6, 2, self.two_piece_away, piece)]
        if stage == 4:
            return self.halves(0, self.one_away, self.two_away)
        if stage == 4.5:
            return self.halves(1, self.one_away, self.two_away)
        if stage == 5:
            return [self.over(9, 1, self.away, self.half)]
        return self.copies(stage)

    def add(self, start, ref, at, count):
        step = 48 if count % 48 == 0 else 56

        def some(i, carry):
            rows = pl.ds(pl.multiple_of(start + i * step, 8), step)
            self.out[rows, :] += ref[pl.ds(pl.multiple_of(at + i * step, 8), step), :]
            return carry

        lax.fori_loop(0, count // step, some, 0)

    def finish(self, stage):
        for copy in self.copies(stage):
            copy.wait_send()
        for copy in self.arrivals(stage):
            copy.wait_recv()
        if stage == 0:
            self.add(self.base, self.near, 0, self.half)
        elif stage == 1:
            self.add(self.one, self.side_land, 0, self.part)
            self.add(self.two, self.across_land, 0, self.part)
        elif stage == 2:
            self.add(self.one_piece, self.across_land, self.part, self.piece)
            self.add(self.two_piece, self.side_land, self.part, self.piece)

    def start(self, stage):
        for copy in self.copies(stage):
            copy.start()

    @staticmethod
    def scratch(rows, width):
        dma = pltpu.SemaphoreType.DMA
        return [
            dma((12,)),
            dma((12,)),
            pltpu.VMEM((rows // 2, width), F32),
            pltpu.VMEM((rows // 8 + rows // 16, width), F32),
            pltpu.VMEM((rows // 8 + rows // 16, width), F32),
        ]


def attend_back_kernel(
    seg_ref, qkv_ref, ot_ref, dt_ref, lse_ref, h1_any, main_any, tail_any,
    dqkv_ref, main_out, rest_out,
    qx, kx, vx, dx, qn, dn, kn, acc, h1_ref, part_ref, main_ref, rest_ref, whole_ref, in_sems, out_sems, main_send, main_recv, side_land, across_land,
    *comm,
):
    step = pl.program_id(0)
    own, length = ot_ref.shape
    width = h1_ref.shape[1]
    heads = own // HEAD_DIM
    tail_at = rest_ref.shape[0] - tail_any.shape[0]
    part = Total(part_ref, main_send, main_recv, None, side_land, across_land)
    main = Total(main_ref, main_send, main_recv)
    rest = Total(rest_ref, *comm)
    whole = Total(whole_ref, *comm[:2])
    loads = [
        pltpu.make_async_copy(main_any.at[pl.ds(pl.multiple_of(at, 8), part.part), :], part.rows(at, part.part), sem)
        for at, sem in ((part.one, in_sems.at[0]), (part.two, in_sems.at[1]))
    ]
    loads.append(pltpu.make_async_copy(tail_any, rest_ref.at[pl.ds(tail_at, tail_any.shape[0]), :], in_sems.at[2]))
    loads.append(pltpu.make_async_copy(h1_any, h1_ref, in_sems.at[3]))
    stores = [
        pltpu.make_async_copy(main_ref, main_out, out_sems.at[0]),
        pltpu.make_async_copy(whole_ref, rest_out, out_sems.at[1]),
    ]

    @pl.when(step == 0)
    def _():
        for copy in loads:
            copy.start()
        greet(*[{"dp": flip(main.device, bit)} for bit in (1, 2, 4)])
        for copy in loads[:2]:
            copy.wait()
        part.start(2)

    @pl.when(step == 1)
    def _():
        part.finish(2)
        for at in (part.one_piece, part.two_piece):
            rows = pl.ds(pl.multiple_of(at, 8), part.piece)
            main_ref[rows, :] = part_ref[rows, :]
        main.start(3)

    @pl.when(step == 2)
    def _():
        main.finish(3)
        main.start(4)

    @pl.when(step == 3)
    def _():
        rest.finish(0)
        rest.start(1)

    @pl.when(step == 4)
    def _():
        rest.finish(1)
        rest.start(2)
        main.finish(4)
        main.start(4.5)

    @pl.when(step == 5)
    def _():
        rest.finish(2)
        for at in (rest.one_piece, rest.two_piece):
            rows = pl.ds(pl.multiple_of(at, 8), rest.piece)
            whole_ref[rows, :] = rest_ref[rows, :]
        whole.start(3)

    @pl.when(step == 6)
    def _():
        whole.finish(3)
        whole.start(4)
        whole.start(4.5)
        main.finish(4.5)
        main.start(5)

    @pl.when(step == 7)
    def _():
        whole.finish(4)
        whole.finish(4.5)
        whole.start(5)
        main.finish(5)
        stores[0].start()

    row = lax.broadcasted_iota(jnp.int32, (EXTRA, length), 0)
    same = row == seg_ref[pl.ds(jnp.where((step == 1) | (step >= 5), 1, 0), 1), :]
    key_extra = jnp.where(same | ((row >= 8) & (row < 11)), 1.0, 0.0).astype(BF)
    value_extra = jnp.where(row < 3, 1.0, 0.0).astype(BF)
    query_extra = jnp.where(same | (row >= 8), 0.0, -BIG)

    def three_rows(value, at):
        first, second, third = split3(value)
        out = jnp.where(row == at, first.astype(F32), 0.0)
        out = jnp.where(row == at + 1, second.astype(F32), out)
        return jnp.where(row == at + 2, third.astype(F32), out)

    head_at = jnp.where(step < 2, 0, lax.rem(step - 2, 3) + 1) * heads

    def head(u):
        rows = slice(u * HEAD_DIM, (u + 1) * HEAD_DIM)
        dq_rows, dk_rows, dv_rows = (slice(rows.start + k * own, rows.stop + k * own) for k in range(3))
        qx[u, :HEAD_DIM, :] = qkv_ref[dq_rows, :]
        kx[u, :HEAD_DIM, :] = qkv_ref[dk_rows, :]
        vx[u, :HEAD_DIM, :] = qkv_ref[dv_rows, :]
        dx[u, :HEAD_DIM, :] = dt_ref[rows, :]
        inner = jnp.sum(dt_ref[rows, :].astype(F32) * ot_ref[rows, :].astype(F32), 0, keepdims=True)
        log_sum = lse_ref[pl.ds(head_at + u, 1), :]
        qx[u, HEAD_DIM:, :] = (query_extra + three_rows(-log_sum, 8)).astype(BF)
        kx[u, HEAD_DIM:, :] = key_extra
        vx[u, HEAD_DIM:, :] = value_extra
        dx[u, HEAD_DIM:, :] = three_rows(-inner, 0).astype(BF)
        qn[u] = qx[u].T
        dn[u] = dx[u].T
        kn[u] = kx[u].T
        for t in range(length // TILE):
            low, high = max(0, t * TILE - REACH), min(length, (t + 1) * TILE + REACH)
            keys = slice(t * TILE, (t + 1) * TILE)
            probs, score_grads = [], []
            for q in range(low, high, TILE):
                prob = jnp.exp2(dot(qn[u, q : q + TILE, :], kx[u, :, keys], NN) * LOG2E)
                prob_grad = dot(dn[u, q : q + TILE, :], vx[u, :, keys], NN)
                probs.append(prob.astype(BF))
                score_grads.append((prob * prob_grad).astype(BF))
            probs = jnp.concatenate(probs, 0)
            score_grads = jnp.concatenate(score_grads, 0)
            dqkv_ref[dv_rows, keys] = dot(dx[u, :HEAD_DIM, low:high], probs, NN).astype(BF)
            dqkv_ref[dk_rows, keys] = dot(qx[u, :HEAD_DIM, low:high], score_grads, NN).astype(BF)
            part = dot(score_grads, kx[u, :HEAD_DIM, keys], NT)
            if t == 0:
                acc[u, low:high, :] = part
                if high < length:
                    acc[u, high:, :] = jnp.zeros((length - high, HEAD_DIM), F32)
            else:
                acc[u, low:high, :] += part
        dqkv_ref[dq_rows, :] = (acc[u] * HEAD_DIM**-0.5).T.astype(BF)

    for u in range(heads):
        head(u)

    def own_grads(tokens, add):
        part = dot(dqkv_ref[...], h1_ref[tokens, :], NN)
        rest_ref[: 3 * own, :] = rest_ref[: 3 * own, :] + part if add else part
        ones = jnp.ones((8, length), BF)
        for k in (0, 2):
            rows = slice(3 * own + k * 4, 3 * own + k * 4 + 8)
            part = dot(ones, dqkv_ref[k * own : (k + 1) * own, :], NT)
            rest_ref[rows, :own] = rest_ref[rows, :own] + part if add else part

    @pl.when(step == 0)
    def _():
        rest_ref[3 * own : tail_at, :] = jnp.zeros((tail_at - 3 * own, width), F32)
        loads[3].wait()
        own_grads(slice(0, length), False)

    @pl.when(step == 1)
    def _():
        own_grads(slice(length, 2 * length), True)
        loads[2].wait()
        rest.start(0)

    @pl.when(step == 7)
    def _():
        whole.finish(5)
        stores[1].start()
        for copy in stores:
            copy.wait()


def attend_back(seg, qkvt, ot, dt, lse, h1, main, tail):
    width, tokens = ot.shape
    _, length = seg.shape
    own = width // 4
    heads = own // HEAD_DIM
    wide = HEAD_DIM + EXTRA
    rest_rows = 3 * own + 64 + tail.shape[0]
    row_of = lambda s: jnp.where((s == 1) | (s >= 5), 1, 0)
    part_of = lambda s: jnp.where(s < 2, 0, lax.rem(s - 2, 3) + 1)
    block = pl.BlockSpec((own, length), lambda s: (part_of(s), row_of(s)))
    wide_block = pl.BlockSpec((3 * own, length), lambda s: (part_of(s), row_of(s)))
    dma = pltpu.SemaphoreType.DMA
    return pl.pallas_call(
        attend_back_kernel,
        grid=(8,),
        in_specs=[ONCE, wide_block, block, block]
        + [pl.BlockSpec((16, length), lambda s: (0, row_of(s))), ANY, ANY, ANY],
        out_specs=[wide_block, ANY, ANY],
        out_shape=[shape_of(qkvt.shape, BF), shape_of(main.shape, F32), shape_of((rest_rows, width), F32)],
        scratch_shapes=[pltpu.VMEM((heads, wide, length), BF)] * 4
        + [pltpu.VMEM((heads, length, wide), BF)] * 3
        + [
            pltpu.VMEM((heads, length, HEAD_DIM), F32),
            pltpu.VMEM((tokens, width), BF),
            pltpu.VMEM(main.shape, F32),
            pltpu.VMEM(main.shape, F32),
            pltpu.VMEM((rest_rows, width), F32),
            pltpu.VMEM((rest_rows, width), F32),
            dma((4,)),
            dma((2,)),
            dma((12,)),
            dma((12,)),
            pltpu.VMEM((main.shape[0] // 8 + main.shape[0] // 16, width), F32),
            pltpu.VMEM((main.shape[0] // 8 + main.shape[0] // 16, width), F32),
        ]
        + Total.scratch(rest_rows, width),
        compiler_params=pltpu.CompilerParams(vmem_limit_bytes=60 * 2**20, collective_id=2, has_side_effects=True),
        name="attend_back",
    )(seg, qkvt, ot, dt, lse, h1, main, tail)


def token_kernel(
    dqkv_ref, w_ref, x_ref, mg_ref, gain_ref, main_any, rest_any, result_any,
    tg_ref, sums_ref, down_ref, up_ref, out_ref, result_ref, qkv_ref,
    main_v, rest_v, result_v, in_sems, out_sems,
):
    step = pl.program_id(0)
    last = pl.num_programs(0) - 1
    ff = down_ref.shape[0]
    own = out_ref.shape[0]
    out_at = 3 * own + 64
    loads = [
        pltpu.make_async_copy(source, target, in_sems.at[i])
        for i, (source, target) in enumerate(((rest_any, rest_v), (main_any, main_v), (result_any, result_v)))
    ]
    stores = [
        pltpu.make_async_copy(source, target, out_sems.at[i])
        for i, (source, target) in enumerate((
            (main_v.at[pl.ds(0, ff), :], down_ref),
            (main_v.at[pl.ds(ff, up_ref.shape[0]), :], up_ref),
            (rest_v.at[pl.ds(out_at, own), :], out_ref),
            (result_v, result_ref),
            (rest_v.at[pl.ds(0, 3 * own), :], qkv_ref),
        ))
    ]

    @pl.when(step == 0)
    def _():
        for copy in loads:
            copy.start()
        sums_ref[...] = jnp.zeros_like(sums_ref)

    @pl.when(step == last - 1)
    def _():
        for copy in loads:
            copy.wait()
        for copy in stores:
            copy.start()

    hg = dot(dqkv_ref[...], w_ref[...], TN)
    normed, inv_std = standardize(x_ref[...].astype(F32))
    tg_ref[...] = mg_ref[...] + norm_back(hg, normed, inv_std, gain_ref[0:1, :])
    sums_ref[0:1, :] += jnp.sum(hg * normed, 0, keepdims=True)
    sums_ref[1:2, :] += jnp.sum(hg, 0, keepdims=True)

    @pl.when(step == last)
    def _():
        for copy in stores:
            copy.wait()


def token_back(dqkv, weights, x, mg, gains, main, rest, result, ff, own):
    tokens, width = x.shape
    row = pl.BlockSpec((LONG_TILE, width), lambda t: (t, 0))
    col = pl.BlockSpec((weights.shape[0], LONG_TILE), lambda t: (0, t))
    dma = pltpu.SemaphoreType.DMA
    return pl.pallas_call(
        token_kernel,
        grid=(tokens // LONG_TILE,),
        in_specs=[col, ONCE, row, row, ONCE, ANY, ANY, ANY],
        out_specs=[row, ONCE, ANY, ANY, ANY, ANY, ANY],
        out_shape=[
            shape_of((tokens, width), F32),
            shape_of((8, width), F32),
            shape_of((ff, width), F32),
            shape_of((width, ff), F32),
            shape_of((own, width), F32),
            shape_of((tokens, width), BF),
            shape_of((3 * own, width), F32),
        ],
        scratch_shapes=[
            pltpu.VMEM(main.shape, F32),
            pltpu.VMEM(rest.shape, F32),
            pltpu.VMEM((tokens, width), BF),
            dma((3,)),
            dma((5,)),
        ],
        compiler_params=params(),
        name="token_back",
    )(dqkv, weights, x, mg, gains, main, rest, result)


def sums_kernel(in_ref, out_ref, land, sends, recvs):
    device = lax.axis_index("dp")
    place = lax.rem(device, 8)
    others = []
    for bits in range(1, 8):
        other = device
        for bit in (1, 2, 4):
            if bits & bit:
                other = flip(other, bit)
        others.append(other)
    greet(*[{"dp": other} for other in others])
    copies = [
        remote(in_ref, land.at[place], sends.at[i], recvs.at[place], dp=other) for i, other in enumerate(others)
    ]
    for copy in copies:
        copy.start()
    land[place] = in_ref[...]
    for other in others:
        peer = lax.rem(other, 8)
        remote(in_ref, land.at[peer], sends.at[0], recvs.at[peer], dp=other).wait_recv()
    out_ref[...] = jnp.sum(land[...], 0)
    for copy in copies:
        copy.wait_send()


def add_sums(sums):
    dma = pltpu.SemaphoreType.DMA
    return pl.pallas_call(
        sums_kernel,
        in_specs=[WHOLE],
        out_specs=WHOLE,
        out_shape=shape_of(sums.shape, F32),
        scratch_shapes=[pltpu.VMEM((8,) + sums.shape, F32), dma((7,)), dma((8,))],
        compiler_params=pltpu.CompilerParams(collective_id=3, has_side_effects=True),
        name="add_sums",
    )(sums)


def arrange_kernel(sums_ref, rest_any, gains_ref, shifts_ref, biases_ref, qv_bias_ref, up_bias_ref, rows_v, sems, *, own):
    loads = [
        pltpu.make_async_copy(rest_any.at[pl.ds(low, 16), :], rows_v.at[i], sems.at[i])
        for i, low in enumerate((3 * own, 4 * own + 64))
    ]
    for copy in loads:
        copy.start()
    gains_ref[0:1, :] = sums_ref[0:1, :]
    shifts_ref[0:1, :] = sums_ref[1:2, :]
    for copy in loads:
        copy.wait()
    gains_ref[1:2, :] = rows_v[1, GAIN_TWO : GAIN_TWO + 1, :]
    shifts_ref[1:2, :] = rows_v[1, SHIFT_TWO : SHIFT_TWO + 1, :]
    biases_ref[...] = rows_v[1, BIAS_ONE : BIAS_TWO + 1, :]
    up_bias_ref[...] = rows_v[1, UP_BIAS, :]
    qv_bias_ref[0:1, :] = rows_v[0, 0:1, :own]
    qv_bias_ref[1:2, :] = rows_v[0, 8:9, :own]


def arrange(sums, rest, own):
    width = sums.shape[1]
    return pl.pallas_call(
        partial(arrange_kernel, own=own),
        in_specs=[WHOLE, ANY],
        out_specs=[WHOLE] * 5,
        out_shape=[shape_of((2, width), F32)] * 3 + [shape_of((2, own), F32), shape_of((width,), F32)],
        scratch_shapes=[pltpu.VMEM((2, 16, width), F32), pltpu.SemaphoreType.DMA((2,))],
        name="arrange",
    )(sums, rest)


GELU_C = 0.7978845608028654
GELU_A = 0.044715


def gelu_both(pre):
    square = pre * pre
    half = 0.5 + 0.5 * jnp.tanh(pre * (GELU_C + (GELU_C * GELU_A) * square))
    act = pre * half
    slope = half + act * (1.0 - half) * (2.0 * GELU_C + (6.0 * GELU_C * GELU_A) * square)
    return act, slope


GAIN_TWO, SHIFT_TWO, BIAS_ONE, BIAS_TWO, UP_BIAS = range(5)


def mlp_kernel(
    wo_ref, smalls_ref, bias_ref, gain_ref, shift_ref, x_any, ot_any, g_any, up_any, down_any, land_any, z_any,
    result_out, mg_out, dt_out, main_out, tail_out,
    land, z_far, wide_w, own_w, g_ref, h2_ref, dt_ref, mine_ref, main_ref, tail_ref, normed_ref, inv_ref, res_ref, hg_ref,
    up_low, down_low, pre_s, ag_s,
    in_sems, w_sems, keep_sems, far_keep, far_send, far_recv, out_sems, tile_sems, send_sems, recv_sems, *comm,
):
    tokens, width = g_ref.shape
    parts = smalls_ref.shape[0]
    own = mine_ref.shape[0]
    ff = up_any.shape[1]
    units = ff // UNIT
    chunks = units * (parts - 1)
    late = land.shape[0]
    early = chunks - late
    share = z_any.shape[3]
    strip = UNIT // 8
    tiles = tokens // TILE
    me = lax.axis_index("mp")
    order = foreign_order(me)
    total = Total(main_ref, *comm)

    def source_of(c):
        j = lax.div(c, units)
        return jnp.where(j == 0, order[0], jnp.where(j == 1, order[1], order[2]))

    def pieces_at(e, at, count, half):
        rows = pl.ds(pl.multiple_of(at * share, 8), count * share)
        if half is None:
            return land.at[e, :, rows, :]
        return land.at[e, half, rows, :]

    spread = Spread(pieces_at, send_sems, recv_sems)
    far_at = units - early
    far_count = units * (parts - 2)

    def mine(e):
        return z_any.at[order[(early + e) // units], (early + e) % units]

    inner = (me > 0) & (me < parts - 1)

    def far_source(u):
        return z_any.at[jnp.where(u < units, order[1], order[2]), lax.rem(u, units)]

    def far_copy(u):
        step = jnp.where(lax.div(me, 2) == 0, -1, 1)
        return remote(far_source(u), z_far.at[u], far_send.at[u], far_recv.at[u], mp=me + step)

    def far_local(u):
        return pltpu.make_async_copy(far_source(u), z_far.at[u], far_keep.at[u])

    def far(u):
        @pl.when(inner)
        def _():
            far_local(u).wait()

        @pl.when(jnp.logical_not(inner))
        def _():
            remote(z_far.at[u], z_far.at[u], far_send.at[u], far_recv.at[u], mp=me).wait_recv()

    def keep(e, source):
        return pltpu.make_async_copy(source, pieces_at(e, spread.at, 1, None), keep_sems.at[e])

    def send(e):
        @pl.when((e >= far_at) & (e < late))
        def _():
            far(e - far_at)
            keep(e, z_far.at[e - far_at]).start()

        @pl.when(e < late)
        def _():
            keep(e, z_far.at[0]).wait()
            spread.send(e)

    def serve(n):
        send(n + 1)

        @pl.when(n - 1 < late)
        def _():
            spread.forward(n - 1)

        @pl.when((n > 1) & (n - 2 < late))
        def _():
            spread.corner(n - 2)

    def reduce(n):
        @pl.when(n == units)
        def _():
            total.start(0)

        @pl.when(n == units + 7)
        def _():
            total.finish(0)
            total.start(1)

    def unit(bias, grads_at):
        def front(i):
            rows = slice(i * TILE, (i + 1) * TILE)
            pre_s[i % 2] = dot(h2_ref[rows, :], up_low[...], NN) + bias
            ag_s[i % 2] = dot(g_ref[rows, :], down_low[...], NT)

        def back(i):
            rows = slice(i * TILE, (i + 1) * TILE)
            act, slope = gelu_both(pre_s[i % 2])
            act = act.astype(BF)
            pre_grad = (ag_s[i % 2] * slope).astype(BF)
            res_ref[rows, :] += dot(act, down_low[...], NN)
            hg_ref[rows, :] += dot(pre_grad, up_low[...], NT)
            if grads_at is not None:
                h2 = h2_ref[rows, :]
                g = g_ref[rows, :]
                cols = pl.ds(pl.multiple_of(grads_at, UNIT), UNIT)
                main_ref[cols, :] += dot(act, g, TN)
                main_ref[ff:, cols] += dot(h2, pre_grad, TN)
                at = own + UP_BIAS
                tail_ref[at : at + 1, cols] += jnp.sum(pre_grad.astype(F32), 0, keepdims=True)

        front(0)
        for i in range(tiles):
            if i + 1 < tiles:
                front(i + 1)
            back(i)

    loads = [
        pltpu.make_async_copy(source, target, in_sems.at[i])
        for i, (source, target) in enumerate(((ot_any, dt_ref), (x_any, h2_ref), (g_any, g_ref)))
    ]

    def own_load(u):
        cols = pl.ds(pl.multiple_of(u * UNIT, UNIT), UNIT)
        return [
            pltpu.make_async_copy(up_any.at[:, cols], wide_w.at[0], w_sems.at[0]),
            pltpu.make_async_copy(down_any.at[cols, :], own_w, w_sems.at[1]),
        ]

    def chunk_load(c):
        return pltpu.make_async_copy(land_any.at[c], wide_w, w_sems.at[0])

    for copy in loads:
        copy.start()
    for copy in own_load(0):
        copy.start()
    for e in range(far_at):
        keep(e, mine(e)).start()

    @pl.when(inner)
    def _():
        for u in range(far_count):
            far_local(u).start()

    greet(
        *[{"mp": lax.rem(me + s, parts)} for s in range(1, parts)],
        *[{"dp": flip(spread.device, bit)} for bit in (1, 2, 4)],
    )

    @pl.when(inner)
    def _():
        for u in range(far_count):
            far_copy(u).start()

    send(0)
    send(1)
    main_ref[...] = jnp.zeros_like(main_ref)
    tail_ref[...] = jnp.zeros_like(tail_ref)
    for copy in loads[:2]:
        copy.wait()
    mine_ref[...] = dt_ref[:own, :]

    def first(i, carry):
        rows = pl.ds(pl.multiple_of(i * TILE, TILE), TILE)
        mixed = h2_ref[rows, :].astype(F32) + dot(dt_ref[:, rows], wo_ref[...], TN) + bias_ref[0:1, :]
        res_ref[rows, :] = mixed + bias_ref[1:2, :]
        hg_ref[rows, :] = jnp.zeros((TILE, width), F32)
        normed, inv_std = standardize(mixed)
        normed_ref[rows, :] = normed
        inv_ref[rows, :] = inv_std
        h2_ref[rows, :] = (normed * gain_ref[1:2, :] + shift_ref[1:2, :]).astype(BF)
        return carry

    lax.fori_loop(0, tiles, first, 0, unroll=2)
    serve(1)
    loads[2].wait()

    def own_unit(u, carry):
        for copy in own_load(u):
            copy.wait()
        up_low[...] = wide_w[0].astype(BF)
        down_low[...] = own_w[...].astype(BF)

        @pl.when(u + 1 < units)
        def _():
            for copy in own_load(u + 1):
                copy.start()

        @pl.when(u + 1 == units)
        def _():
            chunk_load(0).start()

        unit(smalls_ref[me, 2:3, pl.ds(pl.multiple_of(u * UNIT, UNIT), UNIT)], u * UNIT)
        serve(u + 2)
        reduce(u + 1)
        return carry

    lax.fori_loop(0, units, own_unit, 0)

    def take(ref, at):
        up_low[...] = ref[at + (0,)].astype(BF)
        for q in range(8):
            for k in range(width // UNIT):
                low = q * share + k * strip
                down_low[q * strip : (q + 1) * strip, k * UNIT : (k + 1) * UNIT] = ref[
                    at + (1, slice(low, low + strip))
                ].astype(BF)

    def foreign_unit(c, carry):
        @pl.when(c < early)
        def _():
            chunk_load(c).wait()
            take(wide_w, ())

        @pl.when(c + 1 < early)
        def _():
            chunk_load(c + 1).start()

        @pl.when(c >= early)
        def _():
            e = c - early
            spread.complete(e)
            take(land, (e,))

        cols = pl.ds(pl.multiple_of(lax.rem(c, units) * UNIT, UNIT), UNIT)
        unit(smalls_ref[source_of(c), 2:3, cols], None)
        serve(c + units + 2)
        reduce(c + units + 1)
        return carry

    lax.fori_loop(0, chunks, foreign_unit, 0)

    def tile_stores(i):
        rows = pl.ds(pl.multiple_of(i * TILE, TILE), TILE)
        return [
            pltpu.make_async_copy(source, target, tile_sems.at[k])
            for k, (source, target) in enumerate((
                (h2_ref.at[rows, :], result_out.at[rows, :]),
                (hg_ref.at[rows, :], mg_out.at[rows, :]),
                (dt_ref.at[:, rows], dt_out.at[:, rows]),
            ))
        ]

    def finish(i, carry):
        rows = pl.ds(pl.multiple_of(i * TILE, TILE), TILE)
        g = g_ref[rows, :].astype(F32)
        h2_ref[rows, :] = res_ref[rows, :].astype(BF)
        normed, inv_std = normed_ref[rows, :], inv_ref[rows, :]
        hg = hg_ref[rows, :]
        mg = g + norm_back(hg, normed, inv_std, gain_ref[1:2, :])
        hg_ref[rows, :] = mg
        low = mg.astype(BF)
        dt_ref[:, rows] = dot(wo_ref[...], low, NT).astype(BF)
        tail_ref[:own, :] += dot(mine_ref[:, rows], low, NN)
        for at, value in ((GAIN_TWO, hg * normed), (SHIFT_TWO, hg), (BIAS_ONE, mg), (BIAS_TWO, g)):
            tail_ref[own + at : own + at + 1, :] += jnp.sum(value, 0, keepdims=True)
        for copy in tile_stores(i):
            copy.start()
        return carry

    lax.fori_loop(0, tiles, finish, 0, unroll=2)
    total.finish(1)
    ends = [
        pltpu.make_async_copy(total.rows(at, total.part), main_out.at[pl.ds(pl.multiple_of(at, 8), total.part), :], sem)
        for at, sem in ((total.one, out_sems.at[0]), (total.two, out_sems.at[1]))
    ]
    ends.append(pltpu.make_async_copy(tail_ref, tail_out, out_sems.at[2]))
    for copy in ends:
        copy.start()
    for e in range(late):
        spread.sent(e)

    @pl.when(inner)
    def _():
        for u in range(far_count):
            far_copy(u).wait_send()

    for k, ref in enumerate((h2_ref, hg_ref, dt_ref)):
        pltpu.make_async_copy(ref, ref, tile_sems.at[k]).wait()
    for copy in ends:
        copy.wait()


def mlp(x, ot, wo, g, up, down, smalls, biases, gains, shifts, land, z):
    tokens, width = x.shape
    parts = smalls.shape[0]
    own = width // parts
    ff = up.shape[1]
    units = ff // UNIT
    chunks = units * (parts - 1)
    late = chunks - land.shape[0]
    tiles = tokens // TILE
    rows = 2 * ff
    tail = own + 64
    dma = pltpu.SemaphoreType.DMA
    return pl.pallas_call(
        mlp_kernel,
        in_specs=[WHOLE] * 5 + [ANY] * 7,
        out_specs=[ANY] * 5,
        out_shape=[
            shape_of((tokens, width), BF),
            shape_of((tokens, width), F32),
            shape_of((width, tokens), BF),
            shape_of((rows, width), F32),
            shape_of((tail, width), F32),
        ],
        scratch_shapes=[
            pltpu.VMEM((late, 2, width, UNIT), F32),
            pltpu.VMEM((units * (parts - 2), 2, width // 8, UNIT), F32),
            pltpu.VMEM((2, width, UNIT), F32),
            pltpu.VMEM((UNIT, width), F32),
            pltpu.VMEM((tokens, width), BF),
            pltpu.VMEM((tokens, width), BF),
            pltpu.VMEM((width, tokens), BF),
            pltpu.VMEM((own, tokens), BF),
            pltpu.VMEM((rows, width), F32),
            pltpu.VMEM((tail, width), F32),
            pltpu.VMEM((tokens, width), F32),
            pltpu.VMEM((tokens, 1), F32),
            pltpu.VMEM((tokens, width), F32),
            pltpu.VMEM((tokens, width), F32),
            pltpu.VMEM((width, UNIT), BF),
            pltpu.VMEM((UNIT, width), BF),
            pltpu.VMEM((2, TILE, UNIT), F32),
            pltpu.VMEM((2, TILE, UNIT), F32),
            dma((3,)),
            dma((2,)),
            dma((late,)),
            dma((units * (parts - 2),)),
            dma((units * (parts - 2),)),
            dma((units * (parts - 2),)),
            dma((3,)),
            dma((3,)),
            dma((late,)),
            dma((late, 3)),
        ]
        + Total.scratch(rows, width),
        compiler_params=pltpu.CompilerParams(vmem_limit_bytes=63 * 2**20, collective_id=1, has_side_effects=True),
        name="mlp",
    )(wo, smalls, biases, gains, shifts, x, ot, g, up, down, land, z)


def body(
    dp_size,
    tokens,
    segments,
    norm_gains,
    norm_shifts,
    qkv_weight,
    qv_bias,
    out_weight,
    out_biases,
    up_weight,
    up_bias,
    down_weight,
    cotangent,
):
    width = tokens.shape[1]
    own = qkv_weight.shape[2]
    ff = up_weight.shape[1]
    smalls, bound, h1, weights, wo, qkvt, ot, lse, land, z = front(
        tokens, segments, norm_gains, norm_shifts, qkv_weight.transpose(0, 2, 1).reshape(3 * own, width), out_weight,
        qv_bias, up_bias, up_weight, down_weight,
    )
    ot, lse = repair(bound, segments, qkvt, ot, lse)
    result, mg, dt, main, tail = mlp(
        tokens, ot, wo, cotangent, up_weight, down_weight, smalls, out_biases, norm_gains, norm_shifts, land, z
    )
    dqkv, main, rest = attend_back(segments, qkvt, ot, dt, lse, h1, main, tail)
    if dp_size > 8:
        main, rest = (value / 8 for value in lax.psum((main, rest), "dp"))
    token_grad, sums_one, down_grad, up_grad, out_weight_grad, result, qkv_grad = token_back(
        dqkv, weights, tokens, mg, norm_gains, main, rest, result, ff, own
    )
    sums_one = add_sums(sums_one)
    if dp_size > 8:
        sums_one = lax.psum(sums_one, "dp") / 8
    gains_grad, shifts_grad, out_biases_grad, qv_bias_grad, up_bias_grad = arrange(sums_one, rest, own)
    return (
        result,
        token_grad,
        gains_grad,
        shifts_grad,
        qkv_grad.reshape(3, own, width).transpose(0, 2, 1),
        qv_bias_grad,
        out_weight_grad,
        out_biases_grad,
        up_grad,
        up_bias_grad,
        down_grad,
    )


def solution(mesh):
    in_specs = (
        P("dp", None),
        P("dp", None),
        P(),
        P(),
        P(None, None, "mp"),
        P(None, "mp"),
        P("mp", None),
        P(),
        P(None, "mp"),
        P("mp"),
        P("mp", None),
        P("dp", None),
    )
    out_specs = (
        P("dp", None),
        P("dp", None),
        P(),
        P(),
        P(None, None, "mp"),
        P(None, "mp"),
        P("mp", None),
        P(),
        P(None, "mp"),
        P("mp"),
        P("mp", None),
    )
    return jax.shard_map(
        partial(body, mesh.shape["dp"]), mesh=mesh, in_specs=in_specs, out_specs=out_specs, check_vma=False
    )
```

```python
from functools import partial

import jax
import jax.numpy as jnp
from jax import lax
from jax.experimental import pallas as pl
from jax.experimental.pallas import tpu as pltpu
from jax.sharding import PartitionSpec as P

F32 = jnp.float32
BF = jnp.bfloat16
HEAD_DIM = 64
NORM_EPSILON = 1e-06
BIG = 1e30
LOG2E = 1.4426950408889634
SAFE_SCORE = 60.0
REACH = 512
TILE = 256
LONG_TILE = 512
EXTRA = 16
UNIT = 256
EARLY = 1

NN = (((1,), (0,)), ((), ()))
NT = (((1,), (1,)), ((), ()))
TN = (((0,), (0,)), ((), ()))
WHOLE = pl.BlockSpec(memory_space=pltpu.VMEM)
ONCE = pl.BlockSpec(memory_space=pltpu.VMEM, pipeline_mode=pl.Buffered(1))
ANY = pl.BlockSpec(memory_space=pl.ANY)


def dot(left, right, dims):
    return lax.dot_general(left, right, dims, preferred_element_type=F32)


def params(mib=56):
    return pltpu.CompilerParams(vmem_limit_bytes=mib * 2**20)


def standardize(values):
    centered = values - jnp.mean(values, -1, keepdims=True)
    inv_std = lax.rsqrt(jnp.mean(centered * centered, -1, keepdims=True) + NORM_EPSILON)
    return centered * inv_std, inv_std


def norm_back(grad_in, normed, inv_std, gain):
    scaled = grad_in * gain
    return inv_std * (
        scaled
        - jnp.mean(scaled, -1, keepdims=True)
        - normed * jnp.mean(scaled * normed, -1, keepdims=True)
    )


def shape_of(shape, dtype):
    return jax.ShapeDtypeStruct(shape, dtype)


def flip(index, bit):
    return index + bit - 2 * bit * lax.rem(lax.div(index, bit), 2)


def remote(src, dst, send_sem, recv_sem, **where):
    return pltpu.make_async_remote_copy(
        src_ref=src, dst_ref=dst, send_sem=send_sem, recv_sem=recv_sem, device_id=where,
        device_id_type=pl.DeviceIdType.MESH,
    )


SIDE, ACROSS, DIAG_A, DIAG_B, CORE = range(5)
NEAR, CORNER, OTHER = range(3)


def position(device):
    place = lax.rem(device, 8)
    return lax.rem(place, 2) * 4 + lax.div(place, 2)


class Spread:
    def __init__(self, pieces, send_sems, recv_sems, mine=None):
        self.pieces, self.send_sems, self.recv_sems, self.mine = pieces, send_sems, recv_sems, mine
        self.device = lax.axis_index("dp")
        self.at = position(self.device)
        self.side, self.across = flip(self.at, 1), flip(self.at, 2)
        self.corner_at = flip(self.side, 2)
        self.core = lax.div(self.at, 4) * 4

    def copy(self, chunk, kind, src=None):
        at, count, half, bit, arrival = {
            SIDE: (self.at, 1, None, 2, NEAR),
            ACROSS: (self.at, 1, None, 4, NEAR),
            DIAG_A: (self.side, 1, 0, 4, CORNER),
            DIAG_B: (self.across, 1, 1, 2, CORNER),
            CORE: (self.core, 4, None, 1, OTHER),
        }[kind]
        dst = self.pieces(chunk, at, count, half)
        return remote(
            dst if src is None else src, dst, self.send_sems.at[chunk], self.recv_sems.at[chunk, arrival],
            dp=flip(self.device, bit),
        )

    def arrived(self, chunk, arrival, count):
        ref = self.pieces(chunk, 0, count, None)
        remote(ref, ref, self.send_sems.at[chunk], self.recv_sems.at[chunk, arrival], dp=self.device).wait_recv()

    def send(self, chunk):
        src = None if self.mine is None else self.mine(chunk)
        for kind in (SIDE, ACROSS):
            self.copy(chunk, kind, src).start()

    def forward(self, chunk):
        self.arrived(chunk, NEAR, 2)
        for kind in (DIAG_A, DIAG_B):
            self.copy(chunk, kind).start()

    def corner(self, chunk):
        self.arrived(chunk, CORNER, 1)
        self.copy(chunk, CORE).start()

    def complete(self, chunk):
        self.arrived(chunk, OTHER, 4)

    def sent(self, chunk):
        ref = self.pieces(chunk, 0, 7, None)
        remote(ref, ref, self.send_sems.at[chunk], self.recv_sems.at[chunk, 0], dp=self.device).wait_send()


def greet(*peers):
    barrier = pltpu.get_barrier_semaphore()
    for peer in peers:
        pl.semaphore_signal(barrier, inc=1, device_id=peer, device_id_type=pl.DeviceIdType.MESH)
    pl.semaphore_wait(barrier, len(peers))


def foreign_order(me):
    half = lax.div(me, 2)
    return flip(me, 1), 2 - half, 3 - 3 * half


def front_kernel(
    gain_ref, shift_ref, qkv_ref, out_ref, qv_bias_ref, up_bias_ref, seg_ref, x_any, up_any, down_any,
    smalls_ref, bound_ref, h1_out, w_out, wo_out, qkvt_out, ot_out, lse_out, land_out, z_out,
    x_in, h1_ref, land, wo_land, z_land, mlp_land, pieces, small_land, w_low, wo_low, bias_col,
    qkvt_ref, ot_ref, lse_ref, qx, kx, vx, kn,
    x_sem, piece_sem, keep_sems, out_sems, slice_sems, z_send, z_recv, own_send, small_send, small_recv,
    send_sems, recv_sems,
):
    parts, rows, width = land.shape
    own = out_ref.shape[0]
    heads = own // HEAD_DIM
    tokens = x_in.shape[0]
    length = seg_ref.shape[1]
    units = pieces.shape[0]
    items = 3 + units
    early = mlp_land.shape[0]
    share, out_share, mlp_share = rows // 8, own // 8, width // 8
    split = (0, share // 16 * 8 + 8, share)
    strip = UNIT // 8
    me = lax.axis_index("mp")
    device = lax.axis_index("dp")
    order = foreign_order(me)
    out_chunk, mlp_chunk = 2 * (parts - 1), 3 * (parts - 1)

    def some_rows(start, size, at, count, half):
        low, high = 0, count * size
        if half is not None:
            middle = (size + 8) // 16 * 8
            low, high = (0, middle) if half == 0 else (middle, size)
        return pl.ds(pl.multiple_of(start + at * size + low, 8), high - low)

    def slab_rows(h, at, count=1, half=None):
        return some_rows(split[h] * 8, split[h + 1] - split[h], at, count, half)

    def out_rows(at, count=1, half=None):
        return some_rows(0, out_share, at, count, half)

    def pieces_at(c, at, count, half):
        if c < out_chunk:
            return land.at[order[c // 2], slab_rows(c % 2, at, count, half), :]
        if c < mlp_chunk:
            return wo_land.at[order[c - out_chunk], out_rows(at, count, half), :]
        rows = some_rows(0, mlp_share, at, count, None)
        if half is None:
            return mlp_land.at[c - mlp_chunk, :, rows, :]
        return mlp_land.at[c - mlp_chunk, half, rows, :]

    place = position(device)

    def mine(c):
        if c < mlp_chunk:
            return pieces_at(c, place, 1, None)
        return z_land.at[order[(c - mlp_chunk) // units], (c - mlp_chunk) % units]

    spread = Spread(pieces_at, send_sems, recv_sems, mine)

    def hop_ref(source, item):
        if item < 2:
            return land.at[source, slab_rows(item, place), :]
        if item == 2:
            return wo_land.at[source, out_rows(place), :]
        return z_land.at[source, item - 3]

    def own_ref(item):
        if item < 2:
            return qkv_ref.at[slab_rows(item, place), :]
        if item == 2:
            return out_ref.at[out_rows(place), :]
        return pieces.at[item - 3]

    def own_copies(item, act):
        def copy(up):
            return remote(
                own_ref(item), hop_ref(me, item), own_send.at[item, up], z_recv.at[me, item], mp=me + 2 * up - 1
            )

        @pl.when(me < parts - 1)
        def _():
            act(copy(1))

        @pl.when(me > 0)
        def _():
            act(copy(0))

    def pass_on(j, item, act):
        source = order[j]
        ref = hop_ref(source, item)

        def copy(step):
            return remote(ref, ref, z_send.at[source, item], z_recv.at[source, item], mp=me + step)

        end = 0 if item < 3 else 1

        @pl.when((source < me) & (me < parts - 1 - end))
        def _():
            act(copy(1))

        @pl.when((source > me) & (me > end))
        def _():
            act(copy(-1))

    def landed(j, item):
        ref = hop_ref(order[j], item)
        remote(ref, ref, z_send.at[order[j], item], z_recv.at[order[j], item], mp=me).wait_recv()
        pass_on(j, item, lambda copy: copy.start())
        if item >= 3 and j * units + item - 3 < early:
            keep(j * units + item - 3).start()

    inner = (me > 0) & (me < parts - 1)

    def landings(inner_items, outer_items):
        @pl.when(inner)
        def _():
            for j, item in inner_items:
                landed(j, item)

        @pl.when(jnp.logical_not(inner))
        def _():
            for j, item in outer_items:
                landed(j, item)

    def keep(c):
        return pltpu.make_async_copy(
            mine(mlp_chunk + c), pieces_at(mlp_chunk + c, place, 1, None), keep_sems.at[c]
        )

    def small_copy(s):
        ref = small_land.at[me]
        return remote(ref, ref, small_send.at[s - 1], small_recv.at[me], mp=lax.rem(me + s, parts))

    def at_place(at, ref):
        w_low[at] = ref[...].astype(BF)

    def slice_stores(at):
        rows_at = pl.ds(pl.multiple_of(at * rows, rows), rows)
        own_at = pl.ds(pl.multiple_of(at * own, own), own)
        return [
            pltpu.make_async_copy(w_low.at[at], w_out.at[rows_at, :], slice_sems.at[at, 0]),
            pltpu.make_async_copy(qkvt_ref.at[rows_at, :], qkvt_out.at[rows_at, :], slice_sems.at[at, 1]),
            pltpu.make_async_copy(ot_ref.at[own_at, :], ot_out.at[own_at, :], slice_sems.at[at, 2]),
        ]

    x_copy = pltpu.make_async_copy(x_any, x_in, x_sem)
    h1_copy = pltpu.make_async_copy(h1_ref, h1_out, out_sems.at[0])
    lse_copy = pltpu.make_async_copy(lse_ref, lse_out, out_sems.at[1])
    wo_copy = pltpu.make_async_copy(wo_low, wo_out, out_sems.at[2])
    z_copy = pltpu.make_async_copy(z_land, z_out, out_sems.at[3])
    land_copy = pltpu.make_async_copy(mlp_land, land_out, out_sems.at[4])

    x_copy.start()
    copies = []
    for u in range(units):
        at = pl.ds(pl.multiple_of(place * mlp_share, 8), mlp_share)
        copies.append((up_any.at[at, pl.ds(u * UNIT, UNIT)], pieces.at[u, 0]))
        for c in range(width // UNIT):
            at = pl.ds(pl.multiple_of(u * UNIT + place * strip, 8), strip)
            copies.append((down_any.at[at, pl.ds(c * UNIT, UNIT)], pieces.at[u, 1, pl.ds(c * strip, strip), :]))
    for source, target in copies:
        pltpu.make_async_copy(source, target, piece_sem).start()
    greet(
        *[{"mp": lax.rem(me + s, parts)} for s in range(1, parts)],
        *[{"dp": flip(device, bit)} for bit in (1, 2, 4)],
    )
    for item in range(2):
        own_copies(item, lambda copy: copy.start())
    small_land[me] = jnp.zeros(small_land.shape[1:], F32)
    small_land[me, 0:2, :own] = qv_bias_ref[...]
    small_land[me, 2:3, :] = up_bias_ref[...].reshape(1, width)
    for s in range(1, parts):
        small_copy(s).start()
    own_copies(2, lambda copy: copy.start())
    bound_ref[...] = jnp.zeros_like(bound_ref)
    bias_col[...] = jnp.zeros_like(bias_col)
    lse_ref[...] = jnp.zeros_like(lse_ref)
    z_land[me] = jnp.zeros(z_land.shape[1:], F32)

    @pl.when(jnp.logical_not(inner))
    def _():
        for source in order[1:]:
            z_land[source] = jnp.zeros(z_land.shape[1:], F32)

    for j in range(2):
        bias_col[0, 2 * j * own : (2 * j + 1) * own, :] = small_land[me].T[:own, j : j + 1]
    at_place(0, qkv_ref)
    wo_low[:own, :] = out_ref[...].astype(BF)
    x_copy.wait()

    def norm_tile(i, carry):
        at = pl.ds(pl.multiple_of(i * TILE, TILE), TILE)
        normed, _ = standardize(x_in[at, :].astype(F32))
        h1_ref[at, :] = (normed * gain_ref[0:1, :] + shift_ref[0:1, :]).astype(BF)
        return carry

    lax.fori_loop(0, tokens // TILE, norm_tile, 0, unroll=2)
    h1_copy.start()
    row = lax.broadcasted_iota(jnp.int32, (EXTRA, length), 0)
    for u in range(heads):
        vx[u, HEAD_DIM:, :] = jnp.ones((EXTRA, length), BF)

    def norm_bound(ref, u):
        value = ref[u, :HEAD_DIM, :].astype(F32)
        return jnp.max(jnp.sum(value * value, 0, keepdims=True), 1, keepdims=True)

    def project(at, r):
        tokens_r = pl.ds(pl.multiple_of(r * length, length), length)
        base = at * rows
        value = dot(w_low[at], h1_ref[tokens_r, :], NT) + bias_col[at]
        scale = HEAD_DIM**-0.5
        qkvt_ref[pl.ds(pl.multiple_of(base, own), own), tokens_r] = value[:own].astype(BF) * jnp.asarray(scale, BF)
        qkvt_ref[pl.ds(pl.multiple_of(base + own, own), 2 * own), tokens_r] = value[own:].astype(BF)

    def attend(at, r):
        tokens_r = pl.ds(pl.multiple_of(r * length, length), length)
        base = at * rows
        same = row == seg_ref[pl.ds(r, 1), :]
        for u in range(heads):
            qx[u, HEAD_DIM:, :] = jnp.where(same | (row >= 8), 0.0, -BIG).astype(BF)
            kx[u, HEAD_DIM:, :] = jnp.where(same, 1.0, 0.0).astype(BF)
        for u in range(heads):
            for k, ref in enumerate((qx, kx, vx)):
                from_row = pl.multiple_of(base + k * own + u * HEAD_DIM, HEAD_DIM)
                ref[u, :HEAD_DIM, :] = qkvt_ref[pl.ds(from_row, HEAD_DIM), tokens_r]
            kn[u] = kx[u].T
            bound_ref[...] = jnp.maximum(bound_ref[...], norm_bound(qx, u) * norm_bound(kx, u))
            to_row = pl.ds(pl.multiple_of(at * own + u * HEAD_DIM, HEAD_DIM), HEAD_DIM)
            for t in range(length // TILE):
                low, high = max(0, t * TILE - REACH), min(length, (t + 1) * TILE + REACH)
                cols = slice(t * TILE, (t + 1) * TILE)
                to_cols = pl.ds(pl.multiple_of(r * length + t * TILE, TILE), TILE)
                probs = [
                    jnp.exp2(dot(kn[u, k : k + TILE, :], qx[u, :, cols], NN) * LOG2E).astype(BF)
                    for k in range(low, high, TILE)
                ]
                out = dot(vx[u, :, low:high], jnp.concatenate(probs, 0), NN)
                total = out[HEAD_DIM : HEAD_DIM + 1, :]
                ot_ref[to_row, to_cols] = (out[:HEAD_DIM, :] * (1.0 / total)).astype(BF)
                lse_ref[pl.ds(at * heads + u, 1), to_cols] = jnp.log(total)

    w, m = out_chunk, mlp_chunk

    def event(n):
        if n == 0:
            landings(((0, 0), (1, 0)), ((0, 0),))
            spread.send(0)
            landings(((0, 1), (1, 1)), ((0, 1),))
            spread.send(1)
        if n == 1:
            spread.forward(0)
            spread.forward(1)
            landings(((2, 0),), ((1, 0),))
            spread.send(2)
        if n == 1.5:
            landings(((2, 1),), ((1, 1),))
            spread.send(3)
        if n == 2:
            spread.corner(0)
            spread.corner(1)
            landings(((0, 2), (1, 2)), ((2, 0),))
            spread.send(4)
            for s in range(1, parts):
                ref = small_land.at[lax.rem(me + s, parts)]
                remote(ref, ref, small_send.at[0], small_recv.at[lax.rem(me + s, parts)], mp=me).wait_recv()
            smalls_ref[...] = small_land[...]
            for j, source in enumerate(order):
                cols = small_land[source].T
                for k in range(2):
                    bias_col[1 + j, 2 * k * own : (2 * k + 1) * own, :] = cols[:own, k : k + 1]
            spread.complete(0)
            spread.complete(1)
            at_place(1, land.at[order[0]])
        if n == 2.5:
            spread.forward(2)
            landings((), ((2, 1),))
            spread.send(5)
            spread.forward(3)
            pltpu.make_async_copy(pieces, pieces, piece_sem).wait()
            own_copies(3, lambda copy: copy.start())
        if n == 3:
            spread.forward(4)
            landings(((2, 2),), ((0, 2),))
            spread.send(w)
            own_copies(4, lambda copy: copy.start())
        if n == 3.5:
            spread.corner(2)
            spread.corner(3)
            spread.forward(5)
        if n == 4:
            spread.complete(2)
            spread.complete(3)
            at_place(2, land.at[order[1]])
            landings(((0, 3), (1, 3)), ((1, 2), (0, 3)))
            spread.send(w + 1)
            own_copies(5, lambda copy: copy.start())
        if n == 4.5:
            spread.corner(4)
            spread.corner(5)
            spread.forward(w)
            for c in range(early):
                spread.send(m + c)
        if n == 5:
            landings(((0, 4), (1, 4)), ((2, 2), (0, 4)))
            spread.send(w + 2)
            spread.corner(w)
            spread.forward(w + 1)
        if n == 6:
            spread.complete(4)
            spread.complete(5)
            at_place(3, land.at[order[2]])
            landings(((0, 5), (1, 5), (2, 3)), ((0, 5),))
            spread.forward(w + 2)
            spread.corner(w + 1)
            for c in range(early):
                spread.forward(m + c)
        if n == 7:
            landings(((2, 4),), ())
            spread.corner(w + 2)
            for c in range(early):
                keep(c).wait()
                spread.corner(m + c)
            spread.complete(w)
        if n == 8:
            landings(((2, 5),), ())
            z_copy.start()
            spread.complete(w + 1)
            spread.complete(w + 2)
            for c in range(early):
                spread.complete(m + c)
            land_copy.start()
            for j in range(parts - 1):
                wo_low[(j + 1) * own : (j + 2) * own, :] = wo_land[order[j]].astype(BF)
            wo_copy.start()
            lse_copy.start()

    event(0)

    def step(n, carry):
        at, r = lax.div(n, 2), lax.rem(n, 2)
        project(at, r)
        for e in (1, 2, 3, 4):
            @pl.when(n == e)
            def _():
                event(e + 0.5)

        attend(at, r)

        @pl.when(r == 1)
        def _():
            for copy in slice_stores(at):
                copy.start()

        for e in range(1, 9):
            @pl.when(n + 1 == e)
            def _():
                event(e)

        return carry

    lax.fori_loop(0, 2 * parts, step, 0)
    for c in range(mlp_chunk + early):
        spread.sent(c)
    for item in range(items):
        own_copies(item, lambda copy: copy.wait_send())
        for j in range(parts - 1):
            pass_on(j, item, lambda copy: copy.wait_send())
    for s in range(1, parts):
        small_copy(s).wait_send()
    for copy in (h1_copy, lse_copy, wo_copy, z_copy, land_copy):
        copy.wait()
    for at in range(parts):
        for copy in slice_stores(at):
            copy.wait()


def front(x, seg, gains, shifts, qkv, out, qv_bias, up_bias, up, down):
    tokens, width = x.shape
    length = seg.shape[1]
    rows = qkv.shape[0]
    own = out.shape[0]
    parts = width // own
    heads = own // HEAD_DIM
    units = up.shape[1] // UNIT
    chunks = 3 * (parts - 1) + EARLY
    wide = HEAD_DIM + EXTRA
    dma = pltpu.SemaphoreType.DMA
    return pl.pallas_call(
        front_kernel,
        in_specs=[WHOLE] * 7 + [ANY] * 3,
        out_specs=[WHOLE] * 2 + [ANY] * 8,
        out_shape=[
            shape_of((parts, 8, width), F32),
            shape_of((8, 128), F32),
            shape_of((tokens, width), BF),
            shape_of((parts * rows, width), BF),
            shape_of((width, width), BF),
            shape_of((parts * rows, tokens), BF),
            shape_of((width, tokens), BF),
            shape_of((16, tokens), F32),
            shape_of((EARLY, 2, width, UNIT), F32),
            shape_of((parts, units, 2, width // 8, UNIT), F32),
        ],
        scratch_shapes=[
            pltpu.VMEM((tokens, width), BF),
            pltpu.VMEM((tokens, width), BF),
            pltpu.VMEM((parts, rows, width), F32),
            pltpu.VMEM((parts, own, width), F32),
            pltpu.VMEM((parts, units, 2, width // 8, UNIT), F32),
            pltpu.VMEM((EARLY, 2, width, UNIT), F32),
            pltpu.VMEM((units, 2, width // 8, UNIT), F32),
            pltpu.VMEM((parts, 8, width), F32),
            pltpu.VMEM((parts, rows, width), BF),
            pltpu.VMEM((width, width), BF),
            pltpu.VMEM((parts, rows, 1), F32),
            pltpu.VMEM((parts * rows, tokens), BF),
            pltpu.VMEM((width, tokens), BF),
            pltpu.VMEM((16, tokens), F32),
            pltpu.VMEM((heads, wide, length), BF),
            pltpu.VMEM((heads, wide, length), BF),
            pltpu.VMEM((heads, wide, length), BF),
            pltpu.VMEM((heads, length, wide), BF),
            dma,
            dma,
            dma((EARLY,)),
            dma((5,)),
            dma((parts, 3)),
            dma((parts, 3 + units)),
            dma((parts, 3 + units)),
            dma((3 + units, 2)),
            dma((parts - 1,)),
            dma((parts,)),
            dma((chunks,)),
            dma((chunks, 3)),
        ],
        compiler_params=pltpu.CompilerParams(vmem_limit_bytes=62 * 2**20, collective_id=0, has_side_effects=True),
        name="front",
    )(gains, shifts, qkv, out, qv_bias, up_bias, seg, x, up, down)


def repair_kernel(
    bound_ref, seg_ref, qkvt_any, ot_in, lse_in, ot_out, lse_out, qx, kx, vx, lse_row, sems,
):
    rows_here, length = seg_ref.shape
    parts = 4
    own = qkvt_any.shape[0] // (3 * parts)
    heads = parts * own // HEAD_DIM
    safe = jnp.max(bound_ref[...]) < SAFE_SCORE**2

    @pl.when(jnp.logical_not(safe))
    def _():
        row = lax.broadcasted_iota(jnp.int32, (EXTRA, length), 0)
        vx[HEAD_DIM:, :] = jnp.ones((EXTRA, length), BF)

        def move(copies):
            copies = [pltpu.make_async_copy(a, b, sems.at[i]) for i, (a, b) in enumerate(copies)]
            for copy in copies:
                copy.start()
            for copy in copies:
                copy.wait()

        def head(i, carry):
            r, h = lax.div(i, heads), lax.rem(i, heads)
            rows = pl.ds(pl.multiple_of(h * HEAD_DIM, HEAD_DIM), HEAD_DIM)
            tokens = pl.ds(pl.multiple_of(r * length, length), length)
            head_at = lax.div(h, heads // parts) * 3 * own + lax.rem(h, heads // parts) * HEAD_DIM
            same = row == seg_ref[pl.ds(r, 1), :]
            qx[HEAD_DIM:, :] = jnp.where(same | (row >= 8), 0.0, -BIG).astype(BF)
            kx[HEAD_DIM:, :] = jnp.where(same, 1.0, 0.0).astype(BF)
            move([
                (
                    qkvt_any.at[pl.ds(pl.multiple_of(head_at + k * own, HEAD_DIM), HEAD_DIM), tokens],
                    target.at[pl.ds(0, HEAD_DIM), :],
                )
                for k, target in enumerate((qx, kx, vx))
            ])

            @pl.when(h == 0)
            def _():
                lse_row[...] = jnp.zeros_like(lse_row)

            for t in range(length // TILE):
                cols = slice(t * TILE, (t + 1) * TILE)
                scores = dot(kx[...], qx[:, cols], TN)
                highest = jnp.max(scores, 0, keepdims=True)
                probs = jnp.exp2((scores - highest) * LOG2E).astype(BF)
                out = dot(vx[...], probs, NN)
                total = out[HEAD_DIM : HEAD_DIM + 1, :]
                qx[:HEAD_DIM, cols] = (out[:HEAD_DIM, :] * (1.0 / total)).astype(BF)
                lse_row[pl.ds(h, 1), cols] = jnp.log(total) + highest
            move([(qx.at[pl.ds(0, HEAD_DIM), :], ot_out.at[rows, tokens])])

            @pl.when(h == heads - 1)
            def _():
                move([(lse_row, lse_out.at[:, tokens])])

            return carry

        lax.fori_loop(0, rows_here * heads, head, 0)


def repair(bound, seg, qkvt, ot, lse):
    length = seg.shape[1]
    return pl.pallas_call(
        repair_kernel,
        in_specs=[WHOLE, WHOLE, ANY, ANY, ANY],
        out_specs=[ANY, ANY],
        out_shape=[shape_of(ot.shape, BF), shape_of(lse.shape, F32)],
        input_output_aliases={3: 0, 4: 1},
        scratch_shapes=[pltpu.VMEM((HEAD_DIM + EXTRA, length), BF)] * 3
        + [pltpu.VMEM((16, length), F32), pltpu.SemaphoreType.DMA((3,))],
        compiler_params=params(),
        name="repair",
    )(bound, seg, qkvt, ot, lse)


def split3(value):
    first = value.astype(BF)
    rest = value - first.astype(F32)
    second = rest.astype(BF)
    return first, second, (rest - second.astype(F32)).astype(BF)


class Total:
    def __init__(self, out, sends, recvs, near=None, side_land=None, across_land=None):
        self.out, self.near = out, near
        self.side_land, self.across_land, self.sends, self.recvs = side_land, across_land, sends, recvs
        self.device = lax.axis_index("dp")
        place = lax.rem(self.device, 8)
        self.half = out.shape[0] // 2
        self.part, self.piece = self.half // 4, self.half // 8
        bits = [lax.rem(lax.div(place, bit), 2) for bit in (1, 2, 4)]
        self.base = bits[0] * self.half
        self.away = (1 - bits[0]) * self.half
        self.one = self.base + bits[1] * self.part
        self.one_away = self.base + (1 - bits[1]) * self.part
        self.two = self.base + 2 * self.part + bits[2] * self.part
        self.two_away = self.base + 2 * self.part + (1 - bits[2]) * self.part
        self.one_piece = self.one + bits[2] * self.piece
        self.one_piece_away = self.one + (1 - bits[2]) * self.piece
        self.two_piece = self.two + bits[1] * self.piece
        self.two_piece_away = self.two + (1 - bits[1]) * self.piece

    def rows(self, start, count):
        return self.out.at[pl.ds(pl.multiple_of(start, 8), count), :]

    def copy(self, sem, bit, src, dst):
        return remote(src, dst, self.sends.at[sem], self.recvs.at[sem], dp=flip(self.device, bit))

    def over(self, sem, bit, start, count):
        ref = self.rows(start, count)
        return self.copy(sem, bit, ref, ref)

    def copies(self, stage):
        part, piece = self.part, self.piece
        first, second = pl.ds(0, part), pl.ds(part, piece)
        if stage == 0:
            return [self.copy(0, 1, self.rows(self.away, self.half), self.near)]
        if stage == 1:
            return [
                self.copy(1, 2, self.rows(self.one_away, part), self.side_land.at[first, :]),
                self.copy(2, 4, self.rows(self.two_away, part), self.across_land.at[first, :]),
            ]
        if stage == 2:
            return [
                self.copy(3, 4, self.rows(self.one_piece_away, piece), self.across_land.at[second, :]),
                self.copy(4, 2, self.rows(self.two_piece_away, piece), self.side_land.at[second, :]),
            ]
        if stage == 3:
            return [self.over(5, 4, self.one_piece, piece), self.over(6, 2, self.two_piece, piece)]
        if stage == 4:
            return self.halves(0, self.one, self.two)
        if stage == 4.5:
            return self.halves(1, self.one, self.two)
        return [self.over(9, 1, self.base, self.half)]

    def halves(self, h, one, two):
        half = self.part // 2
        return [self.over(7 + 3 * h, 2, one + h * half, half), self.over(8 + 3 * h, 4, two + h * half, half)]

    def arrivals(self, stage):
        part, piece = self.part, self.piece
        if stage == 3:
            return [self.over(5, 4, self.one_piece_away, piece), self.over(6, 2, self.two_piece_away, piece)]
        if stage == 4:
            return self.halves(0, self.one_away, self.two_away)
        if stage == 4.5:
            return self.halves(1, self.one_away, self.two_away)
        if stage == 5:
            return [self.over(9, 1, self.away, self.half)]
        return self.copies(stage)

    def add(self, start, ref, at, count):
        step = 48 if count % 48 == 0 else 56

        def some(i, carry):
            rows = pl.ds(pl.multiple_of(start + i * step, 8), step)
            self.out[rows, :] += ref[pl.ds(pl.multiple_of(at + i * step, 8), step), :]
            return carry

        lax.fori_loop(0, count // step, some, 0)

    def finish(self, stage):
        for copy in self.copies(stage):
            copy.wait_send()
        for copy in self.arrivals(stage):
            copy.wait_recv()
        if stage == 0:
            self.add(self.base, self.near, 0, self.half)
        elif stage == 1:
            self.add(self.one, self.side_land, 0, self.part)
            self.add(self.two, self.across_land, 0, self.part)
        elif stage == 2:
            self.add(self.one_piece, self.across_land, self.part, self.piece)
            self.add(self.two_piece, self.side_land, self.part, self.piece)

    def start(self, stage):
        for copy in self.copies(stage):
            copy.start()

    @staticmethod
    def scratch(rows, width):
        dma = pltpu.SemaphoreType.DMA
        return [
            dma((12,)),
            dma((12,)),
            pltpu.VMEM((rows // 2, width), F32),
            pltpu.VMEM((rows // 8 + rows // 16, width), F32),
            pltpu.VMEM((rows // 8 + rows // 16, width), F32),
        ]


def attend_back_kernel(
    seg_ref, qkv_ref, ot_ref, dt_ref, lse_ref, h1_any, main_any, tail_any,
    dqkv_ref, main_out, rest_out,
    qx, kx, vx, dx, qn, dn, kn, acc, h1_ref, part_ref, main_ref, rest_ref, whole_ref, in_sems, out_sems, main_send, main_recv, side_land, across_land,
    *comm,
):
    step = pl.program_id(0)
    own, length = ot_ref.shape
    width = h1_ref.shape[1]
    heads = own // HEAD_DIM
    tail_at = rest_ref.shape[0] - tail_any.shape[0]
    part = Total(part_ref, main_send, main_recv, None, side_land, across_land)
    main = Total(main_ref, main_send, main_recv)
    rest = Total(rest_ref, *comm)
    whole = Total(whole_ref, *comm[:2])
    loads = [
        pltpu.make_async_copy(main_any.at[pl.ds(pl.multiple_of(at, 8), part.part), :], part.rows(at, part.part), sem)
        for at, sem in ((part.one, in_sems.at[0]), (part.two, in_sems.at[1]))
    ]
    loads.append(pltpu.make_async_copy(tail_any, rest_ref.at[pl.ds(tail_at, tail_any.shape[0]), :], in_sems.at[2]))
    loads.append(pltpu.make_async_copy(h1_any, h1_ref, in_sems.at[3]))
    stores = [
        pltpu.make_async_copy(main_ref, main_out, out_sems.at[0]),
        pltpu.make_async_copy(whole_ref, rest_out, out_sems.at[1]),
    ]

    @pl.when(step == 0)
    def _():
        for copy in loads:
            copy.start()
        greet(*[{"dp": flip(main.device, bit)} for bit in (1, 2, 4)])
        for copy in loads[:2]:
            copy.wait()
        part.start(2)

    @pl.when(step == 1)
    def _():
        part.finish(2)
        for at in (part.one_piece, part.two_piece):
            rows = pl.ds(pl.multiple_of(at, 8), part.piece)
            main_ref[rows, :] = part_ref[rows, :]
        main.start(3)

    @pl.when(step == 2)
    def _():
        main.finish(3)
        main.start(4)

    @pl.when(step == 3)
    def _():
        rest.finish(0)
        rest.start(1)

    @pl.when(step == 4)
    def _():
        rest.finish(1)
        rest.start(2)
        main.finish(4)
        main.start(4.5)

    @pl.when(step == 5)
    def _():
        rest.finish(2)
        for at in (rest.one_piece, rest.two_piece):
            rows = pl.ds(pl.multiple_of(at, 8), rest.piece)
            whole_ref[rows, :] = rest_ref[rows, :]
        whole.start(3)

    @pl.when(step == 6)
    def _():
        whole.finish(3)
        whole.start(4)
        whole.start(4.5)
        main.finish(4.5)
        main.start(5)

    @pl.when(step == 7)
    def _():
        whole.finish(4)
        whole.finish(4.5)
        whole.start(5)
        main.finish(5)
        stores[0].start()

    row = lax.broadcasted_iota(jnp.int32, (EXTRA, length), 0)
    same = row == seg_ref[pl.ds(jnp.where((step == 1) | (step >= 5), 1, 0), 1), :]
    key_extra = jnp.where(same | ((row >= 8) & (row < 11)), 1.0, 0.0).astype(BF)
    value_extra = jnp.where(row < 3, 1.0, 0.0).astype(BF)
    query_extra = jnp.where(same | (row >= 8), 0.0, -BIG)

    def three_rows(value, at):
        first, second, third = split3(value)
        out = jnp.where(row == at, first.astype(F32), 0.0)
        out = jnp.where(row == at + 1, second.astype(F32), out)
        return jnp.where(row == at + 2, third.astype(F32), out)

    head_at = jnp.where(step < 2, 0, lax.rem(step - 2, 3) + 1) * heads

    def head(u):
        rows = slice(u * HEAD_DIM, (u + 1) * HEAD_DIM)
        dq_rows, dk_rows, dv_rows = (slice(rows.start + k * own, rows.stop + k * own) for k in range(3))
        qx[u, :HEAD_DIM, :] = qkv_ref[dq_rows, :]
        kx[u, :HEAD_DIM, :] = qkv_ref[dk_rows, :]
        vx[u, :HEAD_DIM, :] = qkv_ref[dv_rows, :]
        dx[u, :HEAD_DIM, :] = dt_ref[rows, :]
        inner = jnp.sum(dt_ref[rows, :].astype(F32) * ot_ref[rows, :].astype(F32), 0, keepdims=True)
        log_sum = lse_ref[pl.ds(head_at + u, 1), :]
        qx[u, HEAD_DIM:, :] = (query_extra + three_rows(-log_sum, 8)).astype(BF)
        kx[u, HEAD_DIM:, :] = key_extra
        vx[u, HEAD_DIM:, :] = value_extra
        dx[u, HEAD_DIM:, :] = three_rows(-inner, 0).astype(BF)
        qn[u] = qx[u].T
        dn[u] = dx[u].T
        kn[u] = kx[u].T
        for t in range(length // TILE):
            low, high = max(0, t * TILE - REACH), min(length, (t + 1) * TILE + REACH)
            keys = slice(t * TILE, (t + 1) * TILE)
            probs, score_grads = [], []
            for q in range(low, high, TILE):
                prob = jnp.exp2(dot(qn[u, q : q + TILE, :], kx[u, :, keys], NN) * LOG2E)
                prob_grad = dot(dn[u, q : q + TILE, :], vx[u, :, keys], NN)
                probs.append(prob.astype(BF))
                score_grads.append((prob * prob_grad).astype(BF))
            probs = jnp.concatenate(probs, 0)
            score_grads = jnp.concatenate(score_grads, 0)
            dqkv_ref[dv_rows, keys] = dot(dx[u, :HEAD_DIM, low:high], probs, NN).astype(BF)
            dqkv_ref[dk_rows, keys] = dot(qx[u, :HEAD_DIM, low:high], score_grads, NN).astype(BF)
            part = dot(score_grads, kx[u, :HEAD_DIM, keys], NT)
            if t == 0:
                acc[u, low:high, :] = part
                if high < length:
                    acc[u, high:, :] = jnp.zeros((length - high, HEAD_DIM), F32)
            else:
                acc[u, low:high, :] += part
        dqkv_ref[dq_rows, :] = (acc[u] * HEAD_DIM**-0.5).T.astype(BF)

    for u in range(heads):
        head(u)

    def own_grads(tokens, add):
        part = dot(dqkv_ref[...], h1_ref[tokens, :], NN)
        rest_ref[: 3 * own, :] = rest_ref[: 3 * own, :] + part if add else part
        ones = jnp.ones((8, length), BF)
        for k in (0, 2):
            rows = slice(3 * own + k * 4, 3 * own + k * 4 + 8)
            part = dot(ones, dqkv_ref[k * own : (k + 1) * own, :], NT)
            rest_ref[rows, :own] = rest_ref[rows, :own] + part if add else part

    @pl.when(step == 0)
    def _():
        rest_ref[3 * own : tail_at, :] = jnp.zeros((tail_at - 3 * own, width), F32)
        loads[3].wait()
        own_grads(slice(0, length), False)

    @pl.when(step == 1)
    def _():
        own_grads(slice(length, 2 * length), True)
        loads[2].wait()
        rest.start(0)

    @pl.when(step == 7)
    def _():
        whole.finish(5)
        stores[1].start()
        for copy in stores:
            copy.wait()


def attend_back(seg, qkvt, ot, dt, lse, h1, main, tail):
    width, tokens = ot.shape
    _, length = seg.shape
    own = width // 4
    heads = own // HEAD_DIM
    wide = HEAD_DIM + EXTRA
    rest_rows = 3 * own + 64 + tail.shape[0]
    row_of = lambda s: jnp.where((s == 1) | (s >= 5), 1, 0)
    part_of = lambda s: jnp.where(s < 2, 0, lax.rem(s - 2, 3) + 1)
    block = pl.BlockSpec((own, length), lambda s: (part_of(s), row_of(s)))
    wide_block = pl.BlockSpec((3 * own, length), lambda s: (part_of(s), row_of(s)))
    dma = pltpu.SemaphoreType.DMA
    return pl.pallas_call(
        attend_back_kernel,
        grid=(8,),
        in_specs=[ONCE, wide_block, block, block]
        + [pl.BlockSpec((16, length), lambda s: (0, row_of(s))), ANY, ANY, ANY],
        out_specs=[wide_block, ANY, ANY],
        out_shape=[shape_of(qkvt.shape, BF), shape_of(main.shape, F32), shape_of((rest_rows, width), F32)],
        scratch_shapes=[pltpu.VMEM((heads, wide, length), BF)] * 4
        + [pltpu.VMEM((heads, length, wide), BF)] * 3
        + [
            pltpu.VMEM((heads, length, HEAD_DIM), F32),
            pltpu.VMEM((tokens, width), BF),
            pltpu.VMEM(main.shape, F32),
            pltpu.VMEM(main.shape, F32),
            pltpu.VMEM((rest_rows, width), F32),
            pltpu.VMEM((rest_rows, width), F32),
            dma((4,)),
            dma((2,)),
            dma((12,)),
            dma((12,)),
            pltpu.VMEM((main.shape[0] // 8 + main.shape[0] // 16, width), F32),
            pltpu.VMEM((main.shape[0] // 8 + main.shape[0] // 16, width), F32),
        ]
        + Total.scratch(rest_rows, width),
        compiler_params=pltpu.CompilerParams(vmem_limit_bytes=60 * 2**20, collective_id=2, has_side_effects=True),
        name="attend_back",
    )(seg, qkvt, ot, dt, lse, h1, main, tail)


def token_kernel(
    dqkv_ref, w_ref, x_ref, mg_ref, gain_ref, main_any, rest_any, result_any,
    tg_ref, sums_ref, down_ref, up_ref, out_ref, result_ref, qkv_ref,
    main_v, rest_v, result_v, in_sems, out_sems,
):
    step = pl.program_id(0)
    last = pl.num_programs(0) - 1
    ff = down_ref.shape[0]
    own = out_ref.shape[0]
    out_at = 3 * own + 64
    loads = [
        pltpu.make_async_copy(source, target, in_sems.at[i])
        for i, (source, target) in enumerate(((rest_any, rest_v), (main_any, main_v), (result_any, result_v)))
    ]
    stores = [
        pltpu.make_async_copy(source, target, out_sems.at[i])
        for i, (source, target) in enumerate((
            (main_v.at[pl.ds(0, ff), :], down_ref),
            (main_v.at[pl.ds(ff, up_ref.shape[0]), :], up_ref),
            (rest_v.at[pl.ds(out_at, own), :], out_ref),
            (result_v, result_ref),
            (rest_v.at[pl.ds(0, 3 * own), :], qkv_ref),
        ))
    ]

    @pl.when(step == 0)
    def _():
        for copy in loads:
            copy.start()
        sums_ref[...] = jnp.zeros_like(sums_ref)

    @pl.when(step == last - 1)
    def _():
        for copy in loads:
            copy.wait()
        for copy in stores:
            copy.start()

    hg = dot(dqkv_ref[...], w_ref[...], TN)
    normed, inv_std = standardize(x_ref[...].astype(F32))
    tg_ref[...] = mg_ref[...] + norm_back(hg, normed, inv_std, gain_ref[0:1, :])
    sums_ref[0:1, :] += jnp.sum(hg * normed, 0, keepdims=True)
    sums_ref[1:2, :] += jnp.sum(hg, 0, keepdims=True)

    @pl.when(step == last)
    def _():
        for copy in stores:
            copy.wait()


def token_back(dqkv, weights, x, mg, gains, main, rest, result, ff, own):
    tokens, width = x.shape
    row = pl.BlockSpec((LONG_TILE, width), lambda t: (t, 0))
    col = pl.BlockSpec((weights.shape[0], LONG_TILE), lambda t: (0, t))
    dma = pltpu.SemaphoreType.DMA
    return pl.pallas_call(
        token_kernel,
        grid=(tokens // LONG_TILE,),
        in_specs=[col, ONCE, row, row, ONCE, ANY, ANY, ANY],
        out_specs=[row, ONCE, ANY, ANY, ANY, ANY, ANY],
        out_shape=[
            shape_of((tokens, width), F32),
            shape_of((8, width), F32),
            shape_of((ff, width), F32),
            shape_of((width, ff), F32),
            shape_of((own, width), F32),
            shape_of((tokens, width), BF),
            shape_of((3 * own, width), F32),
        ],
        scratch_shapes=[
            pltpu.VMEM(main.shape, F32),
            pltpu.VMEM(rest.shape, F32),
            pltpu.VMEM((tokens, width), BF),
            dma((3,)),
            dma((5,)),
        ],
        compiler_params=params(),
        name="token_back",
    )(dqkv, weights, x, mg, gains, main, rest, result)


def sums_kernel(in_ref, out_ref, land, sends, recvs):
    device = lax.axis_index("dp")
    place = lax.rem(device, 8)
    others = []
    for bits in range(1, 8):
        other = device
        for bit in (1, 2, 4):
            if bits & bit:
                other = flip(other, bit)
        others.append(other)
    greet(*[{"dp": other} for other in others])
    copies = [
        remote(in_ref, land.at[place], sends.at[i], recvs.at[place], dp=other) for i, other in enumerate(others)
    ]
    for copy in copies:
        copy.start()
    land[place] = in_ref[...]
    for other in others:
        peer = lax.rem(other, 8)
        remote(in_ref, land.at[peer], sends.at[0], recvs.at[peer], dp=other).wait_recv()
    out_ref[...] = jnp.sum(land[...], 0)
    for copy in copies:
        copy.wait_send()


def add_sums(sums):
    dma = pltpu.SemaphoreType.DMA
    return pl.pallas_call(
        sums_kernel,
        in_specs=[WHOLE],
        out_specs=WHOLE,
        out_shape=shape_of(sums.shape, F32),
        scratch_shapes=[pltpu.VMEM((8,) + sums.shape, F32), dma((7,)), dma((8,))],
        compiler_params=pltpu.CompilerParams(collective_id=3, has_side_effects=True),
        name="add_sums",
    )(sums)


def arrange_kernel(sums_ref, rest_any, gains_ref, shifts_ref, biases_ref, qv_bias_ref, up_bias_ref, rows_v, sems, *, own):
    loads = [
        pltpu.make_async_copy(rest_any.at[pl.ds(low, 16), :], rows_v.at[i], sems.at[i])
        for i, low in enumerate((3 * own, 4 * own + 64))
    ]
    for copy in loads:
        copy.start()
    gains_ref[0:1, :] = sums_ref[0:1, :]
    shifts_ref[0:1, :] = sums_ref[1:2, :]
    for copy in loads:
        copy.wait()
    gains_ref[1:2, :] = rows_v[1, GAIN_TWO : GAIN_TWO + 1, :]
    shifts_ref[1:2, :] = rows_v[1, SHIFT_TWO : SHIFT_TWO + 1, :]
    biases_ref[...] = rows_v[1, BIAS_ONE : BIAS_TWO + 1, :]
    up_bias_ref[...] = rows_v[1, UP_BIAS, :]
    qv_bias_ref[0:1, :] = rows_v[0, 0:1, :own]
    qv_bias_ref[1:2, :] = rows_v[0, 8:9, :own]


def arrange(sums, rest, own):
    width = sums.shape[1]
    return pl.pallas_call(
        partial(arrange_kernel, own=own),
        in_specs=[WHOLE, ANY],
        out_specs=[WHOLE] * 5,
        out_shape=[shape_of((2, width), F32)] * 3 + [shape_of((2, own), F32), shape_of((width,), F32)],
        scratch_shapes=[pltpu.VMEM((2, 16, width), F32), pltpu.SemaphoreType.DMA((2,))],
        name="arrange",
    )(sums, rest)


GELU_C = 0.7978845608028654
GELU_A = 0.044715


def gelu_both(pre):
    square = pre * pre
    half = 0.5 + 0.5 * jnp.tanh(pre * (GELU_C + (GELU_C * GELU_A) * square))
    act = pre * half
    slope = half + act * (1.0 - half) * (2.0 * GELU_C + (6.0 * GELU_C * GELU_A) * square)
    return act, slope


GAIN_TWO, SHIFT_TWO, BIAS_ONE, BIAS_TWO, UP_BIAS = range(5)


def mlp_kernel(
    wo_ref, smalls_ref, bias_ref, gain_ref, shift_ref, x_any, ot_any, g_any, up_any, down_any, land_any, z_any,
    result_out, mg_out, dt_out, main_out, tail_out,
    land, z_far, wide_w, own_w, g_ref, h2_ref, dt_ref, mine_ref, main_ref, tail_ref, normed_ref, inv_ref, res_ref, hg_ref,
    up_low, down_low, pre_s, ag_s,
    in_sems, w_sems, keep_sems, far_keep, far_send, far_recv, out_sems, tile_sems, send_sems, recv_sems, *comm,
):
    tokens, width = g_ref.shape
    parts = smalls_ref.shape[0]
    own = mine_ref.shape[0]
    ff = up_any.shape[1]
    units = ff // UNIT
    chunks = units * (parts - 1)
    late = land.shape[0]
    early = chunks - late
    share = z_any.shape[3]
    strip = UNIT // 8
    tiles = tokens // TILE
    me = lax.axis_index("mp")
    order = foreign_order(me)
    total = Total(main_ref, *comm)

    def source_of(c):
        j = lax.div(c, units)
        return jnp.where(j == 0, order[0], jnp.where(j == 1, order[1], order[2]))

    def pieces_at(e, at, count, half):
        rows = pl.ds(pl.multiple_of(at * share, 8), count * share)
        if half is None:
            return land.at[e, :, rows, :]
        return land.at[e, half, rows, :]

    spread = Spread(pieces_at, send_sems, recv_sems)
    far_at = units - early
    far_count = units * (parts - 2)

    def mine(e):
        return z_any.at[order[(early + e) // units], (early + e) % units]

    inner = (me > 0) & (me < parts - 1)

    def far_source(u):
        return z_any.at[jnp.where(u < units, order[1], order[2]), lax.rem(u, units)]

    def far_copy(u):
        step = jnp.where(lax.div(me, 2) == 0, -1, 1)
        return remote(far_source(u), z_far.at[u], far_send.at[u], far_recv.at[u], mp=me + step)

    def far_local(u):
        return pltpu.make_async_copy(far_source(u), z_far.at[u], far_keep.at[u])

    def far(u):
        @pl.when(inner)
        def _():
            far_local(u).wait()

        @pl.when(jnp.logical_not(inner))
        def _():
            remote(z_far.at[u], z_far.at[u], far_send.at[u], far_recv.at[u], mp=me).wait_recv()

    def keep(e, source):
        return pltpu.make_async_copy(source, pieces_at(e, spread.at, 1, None), keep_sems.at[e])

    def send(e):
        @pl.when((e >= far_at) & (e < late))
        def _():
            far(e - far_at)
            keep(e, z_far.at[e - far_at]).start()

        @pl.when(e < late)
        def _():
            keep(e, z_far.at[0]).wait()
            spread.send(e)

    def serve(n):
        @pl.when(n - 1 < late)
        def _():
            spread.forward(n - 1)

        send(n + 1)

        @pl.when((n > 2) & (n - 3 < late))
        def _():
            spread.corner(n - 3)

    def reduce(n):
        @pl.when(n == units)
        def _():
            total.start(0)

        @pl.when(n == units + 7)
        def _():
            total.finish(0)
            total.start(1)

    def unit(bias, grads_at):
        def front(i):
            rows = slice(i * TILE, (i + 1) * TILE)
            pre_s[i % 2] = dot(h2_ref[rows, :], up_low[...], NN) + bias
            ag_s[i % 2] = dot(g_ref[rows, :], down_low[...], NT)

        def back(i):
            rows = slice(i * TILE, (i + 1) * TILE)
            act, slope = gelu_both(pre_s[i % 2])
            act = act.astype(BF)
            pre_grad = (ag_s[i % 2] * slope).astype(BF)
            res_ref[rows, :] += dot(act, down_low[...], NN)
            hg_ref[rows, :] += dot(pre_grad, up_low[...], NT)
            if grads_at is not None:
                h2 = h2_ref[rows, :]
                g = g_ref[rows, :]
                cols = pl.ds(pl.multiple_of(grads_at, UNIT), UNIT)
                main_ref[cols, :] += dot(act, g, TN)
                main_ref[ff:, cols] += dot(h2, pre_grad, TN)
                at = own + UP_BIAS
                tail_ref[at : at + 1, cols] += jnp.sum(pre_grad.astype(F32), 0, keepdims=True)

        front(0)
        for i in range(tiles):
            if i + 1 < tiles:
                front(i + 1)
            back(i)

    loads = [
        pltpu.make_async_copy(source, target, in_sems.at[i])
        for i, (source, target) in enumerate(((ot_any, dt_ref), (x_any, h2_ref), (g_any, g_ref)))
    ]

    def own_load(u):
        cols = pl.ds(pl.multiple_of(u * UNIT, UNIT), UNIT)
        return [
            pltpu.make_async_copy(up_any.at[:, cols], wide_w.at[0], w_sems.at[0]),
            pltpu.make_async_copy(down_any.at[cols, :], own_w, w_sems.at[1]),
        ]

    def chunk_load(c):
        return pltpu.make_async_copy(land_any.at[c], wide_w, w_sems.at[0])

    for copy in loads:
        copy.start()
    for copy in own_load(0):
        copy.start()
    for e in range(far_at):
        keep(e, mine(e)).start()

    @pl.when(inner)
    def _():
        for u in range(far_count):
            far_local(u).start()

    greet(
        *[{"mp": lax.rem(me + s, parts)} for s in range(1, parts)],
        *[{"dp": flip(spread.device, bit)} for bit in (1, 2, 4)],
    )

    @pl.when(inner)
    def _():
        for u in range(far_count):
            far_copy(u).start()

    send(0)
    send(1)
    main_ref[...] = jnp.zeros_like(main_ref)
    tail_ref[...] = jnp.zeros_like(tail_ref)
    for copy in loads[:2]:
        copy.wait()
    mine_ref[...] = dt_ref[:own, :]

    def first(i, carry):
        rows = pl.ds(pl.multiple_of(i * TILE, TILE), TILE)
        mixed = h2_ref[rows, :].astype(F32) + dot(dt_ref[:, rows], wo_ref[...], TN) + bias_ref[0:1, :]
        res_ref[rows, :] = mixed + bias_ref[1:2, :]
        hg_ref[rows, :] = jnp.zeros((TILE, width), F32)
        normed, inv_std = standardize(mixed)
        normed_ref[rows, :] = normed
        inv_ref[rows, :] = inv_std
        h2_ref[rows, :] = (normed * gain_ref[1:2, :] + shift_ref[1:2, :]).astype(BF)
        return carry

    lax.fori_loop(0, tiles, first, 0, unroll=2)
    serve(1)
    loads[2].wait()

    def own_unit(u, carry):
        for copy in own_load(u):
            copy.wait()
        up_low[...] = wide_w[0].astype(BF)
        down_low[...] = own_w[...].astype(BF)

        @pl.when(u + 1 < units)
        def _():
            for copy in own_load(u + 1):
                copy.start()

        @pl.when(u + 1 == units)
        def _():
            chunk_load(0).start()

        unit(smalls_ref[me, 2:3, pl.ds(pl.multiple_of(u * UNIT, UNIT), UNIT)], u * UNIT)
        serve(u + 2)
        reduce(u + 1)
        return carry

    lax.fori_loop(0, units, own_unit, 0)

    def take(ref, at):
        up_low[...] = ref[at + (0,)].astype(BF)
        for q in range(8):
            for k in range(width // UNIT):
                low = q * share + k * strip
                down_low[q * strip : (q + 1) * strip, k * UNIT : (k + 1) * UNIT] = ref[
                    at + (1, slice(low, low + strip))
                ].astype(BF)

    def foreign_unit(c, carry):
        @pl.when(c < early)
        def _():
            chunk_load(c).wait()
            take(wide_w, ())

        @pl.when(c + 1 < early)
        def _():
            chunk_load(c + 1).start()

        @pl.when(c >= early)
        def _():
            e = c - early
            spread.complete(e)
            take(land, (e,))

        cols = pl.ds(pl.multiple_of(lax.rem(c, units) * UNIT, UNIT), UNIT)
        unit(smalls_ref[source_of(c), 2:3, cols], None)
        serve(c + units + 2)
        reduce(c + units + 1)
        return carry

    lax.fori_loop(0, chunks, foreign_unit, 0)

    def tile_stores(i):
        rows = pl.ds(pl.multiple_of(i * TILE, TILE), TILE)
        return [
            pltpu.make_async_copy(source, target, tile_sems.at[k])
            for k, (source, target) in enumerate((
                (h2_ref.at[rows, :], result_out.at[rows, :]),
                (hg_ref.at[rows, :], mg_out.at[rows, :]),
                (dt_ref.at[:, rows], dt_out.at[:, rows]),
            ))
        ]

    def finish(i, carry):
        rows = pl.ds(pl.multiple_of(i * TILE, TILE), TILE)
        g = g_ref[rows, :].astype(F32)
        h2_ref[rows, :] = res_ref[rows, :].astype(BF)
        normed, inv_std = normed_ref[rows, :], inv_ref[rows, :]
        hg = hg_ref[rows, :]
        mg = g + norm_back(hg, normed, inv_std, gain_ref[1:2, :])
        hg_ref[rows, :] = mg
        low = mg.astype(BF)
        dt_ref[:, rows] = dot(wo_ref[...], low, NT).astype(BF)
        tail_ref[:own, :] += dot(mine_ref[:, rows], low, NN)
        for at, value in ((GAIN_TWO, hg * normed), (SHIFT_TWO, hg), (BIAS_ONE, mg), (BIAS_TWO, g)):
            tail_ref[own + at : own + at + 1, :] += jnp.sum(value, 0, keepdims=True)
        for copy in tile_stores(i):
            copy.start()
        return carry

    lax.fori_loop(0, tiles, finish, 0, unroll=2)
    total.finish(1)
    ends = [
        pltpu.make_async_copy(total.rows(at, total.part), main_out.at[pl.ds(pl.multiple_of(at, 8), total.part), :], sem)
        for at, sem in ((total.one, out_sems.at[0]), (total.two, out_sems.at[1]))
    ]
    ends.append(pltpu.make_async_copy(tail_ref, tail_out, out_sems.at[2]))
    for copy in ends:
        copy.start()
    for e in range(late):
        spread.sent(e)

    @pl.when(inner)
    def _():
        for u in range(far_count):
            far_copy(u).wait_send()

    for k, ref in enumerate((h2_ref, hg_ref, dt_ref)):
        pltpu.make_async_copy(ref, ref, tile_sems.at[k]).wait()
    for copy in ends:
        copy.wait()


def mlp(x, ot, wo, g, up, down, smalls, biases, gains, shifts, land, z):
    tokens, width = x.shape
    parts = smalls.shape[0]
    own = width // parts
    ff = up.shape[1]
    units = ff // UNIT
    chunks = units * (parts - 1)
    late = chunks - land.shape[0]
    tiles = tokens // TILE
    rows = 2 * ff
    tail = own + 64
    dma = pltpu.SemaphoreType.DMA
    return pl.pallas_call(
        mlp_kernel,
        in_specs=[WHOLE] * 5 + [ANY] * 7,
        out_specs=[ANY] * 5,
        out_shape=[
            shape_of((tokens, width), BF),
            shape_of((tokens, width), F32),
            shape_of((width, tokens), BF),
            shape_of((rows, width), F32),
            shape_of((tail, width), F32),
        ],
        scratch_shapes=[
            pltpu.VMEM((late, 2, width, UNIT), F32),
            pltpu.VMEM((units * (parts - 2), 2, width // 8, UNIT), F32),
            pltpu.VMEM((2, width, UNIT), F32),
            pltpu.VMEM((UNIT, width), F32),
            pltpu.VMEM((tokens, width), BF),
            pltpu.VMEM((tokens, width), BF),
            pltpu.VMEM((width, tokens), BF),
            pltpu.VMEM((own, tokens), BF),
            pltpu.VMEM((rows, width), F32),
            pltpu.VMEM((tail, width), F32),
            pltpu.VMEM((tokens, width), F32),
            pltpu.VMEM((tokens, 1), F32),
            pltpu.VMEM((tokens, width), F32),
            pltpu.VMEM((tokens, width), F32),
            pltpu.VMEM((width, UNIT), BF),
            pltpu.VMEM((UNIT, width), BF),
            pltpu.VMEM((2, TILE, UNIT), F32),
            pltpu.VMEM((2, TILE, UNIT), F32),
            dma((3,)),
            dma((2,)),
            dma((late,)),
            dma((units * (parts - 2),)),
            dma((units * (parts - 2),)),
            dma((units * (parts - 2),)),
            dma((3,)),
            dma((3,)),
            dma((late,)),
            dma((late, 3)),
        ]
        + Total.scratch(rows, width),
        compiler_params=pltpu.CompilerParams(vmem_limit_bytes=63 * 2**20, collective_id=1, has_side_effects=True),
        name="mlp",
    )(wo, smalls, biases, gains, shifts, x, ot, g, up, down, land, z)


def body(
    dp_size,
    tokens,
    segments,
    norm_gains,
    norm_shifts,
    qkv_weight,
    qv_bias,
    out_weight,
    out_biases,
    up_weight,
    up_bias,
    down_weight,
    cotangent,
):
    width = tokens.shape[1]
    own = qkv_weight.shape[2]
    ff = up_weight.shape[1]
    smalls, bound, h1, weights, wo, qkvt, ot, lse, land, z = front(
        tokens, segments, norm_gains, norm_shifts, qkv_weight.transpose(0, 2, 1).reshape(3 * own, width), out_weight,
        qv_bias, up_bias, up_weight, down_weight,
    )
    ot, lse = repair(bound, segments, qkvt, ot, lse)
    result, mg, dt, main, tail = mlp(
        tokens, ot, wo, cotangent, up_weight, down_weight, smalls, out_biases, norm_gains, norm_shifts, land, z
    )
    dqkv, main, rest = attend_back(segments, qkvt, ot, dt, lse, h1, main, tail)
    if dp_size > 8:
        main, rest = (value / 8 for value in lax.psum((main, rest), "dp"))
    token_grad, sums_one, down_grad, up_grad, out_weight_grad, result, qkv_grad = token_back(
        dqkv, weights, tokens, mg, norm_gains, main, rest, result, ff, own
    )
    sums_one = add_sums(sums_one)
    if dp_size > 8:
        sums_one = lax.psum(sums_one, "dp") / 8
    gains_grad, shifts_grad, out_biases_grad, qv_bias_grad, up_bias_grad = arrange(sums_one, rest, own)
    return (
        result,
        token_grad,
        gains_grad,
        shifts_grad,
        qkv_grad.reshape(3, own, width).transpose(0, 2, 1),
        qv_bias_grad,
        out_weight_grad,
        out_biases_grad,
        up_grad,
        up_bias_grad,
        down_grad,
    )


def solution(mesh):
    in_specs = (
        P("dp", None),
        P("dp", None),
        P(),
        P(),
        P(None, None, "mp"),
        P(None, "mp"),
        P("mp", None),
        P(),
        P(None, "mp"),
        P("mp"),
        P("mp", None),
        P("dp", None),
    )
    out_specs = (
        P("dp", None),
        P("dp", None),
        P(),
        P(),
        P(None, None, "mp"),
        P(None, "mp"),
        P("mp", None),
        P(),
        P(None, "mp"),
        P("mp"),
        P("mp", None),
    )
    return jax.shard_map(
        partial(body, mesh.shape["dp"]), mesh=mesh, in_specs=in_specs, out_specs=out_specs, check_vma=False
    )
```

```python
from functools import partial

import jax
import jax.numpy as jnp
from jax import lax
from jax.experimental import pallas as pl
from jax.experimental.pallas import tpu as pltpu
from jax.sharding import PartitionSpec as P

F32 = jnp.float32
BF = jnp.bfloat16
HEAD_DIM = 64
NORM_EPSILON = 1e-06
BIG = 1e30
LOG2E = 1.4426950408889634
SAFE_SCORE = 60.0
REACH = 512
TILE = 256
LONG_TILE = 512
EXTRA = 16
UNIT = 256
EARLY = 1

NN = (((1,), (0,)), ((), ()))
NT = (((1,), (1,)), ((), ()))
TN = (((0,), (0,)), ((), ()))
WHOLE = pl.BlockSpec(memory_space=pltpu.VMEM)
ONCE = pl.BlockSpec(memory_space=pltpu.VMEM, pipeline_mode=pl.Buffered(1))
ANY = pl.BlockSpec(memory_space=pl.ANY)


def dot(left, right, dims):
    return lax.dot_general(left, right, dims, preferred_element_type=F32)


def params(mib=56):
    return pltpu.CompilerParams(vmem_limit_bytes=mib * 2**20)


def standardize(values):
    centered = values - jnp.mean(values, -1, keepdims=True)
    inv_std = lax.rsqrt(jnp.mean(centered * centered, -1, keepdims=True) + NORM_EPSILON)
    return centered * inv_std, inv_std


def norm_back(grad_in, normed, inv_std, gain):
    scaled = grad_in * gain
    return inv_std * (
        scaled
        - jnp.mean(scaled, -1, keepdims=True)
        - normed * jnp.mean(scaled * normed, -1, keepdims=True)
    )


def shape_of(shape, dtype):
    return jax.ShapeDtypeStruct(shape, dtype)


def flip(index, bit):
    return index + bit - 2 * bit * lax.rem(lax.div(index, bit), 2)


def remote(src, dst, send_sem, recv_sem, **where):
    return pltpu.make_async_remote_copy(
        src_ref=src, dst_ref=dst, send_sem=send_sem, recv_sem=recv_sem, device_id=where,
        device_id_type=pl.DeviceIdType.MESH,
    )


SIDE, ACROSS, DIAG_A, DIAG_B, CORE = range(5)
NEAR, CORNER, OTHER = range(3)


def position(device):
    place = lax.rem(device, 8)
    return lax.rem(place, 2) * 4 + lax.div(place, 2)


class Spread:
    def __init__(self, pieces, send_sems, recv_sems, mine=None):
        self.pieces, self.send_sems, self.recv_sems, self.mine = pieces, send_sems, recv_sems, mine
        self.device = lax.axis_index("dp")
        self.at = position(self.device)
        self.side, self.across = flip(self.at, 1), flip(self.at, 2)
        self.corner_at = flip(self.side, 2)
        self.core = lax.div(self.at, 4) * 4

    def copy(self, chunk, kind, src=None):
        at, count, half, bit, arrival = {
            SIDE: (self.at, 1, None, 2, NEAR),
            ACROSS: (self.at, 1, None, 4, NEAR),
            DIAG_A: (self.side, 1, 0, 4, CORNER),
            DIAG_B: (self.across, 1, 1, 2, CORNER),
            CORE: (self.core, 4, None, 1, OTHER),
        }[kind]
        dst = self.pieces(chunk, at, count, half)
        return remote(
            dst if src is None else src, dst, self.send_sems.at[chunk], self.recv_sems.at[chunk, arrival],
            dp=flip(self.device, bit),
        )

    def arrived(self, chunk, arrival, count):
        ref = self.pieces(chunk, 0, count, None)
        remote(ref, ref, self.send_sems.at[chunk], self.recv_sems.at[chunk, arrival], dp=self.device).wait_recv()

    def send(self, chunk):
        src = None if self.mine is None else self.mine(chunk)
        for kind in (SIDE, ACROSS):
            self.copy(chunk, kind, src).start()

    def forward(self, chunk):
        self.arrived(chunk, NEAR, 2)
        for kind in (DIAG_A, DIAG_B):
            self.copy(chunk, kind).start()

    def corner(self, chunk):
        self.arrived(chunk, CORNER, 1)
        self.copy(chunk, CORE).start()

    def complete(self, chunk):
        self.arrived(chunk, OTHER, 4)

    def sent(self, chunk):
        ref = self.pieces(chunk, 0, 7, None)
        remote(ref, ref, self.send_sems.at[chunk], self.recv_sems.at[chunk, 0], dp=self.device).wait_send()


def greet(*peers):
    barrier = pltpu.get_barrier_semaphore()
    for peer in peers:
        pl.semaphore_signal(barrier, inc=1, device_id=peer, device_id_type=pl.DeviceIdType.MESH)
    pl.semaphore_wait(barrier, len(peers))


def foreign_order(me):
    half = lax.div(me, 2)
    return flip(me, 1), 2 - half, 3 - 3 * half


def front_kernel(
    gain_ref, shift_ref, qkv_ref, out_ref, qv_bias_ref, up_bias_ref, seg_ref, x_any, up_any, down_any,
    smalls_ref, bound_ref, h1_out, w_out, wo_out, qkvt_out, ot_out, lse_out, land_out, z_out,
    x_in, h1_ref, land, wo_land, z_land, mlp_land, pieces, small_land, w_low, wo_low, bias_col,
    qkvt_ref, ot_ref, lse_ref, qx, kx, vx, kn,
    x_sem, piece_sem, keep_sems, out_sems, slice_sems, z_send, z_recv, own_send, small_send, small_recv,
    send_sems, recv_sems,
):
    parts, rows, width = land.shape
    own = out_ref.shape[0]
    heads = own // HEAD_DIM
    tokens = x_in.shape[0]
    length = seg_ref.shape[1]
    units = pieces.shape[0]
    items = 3 + units
    early = mlp_land.shape[0]
    share, out_share, mlp_share = rows // 8, own // 8, width // 8
    split = (0, share // 16 * 8 + 8, share)
    strip = UNIT // 8
    me = lax.axis_index("mp")
    device = lax.axis_index("dp")
    order = foreign_order(me)
    out_chunk, mlp_chunk = 2 * (parts - 1), 3 * (parts - 1)

    def some_rows(start, size, at, count, half):
        low, high = 0, count * size
        if half is not None:
            middle = (size + 8) // 16 * 8
            low, high = (0, middle) if half == 0 else (middle, size)
        return pl.ds(pl.multiple_of(start + at * size + low, 8), high - low)

    def slab_rows(h, at, count=1, half=None):
        return some_rows(split[h] * 8, split[h + 1] - split[h], at, count, half)

    def out_rows(at, count=1, half=None):
        return some_rows(0, out_share, at, count, half)

    def pieces_at(c, at, count, half):
        if c < out_chunk:
            return land.at[order[c // 2], slab_rows(c % 2, at, count, half), :]
        if c < mlp_chunk:
            return wo_land.at[order[c - out_chunk], out_rows(at, count, half), :]
        rows = some_rows(0, mlp_share, at, count, None)
        if half is None:
            return mlp_land.at[c - mlp_chunk, :, rows, :]
        return mlp_land.at[c - mlp_chunk, half, rows, :]

    place = position(device)

    def mine(c):
        if c < mlp_chunk:
            return pieces_at(c, place, 1, None)
        return z_land.at[order[(c - mlp_chunk) // units], (c - mlp_chunk) % units]

    spread = Spread(pieces_at, send_sems, recv_sems, mine)

    def hop_ref(source, item):
        if item < 2:
            return land.at[source, slab_rows(item, place), :]
        if item == 2:
            return wo_land.at[source, out_rows(place), :]
        return z_land.at[source, item - 3]

    def own_ref(item):
        if item < 2:
            return qkv_ref.at[slab_rows(item, place), :]
        if item == 2:
            return out_ref.at[out_rows(place), :]
        return pieces.at[item - 3]

    def own_copies(item, act):
        def copy(up):
            return remote(
                own_ref(item), hop_ref(me, item), own_send.at[item, up], z_recv.at[me, item], mp=me + 2 * up - 1
            )

        @pl.when(me < parts - 1)
        def _():
            act(copy(1))

        @pl.when(me > 0)
        def _():
            act(copy(0))

    def pass_on(j, item, act):
        source = order[j]
        ref = hop_ref(source, item)

        def copy(step):
            return remote(ref, ref, z_send.at[source, item], z_recv.at[source, item], mp=me + step)

        end = 0 if item < 3 else 1

        @pl.when((source < me) & (me < parts - 1 - end))
        def _():
            act(copy(1))

        @pl.when((source > me) & (me > end))
        def _():
            act(copy(-1))

    def landed(j, item):
        ref = hop_ref(order[j], item)
        remote(ref, ref, z_send.at[order[j], item], z_recv.at[order[j], item], mp=me).wait_recv()
        pass_on(j, item, lambda copy: copy.start())
        if item >= 3 and j * units + item - 3 < early:
            keep(j * units + item - 3).start()

    inner = (me > 0) & (me < parts - 1)

    def landings(inner_items, outer_items):
        @pl.when(inner)
        def _():
            for j, item in inner_items:
                landed(j, item)

        @pl.when(jnp.logical_not(inner))
        def _():
            for j, item in outer_items:
                landed(j, item)

    def keep(c):
        return pltpu.make_async_copy(
            mine(mlp_chunk + c), pieces_at(mlp_chunk + c, place, 1, None), keep_sems.at[c]
        )

    def small_copy(s):
        ref = small_land.at[me]
        return remote(ref, ref, small_send.at[s - 1], small_recv.at[me], mp=lax.rem(me + s, parts))

    def at_place(at, ref):
        w_low[at] = ref[...].astype(BF)

    def slice_stores(at):
        rows_at = pl.ds(pl.multiple_of(at * rows, rows), rows)
        own_at = pl.ds(pl.multiple_of(at * own, own), own)
        return [
            pltpu.make_async_copy(w_low.at[at], w_out.at[rows_at, :], slice_sems.at[at, 0]),
            pltpu.make_async_copy(qkvt_ref.at[rows_at, :], qkvt_out.at[rows_at, :], slice_sems.at[at, 1]),
            pltpu.make_async_copy(ot_ref.at[own_at, :], ot_out.at[own_at, :], slice_sems.at[at, 2]),
        ]

    x_copy = pltpu.make_async_copy(x_any, x_in, x_sem)
    h1_copy = pltpu.make_async_copy(h1_ref, h1_out, out_sems.at[0])
    lse_copy = pltpu.make_async_copy(lse_ref, lse_out, out_sems.at[1])
    wo_copy = pltpu.make_async_copy(wo_low, wo_out, out_sems.at[2])
    z_copy = pltpu.make_async_copy(z_land, z_out, out_sems.at[3])
    land_copy = pltpu.make_async_copy(mlp_land, land_out, out_sems.at[4])

    x_copy.start()
    copies = []
    for u in range(units):
        at = pl.ds(pl.multiple_of(place * mlp_share, 8), mlp_share)
        copies.append((up_any.at[at, pl.ds(u * UNIT, UNIT)], pieces.at[u, 0]))
        for c in range(width // UNIT):
            at = pl.ds(pl.multiple_of(u * UNIT + place * strip, 8), strip)
            copies.append((down_any.at[at, pl.ds(c * UNIT, UNIT)], pieces.at[u, 1, pl.ds(c * strip, strip), :]))
    for source, target in copies:
        pltpu.make_async_copy(source, target, piece_sem).start()
    greet(
        *[{"mp": lax.rem(me + s, parts)} for s in range(1, parts)],
        *[{"dp": flip(device, bit)} for bit in (1, 2, 4)],
    )
    for item in range(2):
        own_copies(item, lambda copy: copy.start())
    small_land[me] = jnp.zeros(small_land.shape[1:], F32)
    small_land[me, 0:2, :own] = qv_bias_ref[...]
    small_land[me, 2:3, :] = up_bias_ref[...].reshape(1, width)
    for s in range(1, parts):
        small_copy(s).start()
    own_copies(2, lambda copy: copy.start())
    bound_ref[...] = jnp.zeros_like(bound_ref)
    bias_col[...] = jnp.zeros_like(bias_col)
    lse_ref[...] = jnp.zeros_like(lse_ref)
    z_land[me] = jnp.zeros(z_land.shape[1:], F32)

    @pl.when(jnp.logical_not(inner))
    def _():
        for source in order[1:]:
            z_land[source] = jnp.zeros(z_land.shape[1:], F32)

    for j in range(2):
        bias_col[0, 2 * j * own : (2 * j + 1) * own, :] = small_land[me].T[:own, j : j + 1]
    at_place(0, qkv_ref)
    wo_low[:own, :] = out_ref[...].astype(BF)
    x_copy.wait()

    def norm_tile(i, carry):
        at = pl.ds(pl.multiple_of(i * TILE, TILE), TILE)
        normed, _ = standardize(x_in[at, :].astype(F32))
        h1_ref[at, :] = (normed * gain_ref[0:1, :] + shift_ref[0:1, :]).astype(BF)
        return carry

    lax.fori_loop(0, tokens // TILE, norm_tile, 0, unroll=2)
    h1_copy.start()
    row = lax.broadcasted_iota(jnp.int32, (EXTRA, length), 0)
    for u in range(heads):
        vx[u, HEAD_DIM:, :] = jnp.ones((EXTRA, length), BF)

    def norm_bound(ref, u):
        value = ref[u, :HEAD_DIM, :].astype(F32)
        return jnp.max(jnp.sum(value * value, 0, keepdims=True), 1, keepdims=True)

    def project(at, r):
        tokens_r = pl.ds(pl.multiple_of(r * length, length), length)
        base = at * rows
        value = dot(w_low[at], h1_ref[tokens_r, :], NT) + bias_col[at]
        scale = HEAD_DIM**-0.5
        qkvt_ref[pl.ds(pl.multiple_of(base, own), own), tokens_r] = value[:own].astype(BF) * jnp.asarray(scale, BF)
        qkvt_ref[pl.ds(pl.multiple_of(base + own, own), 2 * own), tokens_r] = value[own:].astype(BF)

    def attend(at, r):
        tokens_r = pl.ds(pl.multiple_of(r * length, length), length)
        base = at * rows
        same = row == seg_ref[pl.ds(r, 1), :]
        for u in range(heads):
            qx[u, HEAD_DIM:, :] = jnp.where(same | (row >= 8), 0.0, -BIG).astype(BF)
            kx[u, HEAD_DIM:, :] = jnp.where(same, 1.0, 0.0).astype(BF)
        for u in range(heads):
            for k, ref in enumerate((qx, kx, vx)):
                from_row = pl.multiple_of(base + k * own + u * HEAD_DIM, HEAD_DIM)
                ref[u, :HEAD_DIM, :] = qkvt_ref[pl.ds(from_row, HEAD_DIM), tokens_r]
            kn[u] = kx[u].T
            bound_ref[...] = jnp.maximum(bound_ref[...], norm_bound(qx, u) * norm_bound(kx, u))
            to_row = pl.ds(pl.multiple_of(at * own + u * HEAD_DIM, HEAD_DIM), HEAD_DIM)
            for t in range(length // TILE):
                low, high = max(0, t * TILE - REACH), min(length, (t + 1) * TILE + REACH)
                cols = slice(t * TILE, (t + 1) * TILE)
                to_cols = pl.ds(pl.multiple_of(r * length + t * TILE, TILE), TILE)
                probs = [
                    jnp.exp2(dot(kn[u, k : k + TILE, :], qx[u, :, cols], NN) * LOG2E).astype(BF)
                    for k in range(low, high, TILE)
                ]
                out = dot(vx[u, :, low:high], jnp.concatenate(probs, 0), NN)
                total = out[HEAD_DIM : HEAD_DIM + 1, :]
                ot_ref[to_row, to_cols] = (out[:HEAD_DIM, :] * (1.0 / total)).astype(BF)
                lse_ref[pl.ds(at * heads + u, 1), to_cols] = jnp.log(total)

    w, m = out_chunk, mlp_chunk

    def event(n):
        if n == 0:
            landings(((0, 0), (1, 0)), ((0, 0),))
            spread.send(0)
            landings(((0, 1), (1, 1)), ((0, 1),))
            spread.send(1)
        if n == 1:
            spread.forward(0)
            spread.forward(1)
            landings(((2, 0),), ((1, 0),))
            spread.send(2)
        if n == 1.5:
            landings(((2, 1),), ((1, 1),))
            spread.send(3)
        if n == 2:
            spread.corner(0)
            spread.corner(1)
            landings(((0, 2), (1, 2)), ((2, 0),))
            spread.send(4)
            for s in range(1, parts):
                ref = small_land.at[lax.rem(me + s, parts)]
                remote(ref, ref, small_send.at[0], small_recv.at[lax.rem(me + s, parts)], mp=me).wait_recv()
            smalls_ref[...] = small_land[...]
            for j, source in enumerate(order):
                cols = small_land[source].T
                for k in range(2):
                    bias_col[1 + j, 2 * k * own : (2 * k + 1) * own, :] = cols[:own, k : k + 1]
            spread.complete(0)
            spread.complete(1)
            at_place(1, land.at[order[0]])
        if n == 2.5:
            spread.forward(2)
            landings((), ((2, 1),))
            spread.send(5)
            spread.forward(3)
            pltpu.make_async_copy(pieces, pieces, piece_sem).wait()
            own_copies(3, lambda copy: copy.start())
        if n == 3:
            spread.forward(4)
            landings(((2, 2),), ((0, 2),))
            spread.send(w)
            own_copies(4, lambda copy: copy.start())
        if n == 3.5:
            spread.corner(2)
            spread.corner(3)
            spread.forward(5)
        if n == 4:
            spread.complete(2)
            spread.complete(3)
            at_place(2, land.at[order[1]])
            landings(((0, 3), (1, 3)), ((1, 2), (0, 3)))
            spread.send(w + 1)
            own_copies(5, lambda copy: copy.start())
        if n == 4.5:
            spread.corner(4)
            spread.corner(5)
            spread.forward(w)
            for c in range(early):
                spread.send(m + c)
        if n == 5:
            landings(((0, 4), (1, 4)), ((2, 2), (0, 4)))
            spread.send(w + 2)
            spread.corner(w)
            spread.forward(w + 1)
        if n == 6:
            spread.complete(4)
            spread.complete(5)
            at_place(3, land.at[order[2]])
            landings(((0, 5), (1, 5), (2, 3)), ((0, 5),))
            spread.forward(w + 2)
            spread.corner(w + 1)
            for c in range(early):
                spread.forward(m + c)
        if n == 7:
            landings(((2, 4),), ())
            spread.corner(w + 2)
            for c in range(early):
                keep(c).wait()
                spread.corner(m + c)
            spread.complete(w)
        if n == 8:
            landings(((2, 5),), ())
            z_copy.start()
            spread.complete(w + 1)
            spread.complete(w + 2)
            for c in range(early):
                spread.complete(m + c)
            land_copy.start()
            for j in range(parts - 1):
                wo_low[(j + 1) * own : (j + 2) * own, :] = wo_land[order[j]].astype(BF)
            wo_copy.start()
            lse_copy.start()

    event(0)

    def step(n, carry):
        at, r = lax.div(n, 2), lax.rem(n, 2)
        project(at, r)
        for e in (1, 2, 3, 4):
            @pl.when(n == e)
            def _():
                event(e + 0.5)

        attend(at, r)

        @pl.when(r == 1)
        def _():
            for copy in slice_stores(at):
                copy.start()

        for e in range(1, 9):
            @pl.when(n + 1 == e)
            def _():
                event(e)

        return carry

    lax.fori_loop(0, 2 * parts, step, 0)
    for c in range(mlp_chunk + early):
        spread.sent(c)
    for item in range(items):
        own_copies(item, lambda copy: copy.wait_send())
        for j in range(parts - 1):
            pass_on(j, item, lambda copy: copy.wait_send())
    for s in range(1, parts):
        small_copy(s).wait_send()
    for copy in (h1_copy, lse_copy, wo_copy, z_copy, land_copy):
        copy.wait()
    for at in range(parts):
        for copy in slice_stores(at):
            copy.wait()


def front(x, seg, gains, shifts, qkv, out, qv_bias, up_bias, up, down):
    tokens, width = x.shape
    length = seg.shape[1]
    rows = qkv.shape[0]
    own = out.shape[0]
    parts = width // own
    heads = own // HEAD_DIM
    units = up.shape[1] // UNIT
    chunks = 3 * (parts - 1) + EARLY
    wide = HEAD_DIM + EXTRA
    dma = pltpu.SemaphoreType.DMA
    return pl.pallas_call(
        front_kernel,
        in_specs=[WHOLE] * 7 + [ANY] * 3,
        out_specs=[WHOLE] * 2 + [ANY] * 8,
        out_shape=[
            shape_of((parts, 8, width), F32),
            shape_of((8, 128), F32),
            shape_of((tokens, width), BF),
            shape_of((parts * rows, width), BF),
            shape_of((width, width), BF),
            shape_of((parts * rows, tokens), BF),
            shape_of((width, tokens), BF),
            shape_of((16, tokens), F32),
            shape_of((EARLY, 2, width, UNIT), F32),
            shape_of((parts, units, 2, width // 8, UNIT), F32),
        ],
        scratch_shapes=[
            pltpu.VMEM((tokens, width), BF),
            pltpu.VMEM((tokens, width), BF),
            pltpu.VMEM((parts, rows, width), F32),
            pltpu.VMEM((parts, own, width), F32),
            pltpu.VMEM((parts, units, 2, width // 8, UNIT), F32),
            pltpu.VMEM((EARLY, 2, width, UNIT), F32),
            pltpu.VMEM((units, 2, width // 8, UNIT), F32),
            pltpu.VMEM((parts, 8, width), F32),
            pltpu.VMEM((parts, rows, width), BF),
            pltpu.VMEM((width, width), BF),
            pltpu.VMEM((parts, rows, 1), F32),
            pltpu.VMEM((parts * rows, tokens), BF),
            pltpu.VMEM((width, tokens), BF),
            pltpu.VMEM((16, tokens), F32),
            pltpu.VMEM((heads, wide, length), BF),
            pltpu.VMEM((heads, wide, length), BF),
            pltpu.VMEM((heads, wide, length), BF),
            pltpu.VMEM((heads, length, wide), BF),
            dma,
            dma,
            dma((EARLY,)),
            dma((5,)),
            dma((parts, 3)),
            dma((parts, 3 + units)),
            dma((parts, 3 + units)),
            dma((3 + units, 2)),
            dma((parts - 1,)),
            dma((parts,)),
            dma((chunks,)),
            dma((chunks, 3)),
        ],
        compiler_params=pltpu.CompilerParams(vmem_limit_bytes=62 * 2**20, collective_id=0, has_side_effects=True),
        name="front",
    )(gains, shifts, qkv, out, qv_bias, up_bias, seg, x, up, down)


def repair_kernel(
    bound_ref, seg_ref, qkvt_any, ot_in, lse_in, ot_out, lse_out, qx, kx, vx, lse_row, sems,
):
    rows_here, length = seg_ref.shape
    parts = 4
    own = qkvt_any.shape[0] // (3 * parts)
    heads = parts * own // HEAD_DIM
    safe = jnp.max(bound_ref[...]) < SAFE_SCORE**2

    @pl.when(jnp.logical_not(safe))
    def _():
        row = lax.broadcasted_iota(jnp.int32, (EXTRA, length), 0)
        vx[HEAD_DIM:, :] = jnp.ones((EXTRA, length), BF)

        def move(copies):
            copies = [pltpu.make_async_copy(a, b, sems.at[i]) for i, (a, b) in enumerate(copies)]
            for copy in copies:
                copy.start()
            for copy in copies:
                copy.wait()

        def head(i, carry):
            r, h = lax.div(i, heads), lax.rem(i, heads)
            rows = pl.ds(pl.multiple_of(h * HEAD_DIM, HEAD_DIM), HEAD_DIM)
            tokens = pl.ds(pl.multiple_of(r * length, length), length)
            head_at = lax.div(h, heads // parts) * 3 * own + lax.rem(h, heads // parts) * HEAD_DIM
            same = row == seg_ref[pl.ds(r, 1), :]
            qx[HEAD_DIM:, :] = jnp.where(same | (row >= 8), 0.0, -BIG).astype(BF)
            kx[HEAD_DIM:, :] = jnp.where(same, 1.0, 0.0).astype(BF)
            move([
                (
                    qkvt_any.at[pl.ds(pl.multiple_of(head_at + k * own, HEAD_DIM), HEAD_DIM), tokens],
                    target.at[pl.ds(0, HEAD_DIM), :],
                )
                for k, target in enumerate((qx, kx, vx))
            ])

            @pl.when(h == 0)
            def _():
                lse_row[...] = jnp.zeros_like(lse_row)

            for t in range(length // TILE):
                cols = slice(t * TILE, (t + 1) * TILE)
                scores = dot(kx[...], qx[:, cols], TN)
                highest = jnp.max(scores, 0, keepdims=True)
                probs = jnp.exp2((scores - highest) * LOG2E).astype(BF)
                out = dot(vx[...], probs, NN)
                total = out[HEAD_DIM : HEAD_DIM + 1, :]
                qx[:HEAD_DIM, cols] = (out[:HEAD_DIM, :] * (1.0 / total)).astype(BF)
                lse_row[pl.ds(h, 1), cols] = jnp.log(total) + highest
            move([(qx.at[pl.ds(0, HEAD_DIM), :], ot_out.at[rows, tokens])])

            @pl.when(h == heads - 1)
            def _():
                move([(lse_row, lse_out.at[:, tokens])])

            return carry

        lax.fori_loop(0, rows_here * heads, head, 0)


def repair(bound, seg, qkvt, ot, lse):
    length = seg.shape[1]
    return pl.pallas_call(
        repair_kernel,
        in_specs=[WHOLE, WHOLE, ANY, ANY, ANY],
        out_specs=[ANY, ANY],
        out_shape=[shape_of(ot.shape, BF), shape_of(lse.shape, F32)],
        input_output_aliases={3: 0, 4: 1},
        scratch_shapes=[pltpu.VMEM((HEAD_DIM + EXTRA, length), BF)] * 3
        + [pltpu.VMEM((16, length), F32), pltpu.SemaphoreType.DMA((3,))],
        compiler_params=params(),
        name="repair",
    )(bound, seg, qkvt, ot, lse)


def split3(value):
    first = value.astype(BF)
    rest = value - first.astype(F32)
    second = rest.astype(BF)
    return first, second, (rest - second.astype(F32)).astype(BF)


class Total:
    def __init__(self, out, sends, recvs, near=None, side_land=None, across_land=None, source=None):
        self.out, self.near = out, near
        self.source = out if source is None else source
        self.side_land, self.across_land, self.sends, self.recvs = side_land, across_land, sends, recvs
        self.device = lax.axis_index("dp")
        place = lax.rem(self.device, 8)
        self.half = out.shape[0] // 2
        self.part, self.piece = self.half // 4, self.half // 8
        bits = [lax.rem(lax.div(place, bit), 2) for bit in (1, 2, 4)]
        self.base = bits[0] * self.half
        self.away = (1 - bits[0]) * self.half
        self.one = self.base + bits[1] * self.part
        self.one_away = self.base + (1 - bits[1]) * self.part
        self.two = self.base + 2 * self.part + bits[2] * self.part
        self.two_away = self.base + 2 * self.part + (1 - bits[2]) * self.part
        self.one_piece = self.one + bits[2] * self.piece
        self.one_piece_away = self.one + (1 - bits[2]) * self.piece
        self.two_piece = self.two + bits[1] * self.piece
        self.two_piece_away = self.two + (1 - bits[1]) * self.piece

    def rows(self, start, count):
        return self.out.at[pl.ds(pl.multiple_of(start, 8), count), :]

    def from_source(self, start, count):
        return self.source.at[pl.ds(pl.multiple_of(start, 8), count), :]

    def copy(self, sem, bit, src, dst):
        return remote(src, dst, self.sends.at[sem], self.recvs.at[sem], dp=flip(self.device, bit))

    def over(self, sem, bit, start, count):
        ref = self.rows(start, count)
        return self.copy(sem, bit, ref, ref)

    def copies(self, stage):
        part, piece = self.part, self.piece
        first, second = pl.ds(0, part), pl.ds(part, piece)
        if stage == 0:
            return [self.copy(0, 1, self.rows(self.away, self.half), self.near)]
        if stage == 1:
            return [
                self.copy(1, 2, self.rows(self.one_away, part), self.side_land.at[first, :]),
                self.copy(2, 4, self.rows(self.two_away, part), self.across_land.at[first, :]),
            ]
        if stage == 2:
            return [
                self.copy(3, 4, self.from_source(self.one_piece_away, piece), self.across_land.at[second, :]),
                self.copy(4, 2, self.from_source(self.two_piece_away, piece), self.side_land.at[second, :]),
            ]
        if stage == 3:
            return [self.over(5, 4, self.one_piece, piece), self.over(6, 2, self.two_piece, piece)]
        if stage == 4:
            return self.halves(0, self.one, self.two)
        if stage == 4.5:
            return self.halves(1, self.one, self.two)
        return [self.over(9, 1, self.base, self.half)]

    def halves(self, h, one, two):
        half = self.part // 2
        return [self.over(7 + 3 * h, 2, one + h * half, half), self.over(8 + 3 * h, 4, two + h * half, half)]

    def arrivals(self, stage):
        part, piece = self.part, self.piece
        if stage == 3:
            return [self.over(5, 4, self.one_piece_away, piece), self.over(6, 2, self.two_piece_away, piece)]
        if stage == 4:
            return self.halves(0, self.one_away, self.two_away)
        if stage == 4.5:
            return self.halves(1, self.one_away, self.two_away)
        if stage == 5:
            return [self.over(9, 1, self.away, self.half)]
        return self.copies(stage)

    def add(self, start, ref, at, count):
        step = 48 if count % 48 == 0 else 56

        def some(i, carry):
            rows = pl.ds(pl.multiple_of(start + i * step, 8), step)
            self.out[rows, :] += ref[pl.ds(pl.multiple_of(at + i * step, 8), step), :]
            return carry

        lax.fori_loop(0, count // step, some, 0)

    def finish(self, stage):
        for copy in self.copies(stage):
            copy.wait_send()
        for copy in self.arrivals(stage):
            copy.wait_recv()
        if stage == 0:
            self.add(self.base, self.near, 0, self.half)
        elif stage == 1:
            self.add(self.one, self.side_land, 0, self.part)
            self.add(self.two, self.across_land, 0, self.part)
        elif stage == 2:
            self.add(self.one_piece, self.across_land, self.part, self.piece)
            self.add(self.two_piece, self.side_land, self.part, self.piece)

    def start(self, stage):
        for copy in self.copies(stage):
            copy.start()

    @staticmethod
    def scratch(rows, width):
        dma = pltpu.SemaphoreType.DMA
        return [
            dma((12,)),
            dma((12,)),
            pltpu.VMEM((rows // 2, width), F32),
            pltpu.VMEM((rows // 8 + rows // 16, width), F32),
            pltpu.VMEM((rows // 8 + rows // 16, width), F32),
        ]


def attend_back_kernel(
    seg_ref, qkv_ref, ot_ref, dt_ref, lse_ref, h1_any, main_any, tail_any,
    dqkv_ref, main_out, rest_out,
    qx, kx, vx, dx, qn, dn, kn, acc, h1_ref, part_ref, main_ref, rest_ref, whole_ref, in_sems, out_sems, main_send, main_recv, side_land, across_land,
    *comm,
):
    step = pl.program_id(0)
    own, length = ot_ref.shape
    width = h1_ref.shape[1]
    heads = own // HEAD_DIM
    tail_at = rest_ref.shape[0] - tail_any.shape[0]
    part = Total(part_ref, main_send, main_recv, None, side_land, across_land, main_any)
    main = Total(main_ref, main_send, main_recv)
    rest = Total(rest_ref, *comm)
    whole = Total(whole_ref, *comm[:2])
    loads = [
        pltpu.make_async_copy(main_any.at[pl.ds(pl.multiple_of(at, 8), part.part), :], part.rows(at, part.part), sem)
        for at, sem in ((part.one, in_sems.at[0]), (part.two, in_sems.at[1]))
    ]
    loads.append(pltpu.make_async_copy(tail_any, rest_ref.at[pl.ds(tail_at, tail_any.shape[0]), :], in_sems.at[2]))
    loads.append(pltpu.make_async_copy(h1_any, h1_ref, in_sems.at[3]))
    stores = [
        pltpu.make_async_copy(main_ref, main_out, out_sems.at[0]),
        pltpu.make_async_copy(whole_ref, rest_out, out_sems.at[1]),
    ]

    @pl.when(step == 0)
    def _():
        for copy in loads:
            copy.start()
        greet(*[{"dp": flip(main.device, bit)} for bit in (1, 2, 4)])
        part.start(2)
        for copy in loads[:2]:
            copy.wait()

    @pl.when(step == 1)
    def _():
        part.finish(2)
        for at in (part.one_piece, part.two_piece):
            rows = pl.ds(pl.multiple_of(at, 8), part.piece)
            main_ref[rows, :] = part_ref[rows, :]
        main.start(3)

    @pl.when(step == 2)
    def _():
        main.finish(3)
        main.start(4)

    @pl.when(step == 3)
    def _():
        rest.finish(0)
        rest.start(1)

    @pl.when(step == 4)
    def _():
        rest.finish(1)
        rest.start(2)
        main.finish(4)
        main.start(4.5)

    @pl.when(step == 5)
    def _():
        rest.finish(2)
        for at in (rest.one_piece, rest.two_piece):
            rows = pl.ds(pl.multiple_of(at, 8), rest.piece)
            whole_ref[rows, :] = rest_ref[rows, :]
        whole.start(3)

    @pl.when(step == 6)
    def _():
        whole.finish(3)
        whole.start(4)
        whole.start(4.5)
        main.finish(4.5)
        main.start(5)

    @pl.when(step == 7)
    def _():
        whole.finish(4)
        whole.finish(4.5)
        whole.start(5)
        main.finish(5)
        stores[0].start()

    row = lax.broadcasted_iota(jnp.int32, (EXTRA, length), 0)
    same = row == seg_ref[pl.ds(jnp.where((step == 1) | (step >= 5), 1, 0), 1), :]
    key_extra = jnp.where(same | ((row >= 8) & (row < 11)), 1.0, 0.0).astype(BF)
    value_extra = jnp.where(row < 3, 1.0, 0.0).astype(BF)
    query_extra = jnp.where(same | (row >= 8), 0.0, -BIG)

    def three_rows(value, at):
        first, second, third = split3(value)
        out = jnp.where(row == at, first.astype(F32), 0.0)
        out = jnp.where(row == at + 1, second.astype(F32), out)
        return jnp.where(row == at + 2, third.astype(F32), out)

    head_at = jnp.where(step < 2, 0, lax.rem(step - 2, 3) + 1) * heads

    def head(u):
        rows = slice(u * HEAD_DIM, (u + 1) * HEAD_DIM)
        dq_rows, dk_rows, dv_rows = (slice(rows.start + k * own, rows.stop + k * own) for k in range(3))
        qx[u, :HEAD_DIM, :] = qkv_ref[dq_rows, :]
        kx[u, :HEAD_DIM, :] = qkv_ref[dk_rows, :]
        vx[u, :HEAD_DIM, :] = qkv_ref[dv_rows, :]
        dx[u, :HEAD_DIM, :] = dt_ref[rows, :]
        inner = jnp.sum(dt_ref[rows, :].astype(F32) * ot_ref[rows, :].astype(F32), 0, keepdims=True)
        log_sum = lse_ref[pl.ds(head_at + u, 1), :]
        qx[u, HEAD_DIM:, :] = (query_extra + three_rows(-log_sum, 8)).astype(BF)
        kx[u, HEAD_DIM:, :] = key_extra
        vx[u, HEAD_DIM:, :] = value_extra
        dx[u, HEAD_DIM:, :] = three_rows(-inner, 0).astype(BF)
        qn[u] = qx[u].T
        dn[u] = dx[u].T
        kn[u] = kx[u].T
        for t in range(length // TILE):
            low, high = max(0, t * TILE - REACH), min(length, (t + 1) * TILE + REACH)
            keys = slice(t * TILE, (t + 1) * TILE)
            probs, score_grads = [], []
            for q in range(low, high, TILE):
                prob = jnp.exp2(dot(qn[u, q : q + TILE, :], kx[u, :, keys], NN) * LOG2E)
                prob_grad = dot(dn[u, q : q + TILE, :], vx[u, :, keys], NN)
                probs.append(prob.astype(BF))
                score_grads.append((prob * prob_grad).astype(BF))
            probs = jnp.concatenate(probs, 0)
            score_grads = jnp.concatenate(score_grads, 0)
            dqkv_ref[dv_rows, keys] = dot(dx[u, :HEAD_DIM, low:high], probs, NN).astype(BF)
            dqkv_ref[dk_rows, keys] = dot(qx[u, :HEAD_DIM, low:high], score_grads, NN).astype(BF)
            part = dot(score_grads, kx[u, :HEAD_DIM, keys], NT)
            if t == 0:
                acc[u, low:high, :] = part
                if high < length:
                    acc[u, high:, :] = jnp.zeros((length - high, HEAD_DIM), F32)
            else:
                acc[u, low:high, :] += part
        dqkv_ref[dq_rows, :] = (acc[u] * HEAD_DIM**-0.5).T.astype(BF)

    for u in range(heads):
        head(u)

    def own_grads(tokens, add):
        part = dot(dqkv_ref[...], h1_ref[tokens, :], NN)
        rest_ref[: 3 * own, :] = rest_ref[: 3 * own, :] + part if add else part
        ones = jnp.ones((8, length), BF)
        for k in (0, 2):
            rows = slice(3 * own + k * 4, 3 * own + k * 4 + 8)
            part = dot(ones, dqkv_ref[k * own : (k + 1) * own, :], NT)
            rest_ref[rows, :own] = rest_ref[rows, :own] + part if add else part

    @pl.when(step == 0)
    def _():
        rest_ref[3 * own : tail_at, :] = jnp.zeros((tail_at - 3 * own, width), F32)
        loads[3].wait()
        own_grads(slice(0, length), False)

    @pl.when(step == 1)
    def _():
        own_grads(slice(length, 2 * length), True)
        loads[2].wait()
        rest.start(0)

    @pl.when(step == 7)
    def _():
        whole.finish(5)
        stores[1].start()
        for copy in stores:
            copy.wait()


def attend_back(seg, qkvt, ot, dt, lse, h1, main, tail):
    width, tokens = ot.shape
    _, length = seg.shape
    own = width // 4
    heads = own // HEAD_DIM
    wide = HEAD_DIM + EXTRA
    rest_rows = 3 * own + 64 + tail.shape[0]
    row_of = lambda s: jnp.where((s == 1) | (s >= 5), 1, 0)
    part_of = lambda s: jnp.where(s < 2, 0, lax.rem(s - 2, 3) + 1)
    block = pl.BlockSpec((own, length), lambda s: (part_of(s), row_of(s)))
    wide_block = pl.BlockSpec((3 * own, length), lambda s: (part_of(s), row_of(s)))
    dma = pltpu.SemaphoreType.DMA
    return pl.pallas_call(
        attend_back_kernel,
        grid=(8,),
        in_specs=[ONCE, wide_block, block, block]
        + [pl.BlockSpec((16, length), lambda s: (0, row_of(s))), ANY, ANY, ANY],
        out_specs=[wide_block, ANY, ANY],
        out_shape=[shape_of(qkvt.shape, BF), shape_of(main.shape, F32), shape_of((rest_rows, width), F32)],
        scratch_shapes=[pltpu.VMEM((heads, wide, length), BF)] * 4
        + [pltpu.VMEM((heads, length, wide), BF)] * 3
        + [
            pltpu.VMEM((heads, length, HEAD_DIM), F32),
            pltpu.VMEM((tokens, width), BF),
            pltpu.VMEM(main.shape, F32),
            pltpu.VMEM(main.shape, F32),
            pltpu.VMEM((rest_rows, width), F32),
            pltpu.VMEM((rest_rows, width), F32),
            dma((4,)),
            dma((2,)),
            dma((12,)),
            dma((12,)),
            pltpu.VMEM((main.shape[0] // 8 + main.shape[0] // 16, width), F32),
            pltpu.VMEM((main.shape[0] // 8 + main.shape[0] // 16, width), F32),
        ]
        + Total.scratch(rest_rows, width),
        compiler_params=pltpu.CompilerParams(vmem_limit_bytes=60 * 2**20, collective_id=2, has_side_effects=True),
        name="attend_back",
    )(seg, qkvt, ot, dt, lse, h1, main, tail)


def token_kernel(
    dqkv_ref, w_ref, x_ref, mg_ref, gain_ref, main_any, rest_any, result_any,
    tg_ref, sums_ref, down_ref, up_ref, out_ref, result_ref, qkv_ref,
    main_v, rest_v, result_v, in_sems, out_sems,
):
    step = pl.program_id(0)
    last = pl.num_programs(0) - 1
    ff = down_ref.shape[0]
    own = out_ref.shape[0]
    out_at = 3 * own + 64
    loads = [
        pltpu.make_async_copy(source, target, in_sems.at[i])
        for i, (source, target) in enumerate(((rest_any, rest_v), (main_any, main_v), (result_any, result_v)))
    ]
    stores = [
        pltpu.make_async_copy(source, target, out_sems.at[i])
        for i, (source, target) in enumerate((
            (main_v.at[pl.ds(0, ff), :], down_ref),
            (main_v.at[pl.ds(ff, up_ref.shape[0]), :], up_ref),
            (rest_v.at[pl.ds(out_at, own), :], out_ref),
            (result_v, result_ref),
            (rest_v.at[pl.ds(0, 3 * own), :], qkv_ref),
        ))
    ]

    @pl.when(step == 0)
    def _():
        for copy in loads:
            copy.start()
        sums_ref[...] = jnp.zeros_like(sums_ref)

    @pl.when(step == last - 1)
    def _():
        for copy in loads:
            copy.wait()
        for copy in stores:
            copy.start()

    hg = dot(dqkv_ref[...], w_ref[...], TN)
    normed, inv_std = standardize(x_ref[...].astype(F32))
    tg_ref[...] = mg_ref[...].astype(F32) + norm_back(hg, normed, inv_std, gain_ref[0:1, :])
    sums_ref[0:1, :] += jnp.sum(hg * normed, 0, keepdims=True)
    sums_ref[1:2, :] += jnp.sum(hg, 0, keepdims=True)

    @pl.when(step == last)
    def _():
        for copy in stores:
            copy.wait()


def token_back(dqkv, weights, x, mg, gains, main, rest, result, ff, own):
    tokens, width = x.shape
    row = pl.BlockSpec((LONG_TILE, width), lambda t: (t, 0))
    col = pl.BlockSpec((weights.shape[0], LONG_TILE), lambda t: (0, t))
    dma = pltpu.SemaphoreType.DMA
    return pl.pallas_call(
        token_kernel,
        grid=(tokens // LONG_TILE,),
        in_specs=[col, ONCE, row, row, ONCE, ANY, ANY, ANY],
        out_specs=[row, ONCE, ANY, ANY, ANY, ANY, ANY],
        out_shape=[
            shape_of((tokens, width), F32),
            shape_of((8, width), F32),
            shape_of((ff, width), F32),
            shape_of((width, ff), F32),
            shape_of((own, width), F32),
            shape_of((tokens, width), BF),
            shape_of((3 * own, width), F32),
        ],
        scratch_shapes=[
            pltpu.VMEM(main.shape, F32),
            pltpu.VMEM(rest.shape, F32),
            pltpu.VMEM((tokens, width), BF),
            dma((3,)),
            dma((5,)),
        ],
        compiler_params=params(),
        name="token_back",
    )(dqkv, weights, x, mg, gains, main, rest, result)


def sums_kernel(in_ref, out_ref, land, sends, recvs):
    device = lax.axis_index("dp")
    place = lax.rem(device, 8)
    others = []
    for bits in range(1, 8):
        other = device
        for bit in (1, 2, 4):
            if bits & bit:
                other = flip(other, bit)
        others.append(other)
    greet(*[{"dp": other} for other in others])
    copies = [
        remote(in_ref, land.at[place], sends.at[i], recvs.at[place], dp=other) for i, other in enumerate(others)
    ]
    for copy in copies:
        copy.start()
    land[place] = in_ref[...]
    for other in others:
        peer = lax.rem(other, 8)
        remote(in_ref, land.at[peer], sends.at[0], recvs.at[peer], dp=other).wait_recv()
    out_ref[...] = jnp.sum(land[...], 0)
    for copy in copies:
        copy.wait_send()


def add_sums(sums):
    dma = pltpu.SemaphoreType.DMA
    return pl.pallas_call(
        sums_kernel,
        in_specs=[WHOLE],
        out_specs=WHOLE,
        out_shape=shape_of(sums.shape, F32),
        scratch_shapes=[pltpu.VMEM((8,) + sums.shape, F32), dma((7,)), dma((8,))],
        compiler_params=pltpu.CompilerParams(collective_id=3, has_side_effects=True),
        name="add_sums",
    )(sums)


def arrange_kernel(sums_ref, rest_any, gains_ref, shifts_ref, biases_ref, qv_bias_ref, up_bias_ref, rows_v, sems, *, own):
    loads = [
        pltpu.make_async_copy(rest_any.at[pl.ds(low, 16), :], rows_v.at[i], sems.at[i])
        for i, low in enumerate((3 * own, 4 * own + 64))
    ]
    for copy in loads:
        copy.start()
    gains_ref[0:1, :] = sums_ref[0:1, :]
    shifts_ref[0:1, :] = sums_ref[1:2, :]
    for copy in loads:
        copy.wait()
    gains_ref[1:2, :] = rows_v[1, GAIN_TWO : GAIN_TWO + 1, :]
    shifts_ref[1:2, :] = rows_v[1, SHIFT_TWO : SHIFT_TWO + 1, :]
    biases_ref[...] = rows_v[1, BIAS_ONE : BIAS_TWO + 1, :]
    up_bias_ref[...] = rows_v[1, UP_BIAS, :]
    qv_bias_ref[0:1, :] = rows_v[0, 0:1, :own]
    qv_bias_ref[1:2, :] = rows_v[0, 8:9, :own]


def arrange(sums, rest, own):
    width = sums.shape[1]
    return pl.pallas_call(
        partial(arrange_kernel, own=own),
        in_specs=[WHOLE, ANY],
        out_specs=[WHOLE] * 5,
        out_shape=[shape_of((2, width), F32)] * 3 + [shape_of((2, own), F32), shape_of((width,), F32)],
        scratch_shapes=[pltpu.VMEM((2, 16, width), F32), pltpu.SemaphoreType.DMA((2,))],
        name="arrange",
    )(sums, rest)


GELU_C = 0.7978845608028654
GELU_A = 0.044715


def gelu_both(pre):
    square = pre * pre
    half = 0.5 + 0.5 * jnp.tanh(pre * (GELU_C + (GELU_C * GELU_A) * square))
    act = pre * half
    slope = half + act * (1.0 - half) * (2.0 * GELU_C + (6.0 * GELU_C * GELU_A) * square)
    return act, slope


GAIN_TWO, SHIFT_TWO, BIAS_ONE, BIAS_TWO, UP_BIAS = range(5)


def mlp_kernel(
    wo_ref, smalls_ref, bias_ref, gain_ref, shift_ref, x_any, ot_any, g_any, up_any, down_any, land_any, z_any,
    result_out, mg_out, dt_out, main_out, tail_out,
    land, z_far, wide_w, own_w, g_ref, h2_ref, dt_ref, mine_ref, main_ref, tail_ref, normed_ref, inv_ref, res_ref, hg_ref,
    up_low, down_low, pre_s, ag_s,
    in_sems, w_sems, keep_sems, far_keep, far_send, far_recv, out_sems, tile_sems, send_sems, recv_sems, *comm,
):
    tokens, width = g_ref.shape
    parts = smalls_ref.shape[0]
    own = mine_ref.shape[0]
    ff = up_any.shape[1]
    units = ff // UNIT
    chunks = units * (parts - 1)
    late = land.shape[0]
    early = chunks - late
    share = z_any.shape[3]
    strip = UNIT // 8
    tiles = tokens // TILE
    me = lax.axis_index("mp")
    order = foreign_order(me)
    total = Total(main_ref, *comm)

    def source_of(c):
        j = lax.div(c, units)
        return jnp.where(j == 0, order[0], jnp.where(j == 1, order[1], order[2]))

    def pieces_at(e, at, count, half):
        rows = pl.ds(pl.multiple_of(at * share, 8), count * share)
        if half is None:
            return land.at[e, :, rows, :]
        return land.at[e, half, rows, :]

    spread = Spread(pieces_at, send_sems, recv_sems)
    far_at = units - early
    far_count = units * (parts - 2)

    def mine(e):
        return z_any.at[order[(early + e) // units], (early + e) % units]

    inner = (me > 0) & (me < parts - 1)

    def far_source(u):
        return z_any.at[jnp.where(u < units, order[1], order[2]), lax.rem(u, units)]

    def far_copy(u):
        step = jnp.where(lax.div(me, 2) == 0, -1, 1)
        return remote(far_source(u), z_far.at[u], far_send.at[u], far_recv.at[u], mp=me + step)

    def far_local(u):
        return pltpu.make_async_copy(far_source(u), z_far.at[u], far_keep.at[u])

    def far(u):
        @pl.when(inner)
        def _():
            far_local(u).wait()

        @pl.when(jnp.logical_not(inner))
        def _():
            remote(z_far.at[u], z_far.at[u], far_send.at[u], far_recv.at[u], mp=me).wait_recv()

    def keep(e, source):
        return pltpu.make_async_copy(source, pieces_at(e, spread.at, 1, None), keep_sems.at[e])

    def send(e):
        @pl.when((e >= far_at) & (e < late))
        def _():
            far(e - far_at)
            keep(e, z_far.at[e - far_at]).start()

        @pl.when(e < late)
        def _():
            keep(e, z_far.at[0]).wait()
            spread.send(e)

    def serve(n):
        @pl.when(n - 1 < late)
        def _():
            spread.forward(n - 1)

        send(n + 1)

        @pl.when((n > 2) & (n - 3 < late))
        def _():
            spread.corner(n - 3)

    def reduce(n):
        @pl.when(n == units)
        def _():
            total.start(0)

        @pl.when(n == units + 7)
        def _():
            total.finish(0)
            total.start(1)

    def unit(bias, grads_at):
        def front(i):
            rows = slice(i * TILE, (i + 1) * TILE)
            pre_s[i % 2] = dot(h2_ref[rows, :], up_low[...], NN) + bias
            ag_s[i % 2] = dot(g_ref[rows, :], down_low[...], NT)

        def back(i):
            rows = slice(i * TILE, (i + 1) * TILE)
            act, slope = gelu_both(pre_s[i % 2])
            act = act.astype(BF)
            pre_grad = (ag_s[i % 2] * slope).astype(BF)
            res_ref[rows, :] += dot(act, down_low[...], NN)
            hg_ref[rows, :] += dot(pre_grad, up_low[...], NT)
            if grads_at is not None:
                h2 = h2_ref[rows, :]
                g = g_ref[rows, :]
                cols = pl.ds(pl.multiple_of(grads_at, UNIT), UNIT)
                main_ref[cols, :] += dot(act, g, TN)
                main_ref[ff:, cols] += dot(h2, pre_grad, TN)
                at = own + UP_BIAS
                tail_ref[at : at + 1, cols] += jnp.sum(pre_grad.astype(F32), 0, keepdims=True)

        front(0)
        for i in range(tiles):
            if i + 1 < tiles:
                front(i + 1)
            back(i)

    loads = [
        pltpu.make_async_copy(source, target, in_sems.at[i])
        for i, (source, target) in enumerate(((ot_any, dt_ref), (x_any, h2_ref), (g_any, g_ref)))
    ]

    def own_load(u):
        cols = pl.ds(pl.multiple_of(u * UNIT, UNIT), UNIT)
        return [
            pltpu.make_async_copy(up_any.at[:, cols], wide_w.at[0], w_sems.at[0]),
            pltpu.make_async_copy(down_any.at[cols, :], own_w, w_sems.at[1]),
        ]

    def chunk_load(c):
        return pltpu.make_async_copy(land_any.at[c], wide_w, w_sems.at[0])

    for copy in loads:
        copy.start()
    for copy in own_load(0):
        copy.start()
    for e in range(far_at):
        keep(e, mine(e)).start()

    @pl.when(inner)
    def _():
        for u in range(far_count):
            far_local(u).start()

    greet(
        *[{"mp": lax.rem(me + s, parts)} for s in range(1, parts)],
        *[{"dp": flip(spread.device, bit)} for bit in (1, 2, 4)],
    )

    @pl.when(inner)
    def _():
        for u in range(far_count):
            far_copy(u).start()

    send(0)
    send(1)
    main_ref[...] = jnp.zeros_like(main_ref)
    tail_ref[...] = jnp.zeros_like(tail_ref)
    for copy in loads[:2]:
        copy.wait()
    mine_ref[...] = dt_ref[:own, :]

    def first(i, carry):
        rows = pl.ds(pl.multiple_of(i * TILE, TILE), TILE)
        mixed = h2_ref[rows, :].astype(F32) + dot(dt_ref[:, rows], wo_ref[...], TN) + bias_ref[0:1, :]
        res_ref[rows, :] = mixed + bias_ref[1:2, :]
        hg_ref[rows, :] = jnp.zeros((TILE, width), F32)
        normed, inv_std = standardize(mixed)
        normed_ref[rows, :] = normed
        inv_ref[rows, :] = inv_std
        h2_ref[rows, :] = (normed * gain_ref[1:2, :] + shift_ref[1:2, :]).astype(BF)
        return carry

    lax.fori_loop(0, tiles, first, 0, unroll=4)
    serve(1)
    loads[2].wait()

    def own_unit(u, carry):
        for copy in own_load(u):
            copy.wait()
        up_low[...] = wide_w[0].astype(BF)
        down_low[...] = own_w[...].astype(BF)

        @pl.when(u + 1 < units)
        def _():
            for copy in own_load(u + 1):
                copy.start()

        @pl.when(u + 1 == units)
        def _():
            chunk_load(0).start()

        unit(smalls_ref[me, 2:3, pl.ds(pl.multiple_of(u * UNIT, UNIT), UNIT)], u * UNIT)
        serve(u + 2)
        reduce(u + 1)
        return carry

    lax.fori_loop(0, units, own_unit, 0)

    def take(ref, at):
        up_low[...] = ref[at + (0,)].astype(BF)
        for q in range(8):
            for k in range(width // UNIT):
                low = q * share + k * strip
                down_low[q * strip : (q + 1) * strip, k * UNIT : (k + 1) * UNIT] = ref[
                    at + (1, slice(low, low + strip))
                ].astype(BF)

    def foreign_unit(c, carry):
        @pl.when(c < early)
        def _():
            chunk_load(c).wait()
            take(wide_w, ())

        @pl.when(c + 1 < early)
        def _():
            chunk_load(c + 1).start()

        @pl.when(c >= early)
        def _():
            e = c - early
            spread.complete(e)
            take(land, (e,))

        cols = pl.ds(pl.multiple_of(lax.rem(c, units) * UNIT, UNIT), UNIT)
        unit(smalls_ref[source_of(c), 2:3, cols], None)
        serve(c + units + 2)
        reduce(c + units + 1)
        return carry

    lax.fori_loop(0, chunks, foreign_unit, 0)

    def tile_stores(i):
        rows = pl.ds(pl.multiple_of(i * TILE, TILE), TILE)
        return [
            pltpu.make_async_copy(source, target, tile_sems.at[k])
            for k, (source, target) in enumerate((
                (h2_ref.at[rows, :], result_out.at[rows, :]),
                (g_ref.at[rows, :], mg_out.at[rows, :]),
                (dt_ref.at[:, rows], dt_out.at[:, rows]),
            ))
        ]

    def finish(i, carry):
        rows = pl.ds(pl.multiple_of(i * TILE, TILE), TILE)
        g = g_ref[rows, :].astype(F32)
        h2_ref[rows, :] = res_ref[rows, :].astype(BF)
        normed, inv_std = normed_ref[rows, :], inv_ref[rows, :]
        hg = hg_ref[rows, :]
        mg = g + norm_back(hg, normed, inv_std, gain_ref[1:2, :])
        low = mg.astype(BF)
        g_ref[rows, :] = low
        dt_ref[:, rows] = dot(wo_ref[...], low, NT).astype(BF)
        tail_ref[:own, :] += dot(mine_ref[:, rows], low, NN)
        for at, value in ((GAIN_TWO, hg * normed), (SHIFT_TWO, hg), (BIAS_ONE, mg), (BIAS_TWO, g)):
            tail_ref[own + at : own + at + 1, :] += jnp.sum(value, 0, keepdims=True)
        for copy in tile_stores(i):
            copy.start()
        return carry

    lax.fori_loop(0, tiles, finish, 0, unroll=4)
    total.finish(1)
    ends = [
        pltpu.make_async_copy(total.rows(at, total.part), main_out.at[pl.ds(pl.multiple_of(at, 8), total.part), :], sem)
        for at, sem in ((total.one, out_sems.at[0]), (total.two, out_sems.at[1]))
    ]
    ends.append(pltpu.make_async_copy(tail_ref, tail_out, out_sems.at[2]))
    for copy in ends:
        copy.start()
    for e in range(late):
        spread.sent(e)

    @pl.when(inner)
    def _():
        for u in range(far_count):
            far_copy(u).wait_send()

    for k, ref in enumerate((h2_ref, g_ref, dt_ref)):
        pltpu.make_async_copy(ref, ref, tile_sems.at[k]).wait()
    for copy in ends:
        copy.wait()


def mlp(x, ot, wo, g, up, down, smalls, biases, gains, shifts, land, z):
    tokens, width = x.shape
    parts = smalls.shape[0]
    own = width // parts
    ff = up.shape[1]
    units = ff // UNIT
    chunks = units * (parts - 1)
    late = chunks - land.shape[0]
    tiles = tokens // TILE
    rows = 2 * ff
    tail = own + 64
    dma = pltpu.SemaphoreType.DMA
    return pl.pallas_call(
        mlp_kernel,
        in_specs=[WHOLE] * 5 + [ANY] * 7,
        out_specs=[ANY] * 5,
        out_shape=[
            shape_of((tokens, width), BF),
            shape_of((tokens, width), BF),
            shape_of((width, tokens), BF),
            shape_of((rows, width), F32),
            shape_of((tail, width), F32),
        ],
        scratch_shapes=[
            pltpu.VMEM((late, 2, width, UNIT), F32),
            pltpu.VMEM((units * (parts - 2), 2, width // 8, UNIT), F32),
            pltpu.VMEM((2, width, UNIT), F32),
            pltpu.VMEM((UNIT, width), F32),
            pltpu.VMEM((tokens, width), BF),
            pltpu.VMEM((tokens, width), BF),
            pltpu.VMEM((width, tokens), BF),
            pltpu.VMEM((own, tokens), BF),
            pltpu.VMEM((rows, width), F32),
            pltpu.VMEM((tail, width), F32),
            pltpu.VMEM((tokens, width), F32),
            pltpu.VMEM((tokens, 1), F32),
            pltpu.VMEM((tokens, width), F32),
            pltpu.VMEM((tokens, width), F32),
            pltpu.VMEM((width, UNIT), BF),
            pltpu.VMEM((UNIT, width), BF),
            pltpu.VMEM((2, TILE, UNIT), F32),
            pltpu.VMEM((2, TILE, UNIT), F32),
            dma((3,)),
            dma((2,)),
            dma((late,)),
            dma((units * (parts - 2),)),
            dma((units * (parts - 2),)),
            dma((units * (parts - 2),)),
            dma((3,)),
            dma((3,)),
            dma((late,)),
            dma((late, 3)),
        ]
        + Total.scratch(rows, width),
        compiler_params=pltpu.CompilerParams(vmem_limit_bytes=63 * 2**20, collective_id=1, has_side_effects=True),
        name="mlp",
    )(wo, smalls, biases, gains, shifts, x, ot, g, up, down, land, z)


def body(
    dp_size,
    tokens,
    segments,
    norm_gains,
    norm_shifts,
    qkv_weight,
    qv_bias,
    out_weight,
    out_biases,
    up_weight,
    up_bias,
    down_weight,
    cotangent,
):
    width = tokens.shape[1]
    own = qkv_weight.shape[2]
    ff = up_weight.shape[1]
    smalls, bound, h1, weights, wo, qkvt, ot, lse, land, z = front(
        tokens, segments, norm_gains, norm_shifts, qkv_weight.transpose(0, 2, 1).reshape(3 * own, width), out_weight,
        qv_bias, up_bias, up_weight, down_weight,
    )
    ot, lse = repair(bound, segments, qkvt, ot, lse)
    result, mg, dt, main, tail = mlp(
        tokens, ot, wo, cotangent, up_weight, down_weight, smalls, out_biases, norm_gains, norm_shifts, land, z
    )
    dqkv, main, rest = attend_back(segments, qkvt, ot, dt, lse, h1, main, tail)
    if dp_size > 8:
        main, rest = (value / 8 for value in lax.psum((main, rest), "dp"))
    token_grad, sums_one, down_grad, up_grad, out_weight_grad, result, qkv_grad = token_back(
        dqkv, weights, tokens, mg, norm_gains, main, rest, result, ff, own
    )
    sums_one = add_sums(sums_one)
    if dp_size > 8:
        sums_one = lax.psum(sums_one, "dp") / 8
    gains_grad, shifts_grad, out_biases_grad, qv_bias_grad, up_bias_grad = arrange(sums_one, rest, own)
    return (
        result,
        token_grad,
        gains_grad,
        shifts_grad,
        qkv_grad.reshape(3, own, width).transpose(0, 2, 1),
        qv_bias_grad,
        out_weight_grad,
        out_biases_grad,
        up_grad,
        up_bias_grad,
        down_grad,
    )


def solution(mesh):
    in_specs = (
        P("dp", None),
        P("dp", None),
        P(),
        P(),
        P(None, None, "mp"),
        P(None, "mp"),
        P("mp", None),
        P(),
        P(None, "mp"),
        P("mp"),
        P("mp", None),
        P("dp", None),
    )
    out_specs = (
        P("dp", None),
        P("dp", None),
        P(),
        P(),
        P(None, None, "mp"),
        P(None, "mp"),
        P("mp", None),
        P(),
        P(None, "mp"),
        P("mp"),
        P("mp", None),
    )
    return jax.shard_map(
        partial(body, mesh.shape["dp"]), mesh=mesh, in_specs=in_specs, out_specs=out_specs, check_vma=False
    )
```
